256 devices in a mesh: dp: 4 (over x), ctx: 64 (over z, y, core).
Axes of the slice: x: 4, y: 4, z: 8, core: 2. Of those that a mesh axis runs over, the one named last changes fastest.
Arguments:
- queries: bfloat16 [4, 8192, 1024], P('dp', 'ctx'), may hold values from -240 to 240
- keys: bfloat16 [4, 8192, 128], P('dp', 'ctx'), may hold values from -5 to 5
- values: bfloat16 [4, 8192, 128], P('dp', 'ctx'), may hold values from -6 to 6
- query_map: bfloat16 [8, 128, 64], replicated, may hold values from -0.5 to 0.5
- key_map: bfloat16 [8, 128, 64], replicated, may hold values from -0.5 to 0.5
- documents: int32 [4, 64], P('dp'), may hold values from 0 to 15, never falling along the last dimension, each value on 1 to 16 neighbouring positions
- assignment: int32 [4, 64, 64], P('dp'), may hold values from 0 to 63, each once within a row
Outputs:
- teacher_relaid: bfloat16 [4, 8192, 1024], P('dp', 'ctx')
- difference: float32 [4, 8192, 1024], P('dp', 'ctx')
- feature_grad: float32 [8, 128, 64], replicated
The draws below stay inside these ranges and needn't reach their ends.
Inputs may be any that keep to these rules, and one draw needn't show every extreme that they name: `documents`: document numbers never fall along a row; each document covers 1 to 16 blocks, and one covers exactly 16. For every row r and shard d, assignment[r, d, :] is a permutation: piece i of shard d goes to context shard assignment[r, d, i], so every shard receives one piece from every shard.
All inputs are finite; a program needn't handle non-finite values.
Results may differ from the reference program's by a relative error of at most 0.015.
Values may be sent and summed in bfloat16 or wider, within the bound.
No kernel may reach another device: no remote copies, remote signals or barrier semaphores. Data moves between devices by JAX's collectives and lax.ppermute only.
A program may use at most 192 MiB of HBM per device.

```python
import math
import jax
import jax.numpy as jnp
import numpy as np
from jax import lax

HEADS = 8
HEAD_DIM = 128
FEATURES = 64
WINDOW = 64
BLOCK = 128
TOK_DEV = 128
SEQUENCE = 8192
PIECE = 2
BLOCKS = 64
DOCUMENTS = 16
LONGEST = 16
N_DP = 4
N_CTX = 64


def common_keys(key):
    raw_keys = jax.random.normal(key, (N_DP, SEQUENCE, HEAD_DIM), jnp.float32)
    return jnp.clip(raw_keys, -5.0, 5.0)


def draw_keys(key, part):
    keys_now = common_keys(key)
    return keys_now.astype(jnp.bfloat16)


def draw_queries(key, part):
    key = jax.random.fold_in(key, 3)
    noise = jax.random.normal(key, (N_DP, SEQUENCE, HEADS * HEAD_DIM), jnp.float32)
    noise = jnp.clip(noise, -5.0, 5.0)
    return noise.astype(jnp.bfloat16)


def steps_of(stream_key, extent, split, smallest, top_value):
    factor_of = 1.0
    for dim, shards_of in split:
        draws = jax.random.uniform(jax.random.fold_in(jax.random.fold_in(stream_key, 6), dim), (shards_of,), jnp.float32, smallest / len(split), top_value / len(split))
        factor_of = factor_of * jnp.repeat(jnp.exp(draws), extent[dim] // shards_of).reshape((-1,) + (1,) * (len(extent) - 1 - dim))
    return factor_of


def split_up(number_of, total, bound, skew):
    portions = [(1 << 20) // math.isqrt(standing ** skew) + 1 for standing in range(2, number_of + 1)]
    surplus, given = total - bound - (number_of - 1), [1] * (number_of - 1)
    while surplus > 0:
        free = [i for i in range(number_of - 1) if given[i] < bound]
        pool, remaining = sum([portions[i] for i in free]), surplus
        for i in free:
            addition = min(bound - given[i], max(1, remaining * portions[i] // pool), surplus)
            given[i] = given[i] + addition
            surplus = surplus - addition
    return np.array([bound] + given)


def ragged(stream_key, count, total, reach, skew):
    if count == 2:
        one = jax.random.randint(stream_key, (), max(1, total - reach), min(reach, total - 1) + 1)
        return jnp.stack([one, total - one])
    tallies = jnp.asarray(split_up(count, total, reach, skew), jnp.int32)
    pairs = (count - 1) // 2
    donor, taker = tallies[1:1 + 2 * pairs:2], tallies[2:2 + 2 * pairs:2]
    room = jnp.minimum(donor - 1, reach - taker)
    moved = jax.random.randint(jax.random.fold_in(stream_key, 1), (pairs,), 0, 1 << 20) % (room + 1)
    tallies = tallies.at[1:1 + 2 * pairs:2].set(donor - moved).at[2:2 + 2 * pairs:2].set(taker + moved)
    return tallies[jax.random.permutation(jax.random.fold_in(stream_key, 2), count)]


def scatter_about(key, extent, width, limit, pieces=(), kind=jnp.bfloat16):
    values = jax.random.normal(key, extent, jnp.float32) * width
    if len(pieces) > 0:
        values = steps_of(key, extent, pieces, -0.22, 0.18) * values
    return jnp.clip(values, min=-limit, max=limit).astype(kind)


def setup_inputs(seed: int = 0) -> dict:
    splits = jax.random.split(jax.random.key(seed), 8)
    return {
        "queries": draw_queries(jax.random.fold_in(splits[7], 71), 0),
        "keys": draw_keys(jax.random.fold_in(splits[7], 71), 0),
        "values": scatter_about(splits[2], (N_DP, SEQUENCE, HEAD_DIM), 1.0, 6.0, ((0, 4), (1, 64))),
        "query_map": scatter_about(splits[3], (HEADS, HEAD_DIM, FEATURES), HEAD_DIM ** -0.5, 0.5),
        "key_map": scatter_about(splits[4], (HEADS, HEAD_DIM, FEATURES), HEAD_DIM ** -0.5, 0.5),
        "documents": jax.vmap(lambda own: jnp.searchsorted(jnp.cumsum(ragged(own, DOCUMENTS, BLOCKS, LONGEST, 2)), jnp.arange(BLOCKS), side="right"))(jax.random.split(splits[5], N_DP)).reshape((N_DP, BLOCKS)).astype(jnp.int32),
        "assignment": jax.vmap(lambda own: jax.random.permutation(own, N_CTX))(jax.random.split(splits[6], N_DP * N_CTX)).reshape((N_DP, N_CTX, N_CTX)).astype(jnp.int32),
    }


HIGHEST = lax.Precision.HIGHEST

def feature_map(logits):
    return jnp.concatenate([jax.nn.softmax(logits, axis=-1), jax.nn.softmax(-logits, axis=-1)], axis=-1)

def token_documents(documents_row):
    return jnp.repeat(documents_row, BLOCK)

def teacher_row(query_row, key_row, value_row, token_docs):
    block_rows = min(512, SEQUENCE)
    block_count = SEQUENCE // block_rows
    key_pos = jnp.arange(SEQUENCE, dtype=jnp.int32)
    key_float = key_row.astype(jnp.float32)
    value_float = value_row.astype(jnp.float32)

    def one_block(step_index):
        anchor = (step_index * block_rows).astype(jnp.int32)
        query_block = lax.dynamic_slice_in_dim(query_row, anchor, block_rows, 0).astype(jnp.float32)
        query_pos = anchor + jnp.arange(block_rows, dtype=jnp.int32)
        query_docs = lax.dynamic_slice_in_dim(token_docs, anchor, block_rows, 0)
        scores = jnp.einsum('qhe,ke->hqk', query_block, key_float, precision=HIGHEST) / math.sqrt(HEAD_DIM)
        allowed = (query_docs[:, None] == token_docs[None, :]) & (query_pos[:, None] >= key_pos[None, :])
        scores = jnp.where(allowed[None], scores, -jnp.inf)
        running_max = lax.optimization_barrier(jnp.max(scores, axis=-1, keepdims=True))
        weights = jnp.exp(scores - running_max)
        denominator = lax.optimization_barrier(jnp.sum(weights, axis=-1))
        rounded = lax.optimization_barrier(weights.astype(jnp.bfloat16)).astype(jnp.float32)
        mixed = jnp.einsum('hqk,ke->qhe', rounded, value_float, precision=HIGHEST)
        return (mixed / jnp.transpose(denominator)[:, :, None]).astype(jnp.bfloat16)
    outputs = lax.map(one_block, jnp.arange(block_count, dtype=jnp.int32))
    return outputs.reshape(SEQUENCE, HEADS, HEAD_DIM)

def block_output(query_block, key_block, value_block, phi_block, lin_state, lin_norm):
    scores = jnp.einsum('qhe,ke->hqk', query_block, key_block, precision=HIGHEST) / math.sqrt(HEAD_DIM)
    rows_here = key_block.shape[0]
    causal = jnp.arange(rows_here)[:, None] >= jnp.arange(rows_here)[None, :]
    scores = jnp.where(causal[None], scores, -jnp.inf)
    window_max = lax.optimization_barrier(jnp.max(scores, axis=-1, keepdims=True))
    weights = jnp.exp(scores - window_max)
    near_sum = jnp.einsum('hqk,ke->qhe', weights, value_block, precision=HIGHEST)
    near_total = jnp.transpose(lax.optimization_barrier(jnp.sum(weights, axis=-1)))
    far_sum = jnp.einsum('qhf,hfe->qhe', phi_block, lin_state, precision=HIGHEST)
    far_total = jnp.einsum('qhf,hf->qh', phi_block, lin_norm, precision=HIGHEST)
    return (near_sum + far_sum) / (near_total + far_total)[:, :, None]

def student_row(map_float, query_row, key_row, value_row, token_docs, key_map):
    query_float = query_row.astype(jnp.float32)
    key_float = key_row.astype(jnp.float32)
    value_float = value_row.astype(jnp.float32)
    query_features = feature_map(jnp.einsum('she,hef->shf', query_float, map_float, precision=HIGHEST))
    key_features = feature_map(jnp.einsum('se,hef->shf', key_float, key_map.astype(jnp.float32), precision=HIGHEST))
    windows = SEQUENCE // WINDOW
    doubled = query_features.shape[-1]
    blocks = (query_float.reshape(windows, WINDOW, HEADS, HEAD_DIM), key_float.reshape(windows, WINDOW, HEAD_DIM), value_float.reshape(windows, WINDOW, HEAD_DIM), query_features.reshape(windows, WINDOW, HEADS, doubled), key_features.reshape(windows, WINDOW, HEADS, doubled), token_docs.reshape(windows, WINDOW)[:, 0])

    def advance(running, inputs):
        lin_state, lin_norm, last_doc = running
        query_block, key_block, value_block, phi_block, psi_block, doc_now = inputs
        retain = (doc_now == last_doc).astype(jnp.float32)
        lin_state = lin_state * retain
        lin_norm = lin_norm * retain
        output = block_output(query_block, key_block, value_block, phi_block, lin_state, lin_norm)
        lin_state = lin_state + jnp.einsum('whf,we->hfe', psi_block, value_block, precision=HIGHEST)
        lin_norm = lin_norm + lax.optimization_barrier(jnp.sum(psi_block, axis=0))
        return ((lin_state, lin_norm, doc_now), output)
    initial = (jnp.zeros((HEADS, doubled, HEAD_DIM), jnp.float32), jnp.zeros((HEADS, doubled), jnp.float32), jnp.array(-1, jnp.int32))
    unused, outputs = lax.scan(advance, initial, blocks)
    return outputs.reshape(SEQUENCE, HEADS * HEAD_DIM)

def reference(queries, keys, values, query_map, key_map, documents, assignment):
    query_heads = queries.reshape(N_DP, SEQUENCE, HEADS, HEAD_DIM)
    doc_lists = [token_documents(documents[row_index]).astype(jnp.int32) for row_index in range(N_DP)]
    teacher = jnp.stack([teacher_row(query_heads[row_index], keys[row_index], values[row_index], doc_lists[row_index]) for row_index in range(N_DP)]).reshape(N_DP, SEQUENCE, HEADS * HEAD_DIM)
    target = teacher.astype(jnp.float32)
    loss_scale = HEAD_DIM / math.sqrt(N_DP * SEQUENCE)

    def loss_of(map_float):
        student = jnp.stack([student_row(map_float, query_heads[row_index], keys[row_index], values[row_index], doc_lists[row_index], key_map) for row_index in range(N_DP)])
        gap = student - target
        return (jnp.sum(gap * gap) * loss_scale, gap)
    total_loss, pullback, difference = jax.vjp(loss_of, query_map.astype(jnp.float32), has_aux=True)
    feature_grad = pullback(jnp.ones_like(total_loss))[0]
    sent_piece = jnp.argsort(assignment, axis=-1).astype(jnp.int32)
    source = jnp.arange(N_CTX, dtype=jnp.int32)
    within = jnp.arange(PIECE, dtype=jnp.int32)
    relaid = []
    for row_index in range(N_DP):
        chosen = jnp.transpose(sent_piece[row_index])
        rows_index = source[None, :, None] * TOK_DEV + chosen[:, :, None] * PIECE + within[None, None, :]
        relaid.append(jnp.take(teacher[row_index], rows_index.reshape(-1), axis=0))
    teacher_relaid = jnp.stack(relaid)
    return (teacher_relaid, difference, feature_grad)
```

```python
import functools
import math

import jax
import jax.numpy as jnp
import numpy as np
from jax import lax
from jax.experimental import pallas as pl
from jax.experimental.pallas import tpu as pltpu
from jax.sharding import Mesh, PartitionSpec as P

HEAD_DIM = 128
WINDOW = 64
BLOCK = 128
HEADS = 8
FEATURES = 64
ROWS = HEADS * BLOCK
CHUNK = 2 * BLOCK
CHUNKS = 8
FAR = CHUNK * CHUNKS
SCALE = math.log2(math.e) / math.sqrt(HEAD_DIM)
NEGATIVE = -1e30
NT = (((1,), (1,)), ((), ()))
NN = (((1,), (0,)), ((), ()))
F32 = jnp.float32
BF16 = jnp.bfloat16
LOG2E = math.log2(math.e)


def dot(a, b, dims=NN):
    return lax.dot_general(a, b, dims, preferred_element_type=F32)


def two_softmax(u):
    u = u * LOG2E
    top = jnp.max(u, axis=1, keepdims=True)
    low = jnp.min(u, axis=1, keepdims=True)
    up = jnp.exp2(u - top)
    down = jnp.exp2(low - u)
    up = up * (1.0 / jnp.sum(up, axis=1, keepdims=True))
    down = down * (1.0 / jnp.sum(down, axis=1, keepdims=True))
    return jnp.concatenate([up, down], axis=1)


def main_kernel(
    loss_scale,
    pos_ref,
    doc_ref,
    q_ref,
    k_ref,
    v_ref,
    a_ref,
    b_ref,
    qm_ref,
    km_ref,
    row_ref,
    diff_ref,
    buf_ref,
    qs,
    s_scr,
    p_scr,
    w_scr,
    psi_scr,
    vp_scr,
    phi_scr,
):
    here = pos_ref[0]
    z = lax.shift_right_logical(here, 3)
    y = lax.shift_right_logical(here, 1) & 3
    c = here & 1
    doc = doc_ref[here]

    def valid(chunk, k):
        yy = chunk % 4
        cc = c if chunk < 4 else 1 - c
        if k == 0:
            back = jnp.where(yy < y, 0, jnp.where(yy > y, 1, 2 * cc))
        else:
            back = jnp.where(yy > y, 2, 1)
        g = (z - back) * 8 + yy * 2 + cc
        inside = (g >= 0) & (g < here) & (g > here - 16)
        return inside & (doc_ref[jnp.maximum(g, 0)] == doc)

    for h in range(HEADS):
        qs[h * BLOCK : (h + 1) * BLOCK, :] = q_ref[:, h * BLOCK : (h + 1) * BLOCK]

    key_own = k_ref[...]
    tile = 256
    lane = lax.broadcasted_iota(jnp.int32, (1, CHUNK), 1)
    col = lax.broadcasted_iota(jnp.int32, (tile, BLOCK), 1)
    row = lax.broadcasted_iota(jnp.int32, (tile, BLOCK), 0) % BLOCK
    causal = col <= row
    near = causal & ((col < WINDOW) == (row < WINDOW))
    biases = []
    key_chunks = []
    for i in range(CHUNKS):
        src = a_ref if i < 4 else b_ref
        ok = [valid(i, 0), valid(i, 1)]
        biases.append(
            jnp.where(
                lane < BLOCK,
                jnp.where(ok[0], 0.0, NEGATIVE),
                jnp.where(ok[1], 0.0, NEGATIVE),
            )
        )
        for k in range(2):
            at = i * CHUNK + k * BLOCK
            value = src[i % 4, k, BLOCK:, :]
            one = jnp.where(ok[k], 1.0, 0.0).astype(BF16)
            vp_scr[at : at + BLOCK, :BLOCK] = value * one
            vp_scr[at : at + BLOCK, BLOCK:] = jnp.ones((BLOCK, BLOCK), BF16) * one
    vp_scr[FAR:, :BLOCK] = v_ref[...]
    vp_scr[FAR:, BLOCK:] = jnp.ones((BLOCK, BLOCK), BF16)
    for r in range(ROWS // tile):
        at = r * tile
        query = qs[at : at + tile, :]
        diag = dot(query, key_own, NT) * SCALE
        own = jnp.where(causal, diag, NEGATIVE)
        top = own
        for i in range(CHUNKS):
            src = a_ref if i < 4 else b_ref
            keys = jnp.concatenate([src[i % 4, 0, :BLOCK, :], src[i % 4, 1, :BLOCK, :]], axis=0)
            s = dot(query, keys, NT) * SCALE + biases[i]
            s_scr[at : at + tile, i * CHUNK : (i + 1) * CHUNK] = s
            top = jnp.maximum(top, jnp.maximum(s[:, :BLOCK], s[:, BLOCK:]))
        top = jnp.max(top, axis=1, keepdims=True)
        p_scr[at : at + tile, FAR:] = jnp.exp2(own - top).astype(BF16)
        for i in range(CHUNKS):
            s = s_scr[at : at + tile, i * CHUNK : (i + 1) * CHUNK]
            p_scr[at : at + tile, i * CHUNK : (i + 1) * CHUNK] = jnp.exp2(s - top).astype(BF16)
        window = jnp.where(near, diag, NEGATIVE)
        window_top = jnp.max(window, axis=1, keepdims=True)
        w_scr[at : at + tile, :] = jnp.exp2(window - window_top).astype(BF16)

    for i in range(CHUNKS):
        src = a_ref if i < 4 else b_ref
        keys = jnp.concatenate([src[i % 4, 0, :BLOCK, :], src[i % 4, 1, :BLOCK, :]], axis=0)
        u = dot(km_ref[...], keys, NT).reshape(HEADS, FEATURES, CHUNK)
        psi_scr[:, i * CHUNK : (i + 1) * CHUNK] = (
            two_softmax(u).reshape(ROWS, CHUNK).astype(BF16)
        )
    u = dot(km_ref[...], key_own, NT).reshape(HEADS, FEATURES, BLOCK)
    psi_own = two_softmax(u).reshape(ROWS, BLOCK).astype(BF16)

    value_own = vp_scr[FAR:, :]
    early = lax.broadcasted_iota(jnp.int32, (BLOCK, CHUNK), 0) < WINDOW
    value_early = jnp.where(early, value_own.astype(F32), 0.0).astype(BF16)

    mixed = dot(p_scr[...], vp_scr[...])
    state = dot(psi_scr[...], vp_scr[:FAR, :])
    state_late = state + dot(psi_own, value_early)
    local = dot(w_scr[...], value_own)
    state = state.astype(BF16)
    state_late = state_late.astype(BF16)

    first_half = lax.broadcasted_iota(jnp.int32, (BLOCK, BLOCK), 1) < WINDOW
    dest = (lax.broadcasted_iota(jnp.int32, (BLOCK, BLOCK), 0) == row_ref[...]).astype(BF16)
    for h in range(HEADS):
        at = h * BLOCK
        query = qs[at : at + BLOCK, :]
        u = dot(qm_ref[h * FEATURES : (h + 1) * FEATURES, :], query, NT)
        phi = two_softmax(u[None])[0]
        phi_both = jnp.concatenate(
            [jnp.where(first_half, phi, 0.0), jnp.where(first_half, 0.0, phi)], axis=0
        )
        states = jnp.concatenate([state[at : at + BLOCK], state_late[at : at + BLOCK]], axis=0)
        far = dot(phi_both.T.astype(BF16), states)
        total = far + local[at : at + BLOCK]
        inverse = 1.0 / total[:, BLOCK:]
        student = total[:, :BLOCK] * inverse
        teacher = (mixed[at : at + BLOCK, :BLOCK] / mixed[at : at + BLOCK, BLOCK:]).astype(BF16)
        gap = student - teacher.astype(F32)
        diff_ref[:, at : at + BLOCK] = gap
        moved = dot(dest, teacher).astype(BF16)
        for s in range(8):
            buf_ref[s, :, at : at + BLOCK] = moved[s * 16 : (s + 1) * 16, :]
        grad_out = gap * inverse * (2.0 * loss_scale)
        grad_both = jnp.concatenate([grad_out, -grad_out * student], axis=1).astype(BF16)
        dphi = dot(states, grad_both, NT)
        dphi = jnp.where(first_half, dphi[:BLOCK], dphi[BLOCK:])
        part = phi * dphi
        up, down = phi[:FEATURES], phi[FEATURES:]
        du = (
            part[:FEATURES]
            - part[FEATURES:]
            - up * jnp.sum(part[:FEATURES], axis=0, keepdims=True)
            + down * jnp.sum(part[FEATURES:], axis=0, keepdims=True)
        )
        grad = dot(du.astype(BF16), query).astype(BF16)
        for s in range(4):
            lanes = 1024 + s * BLOCK
            buf_ref[h, :, lanes : lanes + BLOCK] = grad[s * 16 : (s + 1) * 16, :]


def main_call(loss_scale, pos, doc, q, k, v, a, b, qm, km, row):
    vmem = pl.BlockSpec(memory_space=pltpu.VMEM)
    smem = pl.BlockSpec(memory_space=pltpu.SMEM)
    return pl.pallas_call(
        functools.partial(main_kernel, loss_scale),
        out_shape=(
            jax.ShapeDtypeStruct((BLOCK, HEADS * HEAD_DIM), F32),
            jax.ShapeDtypeStruct((8, 16, 1536), BF16),
        ),
        in_specs=[smem, smem] + [vmem] * 8,
        out_specs=(vmem, vmem),
        scratch_shapes=[
            pltpu.VMEM((ROWS, BLOCK), BF16),
            pltpu.VMEM((ROWS, FAR), F32),
            pltpu.VMEM((ROWS, FAR + BLOCK), BF16),
            pltpu.VMEM((ROWS, BLOCK), BF16),
            pltpu.VMEM((ROWS, FAR), BF16),
            pltpu.VMEM((FAR + BLOCK, CHUNK), BF16),
            pltpu.VMEM((BLOCK, BLOCK), F32),
        ],
        compiler_params=pltpu.CompilerParams(vmem_limit_bytes=48 * 1024 * 1024),
        cost_estimate=pl.CostEstimate(
            flops=3_000_000_000, bytes_accessed=3_000_000, transcendentals=4_000_000
        ),
        name="transfer",
    )(pos, doc, q, k, v, a, b, qm, km, row)


def on_device(queries, keys, values, query_map, key_map, documents, assignment):
    z, y, c = lax.axis_index("z"), lax.axis_index("y"), lax.axis_index("c")
    device = (z * 4 + y) * 2 + c
    kv = jnp.concatenate([keys[0], values[0]], axis=0)
    plane1 = lax.ppermute(kv, "z", [(i, (i + 1) % 8) for i in range(8)])
    plane2 = lax.ppermute(kv, "z", [(i, (i + 2) % 8) for i in range(8)])
    own = jnp.where(c == 1, plane2, kv)
    slots = jnp.stack(
        [
            jnp.stack(
                [
                    jnp.where(d > y, kv, jnp.where(d < y, plane1, own)),
                    jnp.where(d < y, plane2, plane1),
                ]
            )
            for d in range(4)
        ]
    )
    mine = lax.all_to_all(slots, "y", 0, 0, tiled=True)
    other = lax.ppermute(mine, "c", [(0, 1), (1, 0)])

    targets = lax.dynamic_index_in_dim(assignment[0], device, 0, keepdims=False)
    order = (targets % 8) * 8 + targets // 8
    row = (order[:, None] * 2 + jnp.arange(2, dtype=jnp.int32)[None, :]).reshape(1, BLOCK)
    query_rows = jnp.swapaxes(query_map, 1, 2).reshape(HEADS * FEATURES, HEAD_DIM)
    key_rows = jnp.swapaxes(key_map, 1, 2).reshape(HEADS * FEATURES, HEAD_DIM)
    loss_scale = HEAD_DIM / math.sqrt(4 * 64 * BLOCK)
    difference, outgoing = main_call(
        loss_scale,
        jnp.reshape(device, (1,)).astype(jnp.int32),
        documents[0],
        queries[0],
        keys[0],
        values[0],
        mine,
        other,
        query_rows,
        key_rows,
        row,
    )
    got = lax.all_to_all(outgoing, ("y", "c"), 0, 0, tiled=True)
    relay = got[:, :, :1024].reshape(8, 8, 2, 1024).transpose(1, 0, 2, 3).reshape(8, 16, 1024)
    part = jnp.sum(got[:, :, 1024:].astype(F32), axis=0).astype(BF16)
    part = jnp.broadcast_to(part[None], (8, 16, 512))
    got = lax.all_to_all(jnp.concatenate([relay, part], axis=2), "z", 0, 0, tiled=True)
    relaid = got[:, :, :1024].reshape(1, BLOCK, 1024)
    part = jnp.sum(got[:, :, 1024:].astype(F32), axis=0).astype(BF16)
    part = jnp.broadcast_to(part[None], (32, 16, 512))
    got = lax.all_to_all(part, ("x", "y", "c"), 0, 0, tiled=True)
    grad = jnp.sum(got.reshape(4, 8, 16, 512).astype(F32), axis=0)
    grad = grad.reshape(HEADS, 16, 4, HEAD_DIM).transpose(0, 2, 1, 3).reshape(HEADS, FEATURES, HEAD_DIM)
    return relaid, difference[None], jnp.swapaxes(grad, 1, 2)


def solution(mesh):
    split = Mesh(np.array(mesh.devices).reshape(4, 8, 4, 2), ("x", "z", "y", "c"))
    ctx = ("z", "y", "c")
    return jax.shard_map(
        on_device,
        mesh=split,
        in_specs=(
            P("x", ctx, None),
            P("x", ctx, None),
            P("x", ctx, None),
            P(),
            P(),
            P("x", None),
            P("x", None, None),
        ),
        out_specs=(P("x", ctx, None), P("x", ctx, None), P()),
        check_vma=False,
    )
```

```python
import functools
import math

import jax
import jax.numpy as jnp
import numpy as np
from jax import lax
from jax.experimental import pallas as pl
from jax.experimental.pallas import tpu as pltpu
from jax.sharding import Mesh, PartitionSpec as P

HEAD_DIM = 128
WINDOW = 64
BLOCK = 128
HEADS = 8
FEATURES = 64
ROWS = HEADS * BLOCK
CHUNK = 2 * BLOCK
CHUNKS = 8
FAR = CHUNK * CHUNKS
SCALE = math.log2(math.e) / math.sqrt(HEAD_DIM)
NEGATIVE = -1e30
NT = (((1,), (1,)), ((), ()))
NN = (((1,), (0,)), ((), ()))
TN = (((0,), (0,)), ((), ()))
TALL = HEAD_DIM + 16
F32 = jnp.float32
BF16 = jnp.bfloat16
LOG2E = math.log2(math.e)


def dot(a, b, dims=NN):
    return lax.dot_general(a, b, dims, preferred_element_type=F32)


def two_softmax(u):
    u = u * LOG2E
    top = jnp.max(u, axis=1, keepdims=True)
    low = jnp.min(u, axis=1, keepdims=True)
    up = jnp.exp2(u - top)
    down = jnp.exp2(low - u)
    up = up * (1.0 / jnp.sum(up, axis=1, keepdims=True))
    down = down * (1.0 / jnp.sum(down, axis=1, keepdims=True))
    return jnp.concatenate([up, down], axis=1)


def pack_kernel(k_ref, v_ref, out_ref):
    out_ref[:BLOCK, :] = k_ref[...]
    out_ref[BLOCK:, :] = v_ref[...].T


def pack_call(k, v):
    vmem = pl.BlockSpec(memory_space=pltpu.VMEM)
    return pl.pallas_call(
        pack_kernel,
        out_shape=jax.ShapeDtypeStruct((2 * BLOCK, HEAD_DIM), BF16),
        in_specs=[vmem] * 2,
        out_specs=vmem,
        compiler_params=pltpu.CompilerParams(vmem_limit_bytes=4 * 1024 * 1024),
        name="pack_block",
    )(k, v)


def with_ones(values):
    return jnp.concatenate([values, jnp.ones((TALL - HEAD_DIM, values.shape[1]), BF16)], axis=0)


def shard_index():
    return (lax.axis_index("z") * 4 + lax.axis_index("y")) * 2 + lax.axis_index("c")


def iota(shape, axis):
    return lax.broadcasted_iota(jnp.int32, shape, axis)


def local_kernel(
    q_ref,
    kv_ref,
    qm_ref,
    km_ref,
    route_ref,
    doc_ref,
    own_ref,
    near_ref,
    phi_ref,
    both_ref,
    psi_ref,
    dest_ref,
    ok_ref,
):
    keys = kv_ref[:BLOCK, :]
    values = with_ones(kv_ref[BLOCK:, :])
    col = lax.broadcasted_iota(jnp.int32, (BLOCK, BLOCK), 1)
    row = lax.broadcasted_iota(jnp.int32, (BLOCK, BLOCK), 0)
    causal = row <= col
    near = causal & ((col < WINDOW) == (row < WINDOW))
    first_half = col < WINDOW
    psi = two_softmax(dot(km_ref[...], keys, NT).reshape(HEADS, FEATURES, BLOCK))
    psi_ref[...] = psi.reshape(ROWS, BLOCK).astype(BF16)
    z, y, c = lax.axis_index("z"), lax.axis_index("y"), lax.axis_index("c")
    here = shard_index()
    place = iota((2 * CHUNKS, 64), 0)
    block = iota((2 * CHUNKS, 64), 1)
    from_y = lax.shift_right_logical(place, 1) & 3
    from_c = jnp.where(place < CHUNKS, c, 1 - c)
    first = jnp.where(from_y < y, 0, jnp.where(from_y > y, 1, 2 * from_c))
    second = jnp.where(from_y > y, 2, 1)
    source = (z - jnp.where((place & 1) == 0, first, second)) * 8 + from_y * 2 + from_c
    documents = doc_ref[...]
    own_document = jnp.sum(jnp.where(iota((1, 64), 1) == here, documents, 0), axis=1, keepdims=True)
    same = (documents == own_document) & (iota((1, 64), 1) < here) & (iota((1, 64), 1) > here - 16)
    found = jnp.where((source == block) & same, 1.0, 0.0)
    ok_ref[...] = jnp.broadcast_to(jnp.max(found, axis=1, keepdims=True), ok_ref.shape)
    shard = route_ref[pl.ds(here, 1), :]
    order = (shard & 7) * 8 + lax.shift_right_logical(shard, 3)
    pieces = (iota((64, 64), 0) == order).astype(BF16)
    rows = (lax.shift_right_logical(iota((BLOCK, 64), 0), 1) == iota((BLOCK, 64), 1)).astype(BF16)
    tokens = (iota((64, BLOCK), 0) == lax.shift_right_logical(iota((64, BLOCK), 1), 1)).astype(BF16)
    placed = dot(dot(rows, pieces).astype(BF16), tokens)
    dest_ref[...] = jnp.where((row & 1) == (col & 1), placed, 0.0).astype(BF16)
    for h in range(HEADS):
        at = h * BLOCK
        query = q_ref[:, at : at + BLOCK]
        scores = dot(keys, query, NT)
        own_ref[:, at : at + BLOCK] = jnp.where(causal, scores, NEGATIVE)
        window = jnp.where(near, scores * SCALE, NEGATIVE)
        weights = jnp.exp2(window - jnp.max(window, axis=0, keepdims=True))
        near_ref[:, at : at + BLOCK] = dot(values, weights.astype(BF16))
        u = dot(qm_ref[h * FEATURES : (h + 1) * FEATURES, :], query, NT)
        phi = two_softmax(u[None])[0]
        phi_ref[at : at + BLOCK, :] = phi
        both = jnp.concatenate(
            [jnp.where(first_half, phi, 0.0), jnp.where(first_half, 0.0, phi)], axis=0
        )
        both_ref[h * CHUNK : (h + 1) * CHUNK, :] = both.astype(BF16)


def local_call(q, kv, qm, km, routes, documents):
    vmem = pl.BlockSpec(memory_space=pltpu.VMEM)
    return pl.pallas_call(
        local_kernel,
        out_shape=(
            jax.ShapeDtypeStruct((BLOCK, ROWS), F32),
            jax.ShapeDtypeStruct((TALL, ROWS), F32),
            jax.ShapeDtypeStruct((ROWS, BLOCK), F32),
            jax.ShapeDtypeStruct((2 * ROWS, BLOCK), BF16),
            jax.ShapeDtypeStruct((ROWS, BLOCK), BF16),
            jax.ShapeDtypeStruct((BLOCK, BLOCK), BF16),
            jax.ShapeDtypeStruct((2 * CHUNKS, BLOCK), F32),
        ),
        in_specs=[vmem] * 6,
        out_specs=(vmem,) * 7,
        compiler_params=pltpu.CompilerParams(vmem_limit_bytes=16 * 1024 * 1024),
        cost_estimate=pl.CostEstimate(
            flops=400_000_000, bytes_accessed=4_000_000, transcendentals=500_000
        ),
        name="local_block",
    )(q, kv, qm, km, routes, documents)


def main_kernel(
    loss_scale,
    q_ref,
    kv_ref,
    a_ref,
    b_ref,
    km_ref,
    own_ref,
    near_ref,
    phi_ref,
    both_ref,
    psi_own_ref,
    dest_ref,
    ok_ref,
    diff_ref,
    buf_ref,
    s_scr,
    p_scr,
    psi_scr,
    key_scr,
    vp_scr,
):
    first_key = kv_ref[0:1, :]
    ones = jnp.ones((TALL - HEAD_DIM, BLOCK), BF16)
    for i in range(CHUNKS):
        src = a_ref if i < 4 else b_ref
        for k in range(2):
            at = i * CHUNK + k * BLOCK
            one = ok_ref[2 * i + k : 2 * i + k + 1, :]
            other = (1.0 - one).astype(BF16)
            one = one.astype(BF16)
            key_scr[at : at + BLOCK, :] = src[i % 4, k, :BLOCK, :] * one + first_key * other
            vp_scr[:HEAD_DIM, at : at + BLOCK] = src[i % 4, k, BLOCK:, :] * one
            vp_scr[HEAD_DIM:, at : at + BLOCK] = ones * one
    value_own = with_ones(kv_ref[BLOCK:, :])
    vp_scr[:, FAR:] = value_own
    early = lax.broadcasted_iota(jnp.int32, (TALL, BLOCK), 1) < WINDOW
    value_early = jnp.where(early, value_own.astype(F32), 0.0).astype(BF16)
    first_half = lax.broadcasted_iota(jnp.int32, (BLOCK, BLOCK), 1) < WINDOW
    first_row = lax.broadcasted_iota(jnp.int32, (TALL - HEAD_DIM, CHUNK), 0) == 0
    dest = dest_ref[...]

    groups = HEADS // 2
    tops, sums = [None] * groups, [None] * groups

    def scores(g):
        query = jnp.concatenate(
            [q_ref[:, (2 * g + k) * BLOCK : (2 * g + k + 1) * BLOCK] for k in range(2)], axis=0
        )
        top = jnp.max(
            own_ref[:, g * CHUNK : (g + 1) * CHUNK].reshape(BLOCK // 8, 8, CHUNK), axis=0
        )
        for i in range(CHUNKS):
            s = dot(key_scr[i * CHUNK : (i + 1) * CHUNK, :], query, NT)
            s_scr[g % 2, i * CHUNK : (i + 1) * CHUNK, :] = s
            top = jnp.maximum(top, jnp.max(s.reshape(CHUNK // 8, 8, CHUNK), axis=0))
            yield
        tops[g] = jnp.max(top, axis=0, keepdims=True) * SCALE

    def features(g):
        for i in range(CHUNKS):
            keys = key_scr[i * CHUNK : (i + 1) * CHUNK, :]
            u = dot(km_ref[g * BLOCK : (g + 1) * BLOCK, :], keys, NT)
            psi = two_softmax(u.reshape(2, FEATURES, CHUNK)).reshape(CHUNK, CHUNK)
            psi_scr[g % 3, :, i * CHUNK : (i + 1) * CHUNK] = psi.astype(BF16)
            yield

    def weights(g):
        for i in range(CHUNKS):
            s = s_scr[g % 2, i * CHUNK : (i + 1) * CHUNK, :]
            w = jnp.exp2(s * SCALE - tops[g])
            p_scr[g % 2, i * CHUNK : (i + 1) * CHUNK, :] = w.astype(BF16)
            yield
        s = own_ref[:, g * CHUNK : (g + 1) * CHUNK]
        p_scr[g % 2, FAR:, :] = jnp.exp2(s * SCALE - tops[g]).astype(BF16)
        yield

    def mixes(g):
        mixed = dot(vp_scr[...], p_scr[g % 2])
        yield
        state = dot(vp_scr[:, :FAR], psi_scr[g % 3], NT)
        yield
        late = state + dot(value_early, psi_own_ref[g * CHUNK : (g + 1) * CHUNK, :], NT)
        sums[g] = (mixed, state.astype(BF16), late.astype(BF16))
        yield

    def outputs(g):
        mixed, state, late = sums[g]
        heads = [2 * g, 2 * g + 1]
        parts = [slice(0, BLOCK), slice(BLOCK, CHUNK)]
        wide = slice(g * CHUNK, (g + 1) * CHUNK)
        states = [jnp.concatenate([state[:, p], late[:, p]], axis=1) for p in parts]
        far = [dot(states[k], both_ref[heads[k] * CHUNK : (heads[k] + 1) * CHUNK, :]) for k in range(2)]
        yield
        total = jnp.concatenate(far, axis=1) + near_ref[:, wide]
        share = 1.0 / mixed[HEAD_DIM : HEAD_DIM + 1]
        teacher = (mixed[:HEAD_DIM] * share).astype(BF16)
        yield
        moved = [dot(dest, teacher[:, p], NT) for p in parts]
        inverse = 1.0 / total[HEAD_DIM : HEAD_DIM + 1]
        student = total[:HEAD_DIM] * inverse
        gap = student - teacher.astype(F32)
        yield
        grad_out = gap * (inverse * (2.0 * loss_scale))
        drop = jnp.sum(grad_out * student, axis=0, keepdims=True)
        drop = jnp.where(first_row, -drop, 0.0).astype(BF16)
        grad_both = jnp.concatenate([grad_out.astype(BF16), drop], axis=0)
        yield
        dphi = [dot(states[k], grad_both[:, parts[k]], TN) for k in range(2)]
        yield
        for k in range(2):
            diff_ref[:, heads[k] * BLOCK : (heads[k] + 1) * BLOCK] = gap[:, parts[k]].T
            for shard in range(8):
                buf_ref[shard, :, heads[k] * BLOCK : (heads[k] + 1) * BLOCK] = moved[k][
                    shard * 16 : (shard + 1) * 16
                ].astype(BF16)
        yield
        du = []
        for k in range(2):
            phi = phi_ref[heads[k] * BLOCK : (heads[k] + 1) * BLOCK, :]
            terms = phi * jnp.where(first_half, dphi[k][:BLOCK], dphi[k][BLOCK:])
            up, down = phi[:FEATURES], phi[FEATURES:]
            du.append(
                terms[:FEATURES]
                - terms[FEATURES:]
                - up * jnp.sum(terms[:FEATURES], axis=0, keepdims=True)
                + down * jnp.sum(terms[FEATURES:], axis=0, keepdims=True)
            )
        yield
        for k in range(2):
            h = heads[k]
            grad = dot(du[k].astype(BF16), q_ref[:, h * BLOCK : (h + 1) * BLOCK]).astype(BF16)
            for i in range(4):
                at = (HEADS + i) * BLOCK
                buf_ref[h, :, at : at + BLOCK] = grad[i * 16 : (i + 1) * 16]
        yield

    for step in range(groups + 3):
        running = []
        for stage, length, late_by in (
            (scores, 9, 0),
            (features, 8, 0),
            (weights, 9, 1),
            (mixes, 3, 2),
            (outputs, 8, 3),
        ):
            if 0 <= step - late_by < groups:
                running.append((stage(step - late_by), length))
        marks = sorted(
            ((n + 0.5) / length, at) for at, (_, length) in enumerate(running) for n in range(length)
        )
        for _, at in marks:
            next(running[at][0], None)
        for stage, _ in running:
            for _ in stage:
                pass


def main_call(loss_scale, q, kv, a, b, km, local):
    vmem = pl.BlockSpec(memory_space=pltpu.VMEM)
    return pl.pallas_call(
        functools.partial(main_kernel, loss_scale),
        out_shape=(
            jax.ShapeDtypeStruct((BLOCK, HEADS * HEAD_DIM), F32),
            jax.ShapeDtypeStruct((8, 16, 1536), BF16),
        ),
        in_specs=[vmem] * 12,
        out_specs=(vmem, vmem),
        scratch_shapes=[
            pltpu.VMEM((2, FAR, CHUNK), F32),
            pltpu.VMEM((2, FAR + BLOCK, CHUNK), BF16),
            pltpu.VMEM((3, CHUNK, FAR), BF16),
            pltpu.VMEM((FAR, BLOCK), BF16),
            pltpu.VMEM((TALL, FAR + BLOCK), BF16),
        ],
        compiler_params=pltpu.CompilerParams(vmem_limit_bytes=32 * 1024 * 1024),
        cost_estimate=pl.CostEstimate(
            flops=3_000_000_000, bytes_accessed=3_000_000, transcendentals=4_000_000
        ),
        name="transfer",
    )(q, kv, a, b, km, *local)


def on_device(queries, keys, values, query_map, key_map, documents, assignment):
    y, c = lax.axis_index("y"), lax.axis_index("c")
    query_rows = jnp.swapaxes(query_map, 1, 2).reshape(HEADS * FEATURES, HEAD_DIM)
    key_rows = jnp.swapaxes(key_map, 1, 2).reshape(HEADS * FEATURES, HEAD_DIM)
    kv = pack_call(keys[0], values[0])
    plane1 = lax.ppermute(kv, "z", [(i, (i + 1) % 8) for i in range(8)])
    plane2 = lax.ppermute(kv, "z", [(i, (i + 2) % 8) for i in range(8)])
    local = local_call(queries[0], kv, query_rows, key_rows, assignment[0], documents)
    plane1, plane2, local = lax.optimization_barrier((plane1, plane2, local))
    own = jnp.where(c == 1, plane2, kv)
    slots = jnp.stack(
        [
            jnp.stack(
                [
                    jnp.where(d > y, kv, jnp.where(d < y, plane1, own)),
                    jnp.where(d < y, plane2, plane1),
                ]
            )
            for d in range(4)
        ]
    )
    mine = lax.all_to_all(slots, "y", 0, 0, tiled=True)
    other = lax.ppermute(mine, "c", [(0, 1), (1, 0)])
    loss_scale = HEAD_DIM / math.sqrt(4 * 64 * BLOCK)
    difference, outgoing = main_call(
        loss_scale, queries[0], kv, mine, other, key_rows, local
    )
    got = lax.all_to_all(outgoing, ("y", "c"), 0, 0, tiled=True)
    relay = got[:, :, :1024].reshape(8, 8, 2, 1024).transpose(1, 0, 2, 3).reshape(8, 16, 1024)
    part = jnp.sum(got[:, :, 1024:].astype(F32), axis=0).astype(BF16)
    part = jnp.broadcast_to(part[None], (8, 16, 512))
    got = lax.all_to_all(jnp.concatenate([relay, part], axis=2), "z", 0, 0, tiled=True)
    relaid = got[:, :, :1024].reshape(1, BLOCK, 1024)
    part = jnp.sum(got[:, :, 1024:].astype(F32), axis=0).astype(BF16)
    part = part.reshape(16, 4, HEAD_DIM).transpose(1, 0, 2).reshape(FEATURES, HEAD_DIM)
    part = jnp.broadcast_to(part[None], (32, FEATURES, HEAD_DIM))
    got = lax.all_to_all(part, ("x", "y", "c"), 0, 0, tiled=True)
    grad = jnp.sum(got.reshape(4, HEADS, FEATURES, HEAD_DIM).astype(F32), axis=0)
    return relaid, difference[None], jnp.swapaxes(grad, 1, 2)


def solution(mesh):
    split = Mesh(np.array(mesh.devices).reshape(4, 8, 4, 2), ("x", "z", "y", "c"))
    ctx = ("z", "y", "c")
    return jax.shard_map(
        on_device,
        mesh=split,
        in_specs=(
            P("x", ctx, None),
            P("x", ctx, None),
            P("x", ctx, None),
            P(),
            P(),
            P("x", None),
            P("x", None, None),
        ),
        out_specs=(P("x", ctx, None), P("x", ctx, None), P()),
        check_vma=False,
    )
```

```python
import functools
import math

import jax
import jax.numpy as jnp
import numpy as np
from jax import lax
from jax.experimental import pallas as pl
from jax.experimental.pallas import tpu as pltpu
from jax.sharding import Mesh, PartitionSpec as P

HEAD_DIM = 128
WINDOW = 64
BLOCK = 128
HEADS = 8
FEATURES = 64
ROWS = HEADS * BLOCK
CHUNK = 2 * BLOCK
CHUNKS = 8
FAR = CHUNK * CHUNKS
SCALE = math.log2(math.e) / math.sqrt(HEAD_DIM)
NEGATIVE = -1e30
NT = (((1,), (1,)), ((), ()))
NN = (((1,), (0,)), ((), ()))
TN = (((0,), (0,)), ((), ()))
TALL = HEAD_DIM + 16
F32 = jnp.float32
BF16 = jnp.bfloat16
LOG2E = math.log2(math.e)


def dot(a, b, dims=NN):
    return lax.dot_general(a, b, dims, preferred_element_type=F32)


def two_softmax(u):
    u = u * LOG2E
    top = jnp.max(u, axis=1, keepdims=True)
    low = jnp.min(u, axis=1, keepdims=True)
    up = jnp.exp2(u - top)
    down = jnp.exp2(low - u)
    up = up * (1.0 / jnp.sum(up, axis=1, keepdims=True))
    down = down * (1.0 / jnp.sum(down, axis=1, keepdims=True))
    return jnp.concatenate([up, down], axis=1)


def pack_kernel(k_ref, v_ref, out_ref, key_scr, value_scr, sems):
    key_copy = pltpu.make_async_copy(k_ref, key_scr, sems.at[0])
    value_copy = pltpu.make_async_copy(v_ref, value_scr, sems.at[1])
    value_copy.start()
    key_copy.start()
    value_copy.wait()
    out_ref[BLOCK:, :] = value_scr[...].T
    key_copy.wait()
    out_ref[:BLOCK, :] = key_scr[...]


def pack_call(k, v):
    hbm = pl.BlockSpec(memory_space=pltpu.HBM)
    return pl.pallas_call(
        pack_kernel,
        out_shape=jax.ShapeDtypeStruct((2 * BLOCK, HEAD_DIM), BF16),
        in_specs=[hbm] * 2,
        out_specs=pl.BlockSpec(memory_space=pltpu.VMEM),
        scratch_shapes=[
            pltpu.VMEM((BLOCK, HEAD_DIM), BF16),
            pltpu.VMEM((BLOCK, HEAD_DIM), BF16),
            pltpu.SemaphoreType.DMA((2,)),
        ],
        compiler_params=pltpu.CompilerParams(vmem_limit_bytes=56 * 1024 * 1024),
        name="pack_block",
    )(k, v)


def with_ones(values):
    return jnp.concatenate([values, jnp.ones((TALL - HEAD_DIM, values.shape[1]), BF16)], axis=0)


def shard_index():
    return (lax.axis_index("z") * 4 + lax.axis_index("y")) * 2 + lax.axis_index("c")


def iota(shape, axis):
    return lax.broadcasted_iota(jnp.int32, shape, axis)


def local_kernel(
    q_hbm,
    qm_hbm,
    km_hbm,
    route_hbm,
    doc_hbm,
    kv_ref,
    own_ref,
    near_ref,
    phi_ref,
    both_ref,
    psi_ref,
    dest_ref,
    ok_ref,
    q_ref,
    qm_ref,
    km_ref,
    route_ref,
    doc_ref,
    sems,
):
    pairs = (
        (route_hbm, route_ref),
        (doc_hbm, doc_ref),
        (km_hbm, km_ref),
        (qm_hbm, qm_ref),
        (q_hbm, q_ref),
    )
    copies = [pltpu.make_async_copy(a, b, sems.at[n]) for n, (a, b) in enumerate(pairs)]
    for copy in copies:
        copy.start()
    copies[0].wait()
    copies[1].wait()
    keys = kv_ref[:BLOCK, :]
    values = with_ones(kv_ref[BLOCK:, :])
    col = lax.broadcasted_iota(jnp.int32, (BLOCK, BLOCK), 1)
    row = lax.broadcasted_iota(jnp.int32, (BLOCK, BLOCK), 0)
    causal = row <= col
    near = causal & ((col < WINDOW) == (row < WINDOW))
    first_half = col < WINDOW
    z, y, c = lax.axis_index("z"), lax.axis_index("y"), lax.axis_index("c")
    here = shard_index()
    place = iota((2 * CHUNKS, 64), 0)
    block = iota((2 * CHUNKS, 64), 1)
    from_y = lax.shift_right_logical(place, 1) & 3
    from_c = jnp.where(place < CHUNKS, c, 1 - c)
    first = jnp.where(from_y < y, 0, jnp.where(from_y > y, 1, 2 * from_c))
    second = jnp.where(from_y > y, 2, 1)
    source = (z - jnp.where((place & 1) == 0, first, second)) * 8 + from_y * 2 + from_c
    documents = doc_ref[...]
    own_document = jnp.sum(jnp.where(iota((1, 64), 1) == here, documents, 0), axis=1, keepdims=True)
    same = (documents == own_document) & (iota((1, 64), 1) < here) & (iota((1, 64), 1) > here - 16)
    found = jnp.where((source == block) & same, 1.0, 0.0)
    ok_ref[...] = jnp.broadcast_to(jnp.max(found, axis=1, keepdims=True), ok_ref.shape)
    shard = route_ref[pl.ds(here, 1), :]
    order = (shard & 7) * 8 + lax.shift_right_logical(shard, 3)
    pieces = (iota((64, 64), 0) == order).astype(BF16)
    rows = (lax.shift_right_logical(iota((BLOCK, 64), 0), 1) == iota((BLOCK, 64), 1)).astype(BF16)
    tokens = (iota((64, BLOCK), 0) == lax.shift_right_logical(iota((64, BLOCK), 1), 1)).astype(BF16)
    placed = dot(dot(rows, pieces).astype(BF16), tokens)
    dest_ref[...] = jnp.where((row & 1) == (col & 1), placed, 0.0).astype(BF16)
    copies[2].wait()
    psi = two_softmax(dot(km_ref[...], keys, NT).reshape(HEADS, FEATURES, BLOCK))
    psi_ref[...] = psi.reshape(ROWS, BLOCK).astype(BF16)
    copies[3].wait()
    copies[4].wait()
    for h in range(HEADS):
        at = h * BLOCK
        query = q_ref[:, at : at + BLOCK]
        scores = dot(keys, query, NT)
        own_ref[:, at : at + BLOCK] = jnp.where(causal, scores, NEGATIVE)
        window = jnp.where(near, scores * SCALE, NEGATIVE)
        weights = jnp.exp2(window - jnp.max(window, axis=0, keepdims=True))
        near_ref[:, at : at + BLOCK] = dot(values, weights.astype(BF16))
        u = dot(qm_ref[h * FEATURES : (h + 1) * FEATURES, :], query, NT)
        phi = two_softmax(u[None])[0]
        phi_ref[at : at + BLOCK, :] = phi
        both = jnp.concatenate(
            [jnp.where(first_half, phi, 0.0), jnp.where(first_half, 0.0, phi)], axis=0
        )
        both_ref[h * CHUNK : (h + 1) * CHUNK, :] = both.astype(BF16)


def local_call(q, kv, qm, km, routes, documents):
    vmem = pl.BlockSpec(memory_space=pltpu.VMEM)
    return pl.pallas_call(
        local_kernel,
        out_shape=(
            jax.ShapeDtypeStruct((BLOCK, ROWS), F32),
            jax.ShapeDtypeStruct((TALL, ROWS), F32),
            jax.ShapeDtypeStruct((ROWS, BLOCK), F32),
            jax.ShapeDtypeStruct((2 * ROWS, BLOCK), BF16),
            jax.ShapeDtypeStruct((ROWS, BLOCK), BF16),
            jax.ShapeDtypeStruct((BLOCK, BLOCK), BF16),
            jax.ShapeDtypeStruct((2 * CHUNKS, BLOCK), F32),
        ),
        in_specs=[pl.BlockSpec(memory_space=pltpu.HBM)] * 5 + [vmem],
        out_specs=(vmem,) * 7,
        scratch_shapes=[
            pltpu.VMEM((BLOCK, ROWS), BF16),
            pltpu.VMEM((HEADS * FEATURES, HEAD_DIM), BF16),
            pltpu.VMEM((HEADS * FEATURES, HEAD_DIM), BF16),
            pltpu.VMEM((64, 64), jnp.int32),
            pltpu.VMEM((1, 64), jnp.int32),
            pltpu.SemaphoreType.DMA((5,)),
        ],
        compiler_params=pltpu.CompilerParams(vmem_limit_bytes=56 * 1024 * 1024),
        cost_estimate=pl.CostEstimate(
            flops=400_000_000, bytes_accessed=4_000_000, transcendentals=500_000
        ),
        name="local_block",
    )(q, qm, km, routes, documents, kv)


def main_kernel(
    loss_scale,
    q_ref,
    kv_ref,
    a_ref,
    b_ref,
    km_ref,
    own_ref,
    near_ref,
    phi_ref,
    both_ref,
    psi_own_ref,
    dest_ref,
    ok_ref,
    diff_ref,
    buf_ref,
    s_scr,
    p_scr,
    psi_scr,
    key_scr,
    vp_scr,
):
    first_key = kv_ref[0:1, :]
    ones = jnp.ones((TALL - HEAD_DIM, BLOCK), BF16)
    for i in range(CHUNKS):
        src = a_ref if i < 4 else b_ref
        for k in range(2):
            at = i * CHUNK + k * BLOCK
            one = ok_ref[2 * i + k : 2 * i + k + 1, :]
            other = (1.0 - one).astype(BF16)
            one = one.astype(BF16)
            key_scr[at : at + BLOCK, :] = src[i % 4, k, :BLOCK, :] * one + first_key * other
            vp_scr[:HEAD_DIM, at : at + BLOCK] = src[i % 4, k, BLOCK:, :] * one
            vp_scr[HEAD_DIM:, at : at + BLOCK] = ones * one
    value_own = with_ones(kv_ref[BLOCK:, :])
    vp_scr[:, FAR:] = value_own
    early = lax.broadcasted_iota(jnp.int32, (TALL, BLOCK), 1) < WINDOW
    value_early = jnp.where(early, value_own.astype(F32), 0.0).astype(BF16)
    first_half = lax.broadcasted_iota(jnp.int32, (BLOCK, BLOCK), 1) < WINDOW
    first_row = lax.broadcasted_iota(jnp.int32, (TALL - HEAD_DIM, CHUNK), 0) == 0
    dest = dest_ref[...]

    groups = HEADS // 2
    tops, sums = [None] * groups, [None] * groups

    def scores(g):
        query = jnp.concatenate(
            [q_ref[:, (2 * g + k) * BLOCK : (2 * g + k + 1) * BLOCK] for k in range(2)], axis=0
        )
        top = jnp.max(
            own_ref[:, g * CHUNK : (g + 1) * CHUNK].reshape(BLOCK // 8, 8, CHUNK), axis=0
        )
        for i in range(CHUNKS):
            s = dot(key_scr[i * CHUNK : (i + 1) * CHUNK, :], query, NT)
            s_scr[g % 2, i * CHUNK : (i + 1) * CHUNK, :] = s
            top = jnp.maximum(top, jnp.max(s.reshape(CHUNK // 8, 8, CHUNK), axis=0))
            yield
        tops[g] = jnp.max(top, axis=0, keepdims=True) * SCALE

    def features(g):
        for i in range(CHUNKS):
            keys = key_scr[i * CHUNK : (i + 1) * CHUNK, :]
            u = dot(km_ref[g * BLOCK : (g + 1) * BLOCK, :], keys, NT)
            psi = two_softmax(u.reshape(2, FEATURES, CHUNK)).reshape(CHUNK, CHUNK)
            psi_scr[g % 3, :, i * CHUNK : (i + 1) * CHUNK] = psi.astype(BF16)
            yield

    def weights(g):
        for i in range(CHUNKS):
            s = s_scr[g % 2, i * CHUNK : (i + 1) * CHUNK, :]
            w = jnp.exp2(s * SCALE - tops[g])
            p_scr[g % 2, i * CHUNK : (i + 1) * CHUNK, :] = w.astype(BF16)
            yield
        s = own_ref[:, g * CHUNK : (g + 1) * CHUNK]
        p_scr[g % 2, FAR:, :] = jnp.exp2(s * SCALE - tops[g]).astype(BF16)
        yield

    def mixes(g):
        mixed = dot(vp_scr[...], p_scr[g % 2])
        yield
        state = dot(vp_scr[:, :FAR], psi_scr[g % 3], NT)
        yield
        late = state + dot(value_early, psi_own_ref[g * CHUNK : (g + 1) * CHUNK, :], NT)
        sums[g] = (mixed, state.astype(BF16), late.astype(BF16))
        yield

    def outputs(g):
        mixed, state, late = sums[g]
        heads = [2 * g, 2 * g + 1]
        parts = [slice(0, BLOCK), slice(BLOCK, CHUNK)]
        wide = slice(g * CHUNK, (g + 1) * CHUNK)
        states = [jnp.concatenate([state[:, p], late[:, p]], axis=1) for p in parts]
        far = [dot(states[k], both_ref[heads[k] * CHUNK : (heads[k] + 1) * CHUNK, :]) for k in range(2)]
        yield
        total = jnp.concatenate(far, axis=1) + near_ref[:, wide]
        share = 1.0 / mixed[HEAD_DIM : HEAD_DIM + 1]
        teacher = (mixed[:HEAD_DIM] * share).astype(BF16)
        yield
        moved = [dot(dest, teacher[:, p], NT) for p in parts]
        inverse = 1.0 / total[HEAD_DIM : HEAD_DIM + 1]
        student = total[:HEAD_DIM] * inverse
        gap = student - teacher.astype(F32)
        yield
        grad_out = gap * (inverse * (2.0 * loss_scale))
        drop = jnp.sum(grad_out * student, axis=0, keepdims=True)
        drop = jnp.where(first_row, -drop, 0.0).astype(BF16)
        grad_both = jnp.concatenate([grad_out.astype(BF16), drop], axis=0)
        yield
        dphi = [dot(states[k], grad_both[:, parts[k]], TN) for k in range(2)]
        yield
        for k in range(2):
            diff_ref[:, heads[k] * BLOCK : (heads[k] + 1) * BLOCK] = gap[:, parts[k]].T
            for shard in range(8):
                buf_ref[shard, :, heads[k] * BLOCK : (heads[k] + 1) * BLOCK] = moved[k][
                    shard * 16 : (shard + 1) * 16
                ].astype(BF16)
        yield
        du = []
        for k in range(2):
            phi = phi_ref[heads[k] * BLOCK : (heads[k] + 1) * BLOCK, :]
            terms = phi * jnp.where(first_half, dphi[k][:BLOCK], dphi[k][BLOCK:])
            up, down = phi[:FEATURES], phi[FEATURES:]
            du.append(
                terms[:FEATURES]
                - terms[FEATURES:]
                - up * jnp.sum(terms[:FEATURES], axis=0, keepdims=True)
                + down * jnp.sum(terms[FEATURES:], axis=0, keepdims=True)
            )
        yield
        for k in range(2):
            h = heads[k]
            grad = dot(du[k].astype(BF16), q_ref[:, h * BLOCK : (h + 1) * BLOCK]).astype(BF16)
            for i in range(4):
                at = (HEADS + i) * BLOCK
                buf_ref[h, :, at : at + BLOCK] = grad[i * 16 : (i + 1) * 16]
        yield

    for step in range(groups + 3):
        running = []
        for stage, length, late_by in (
            (scores, 9, 0),
            (features, 8, 0),
            (weights, 9, 1),
            (mixes, 3, 2),
            (outputs, 8, 3),
        ):
            if 0 <= step - late_by < groups:
                running.append((stage(step - late_by), length))
        marks = sorted(
            ((n + 0.5) / length, at) for at, (_, length) in enumerate(running) for n in range(length)
        )
        for _, at in marks:
            next(running[at][0], None)
        for stage, _ in running:
            for _ in stage:
                pass


def main_call(loss_scale, q, kv, a, b, km, local):
    vmem = pl.BlockSpec(memory_space=pltpu.VMEM)
    return pl.pallas_call(
        functools.partial(main_kernel, loss_scale),
        out_shape=(
            jax.ShapeDtypeStruct((BLOCK, HEADS * HEAD_DIM), F32),
            jax.ShapeDtypeStruct((8, 16, 1536), BF16),
        ),
        in_specs=[vmem] * 12,
        out_specs=(vmem, vmem),
        scratch_shapes=[
            pltpu.VMEM((2, FAR, CHUNK), F32),
            pltpu.VMEM((2, FAR + BLOCK, CHUNK), BF16),
            pltpu.VMEM((3, CHUNK, FAR), BF16),
            pltpu.VMEM((FAR, BLOCK), BF16),
            pltpu.VMEM((TALL, FAR + BLOCK), BF16),
        ],
        compiler_params=pltpu.CompilerParams(vmem_limit_bytes=32 * 1024 * 1024),
        cost_estimate=pl.CostEstimate(
            flops=3_000_000_000, bytes_accessed=3_000_000, transcendentals=4_000_000
        ),
        name="transfer",
    )(q, kv, a, b, km, *local)


def on_device(queries, keys, values, query_map, key_map, documents, assignment):
    y, c = lax.axis_index("y"), lax.axis_index("c")
    query_rows = jnp.swapaxes(query_map, 1, 2).reshape(HEADS * FEATURES, HEAD_DIM)
    key_rows = jnp.swapaxes(key_map, 1, 2).reshape(HEADS * FEATURES, HEAD_DIM)
    kv = pack_call(keys[0], values[0])
    plane1 = lax.ppermute(kv, "z", [(i, (i + 1) % 8) for i in range(8)])
    plane2 = lax.ppermute(kv, "z", [(i, (i + 2) % 8) for i in range(8)])
    local = local_call(queries[0], kv, query_rows, key_rows, assignment[0], documents)
    plane1, plane2, local = lax.optimization_barrier((plane1, plane2, local))
    own = jnp.where(c == 1, plane2, kv)
    slots = jnp.stack(
        [
            jnp.stack(
                [
                    jnp.where(d > y, kv, jnp.where(d < y, plane1, own)),
                    jnp.where(d < y, plane2, plane1),
                ]
            )
            for d in range(4)
        ]
    )
    mine = lax.all_to_all(slots, "y", 0, 0, tiled=True)
    other = lax.ppermute(mine, "c", [(0, 1), (1, 0)])
    loss_scale = HEAD_DIM / math.sqrt(4 * 64 * BLOCK)
    difference, outgoing = main_call(
        loss_scale, queries[0], kv, mine, other, key_rows, local
    )
    got = lax.all_to_all(outgoing, ("y", "c"), 0, 0, tiled=True)
    relay = got[:, :, :1024].reshape(8, 8, 2, 1024).transpose(1, 0, 2, 3).reshape(8, 16, 1024)
    part = jnp.sum(got[:, :, 1024:].astype(F32), axis=0).astype(BF16)
    part = jnp.broadcast_to(part[None], (8, 16, 512))
    got = lax.all_to_all(jnp.concatenate([relay, part], axis=2), "z", 0, 0, tiled=True)
    relaid = got[:, :, :1024].reshape(1, BLOCK, 1024)
    part = jnp.sum(got[:, :, 1024:].astype(F32), axis=0).astype(BF16)
    part = part.reshape(16, 4, HEAD_DIM).transpose(1, 0, 2).reshape(FEATURES, HEAD_DIM)
    part = jnp.broadcast_to(part[None], (16, FEATURES, HEAD_DIM))
    got = lax.all_to_all(part, ("x", "y"), 0, 0, tiled=True)
    part = jnp.sum(got.reshape(4, 4, FEATURES, HEAD_DIM).astype(F32), axis=0).astype(BF16)
    far = lax.ppermute(part, "c", [(0, 1), (1, 0)])
    mine_first = lax.broadcasted_iota(jnp.int32, (4, 2, FEATURES, HEAD_DIM), 1) == c
    grad = jnp.where(mine_first, part[:, None], far[:, None]).astype(F32)
    grad = grad.reshape(HEADS, FEATURES, HEAD_DIM)
    return relaid, difference[None], jnp.swapaxes(grad, 1, 2)


def solution(mesh):
    split = Mesh(np.array(mesh.devices).reshape(4, 8, 4, 2), ("x", "z", "y", "c"))
    ctx = ("z", "y", "c")
    return jax.shard_map(
        on_device,
        mesh=split,
        in_specs=(
            P("x", ctx, None),
            P("x", ctx, None),
            P("x", ctx, None),
            P(),
            P(),
            P("x", None),
            P("x", None, None),
        ),
        out_specs=(P("x", ctx, None), P("x", ctx, None), P()),
        check_vma=False,
    )
```

```python
import functools
import math

import jax
import jax.numpy as jnp
import numpy as np
from jax import lax
from jax.experimental import pallas as pl
from jax.experimental.pallas import tpu as pltpu
from jax.sharding import Mesh, PartitionSpec as P

HEAD_DIM = 128
WINDOW = 64
BLOCK = 128
HEADS = 8
FEATURES = 64
ROWS = HEADS * BLOCK
CHUNK = 2 * BLOCK
CHUNKS = 8
FAR = CHUNK * CHUNKS
SCALE = math.log2(math.e) / math.sqrt(HEAD_DIM)
NEGATIVE = -1e30
NT = (((1,), (1,)), ((), ()))
NN = (((1,), (0,)), ((), ()))
TN = (((0,), (0,)), ((), ()))
TALL = HEAD_DIM + 16
F32 = jnp.float32
BF16 = jnp.bfloat16
LOG2E = math.log2(math.e)


def dot(a, b, dims=NN):
    return lax.dot_general(a, b, dims, preferred_element_type=F32)


def two_softmax(u):
    u = u * LOG2E
    top = jnp.max(u, axis=1, keepdims=True)
    low = jnp.min(u, axis=1, keepdims=True)
    up = jnp.exp2(u - top)
    down = jnp.exp2(low - u)
    up = up * (1.0 / jnp.sum(up, axis=1, keepdims=True))
    down = down * (1.0 / jnp.sum(down, axis=1, keepdims=True))
    return jnp.concatenate([up, down], axis=1)


def in_hbm(x):
    return pltpu.with_memory_space_constraint(x, pltpu.HBM)


def shard_index():
    return (lax.axis_index("z") * 4 + lax.axis_index("y")) * 2 + lax.axis_index("c")


def iota(shape, axis):
    return lax.broadcasted_iota(jnp.int32, shape, axis)


def local_kernel(
    q_hbm,
    qm_hbm,
    km_hbm,
    route_hbm,
    doc_hbm,
    k_hbm,
    v_hbm,
    own_ref,
    near_ref,
    phi_ref,
    both_ref,
    psi_ref,
    dest_ref,
    ok_ref,
    q_ref,
    qm_ref,
    km_ref,
    route_ref,
    doc_ref,
    k_ref,
    v_ref,
    sems,
):
    pairs = (
        (route_hbm, route_ref),
        (doc_hbm, doc_ref),
        (k_hbm, k_ref),
        (v_hbm, v_ref),
        (km_hbm, km_ref),
        (qm_hbm, qm_ref),
        (q_hbm, q_ref),
    )
    copies = [pltpu.make_async_copy(a, b, sems.at[n]) for n, (a, b) in enumerate(pairs)]
    for copy in copies:
        copy.start()
    copies[0].wait()
    copies[1].wait()
    col = lax.broadcasted_iota(jnp.int32, (BLOCK, BLOCK), 1)
    row = lax.broadcasted_iota(jnp.int32, (BLOCK, BLOCK), 0)
    causal = row <= col
    near = causal & ((col < WINDOW) == (row < WINDOW))
    first_half = col < WINDOW
    z, y, c = lax.axis_index("z"), lax.axis_index("y"), lax.axis_index("c")
    here = shard_index()
    place = iota((2 * CHUNKS, 64), 0)
    block = iota((2 * CHUNKS, 64), 1)
    from_y = lax.shift_right_logical(place, 1) & 3
    from_c = jnp.where(place < CHUNKS, c, 1 - c)
    first = jnp.where(from_y < y, 0, jnp.where(from_y > y, 1, 2 * from_c))
    second = jnp.where(from_y > y, 2, 1)
    source = (z - jnp.where((place & 1) == 0, first, second)) * 8 + from_y * 2 + from_c
    documents = doc_ref[...]
    own_document = jnp.sum(jnp.where(iota((1, 64), 1) == here, documents, 0), axis=1, keepdims=True)
    same = (documents == own_document) & (iota((1, 64), 1) < here) & (iota((1, 64), 1) > here - 16)
    found = jnp.where((source == block) & same, 1.0, 0.0)
    ok_ref[...] = jnp.broadcast_to(jnp.max(found, axis=1, keepdims=True), ok_ref.shape)
    shard = route_ref[pl.ds(here, 1), :]
    order = (shard & 7) * 8 + lax.shift_right_logical(shard, 3)
    pieces = (iota((64, 64), 0) == order).astype(BF16)
    rows = (lax.shift_right_logical(iota((BLOCK, 64), 0), 1) == iota((BLOCK, 64), 1)).astype(BF16)
    tokens = (iota((64, BLOCK), 0) == lax.shift_right_logical(iota((64, BLOCK), 1), 1)).astype(BF16)
    placed = dot(dot(rows, pieces).astype(BF16), tokens)
    dest_ref[...] = jnp.where((row & 1) == (col & 1), placed, 0.0).astype(BF16)
    for copy in copies[2:5]:
        copy.wait()
    keys = k_ref[...]
    values = jnp.concatenate([v_ref[...], jnp.ones((BLOCK, BLOCK), BF16)], axis=1)
    psi = two_softmax(dot(km_ref[...], keys, NT).reshape(HEADS, FEATURES, BLOCK))
    psi_ref[...] = psi.reshape(ROWS, BLOCK).astype(BF16)
    copies[5].wait()
    copies[6].wait()
    for h in range(HEADS):
        at = h * BLOCK
        query = q_ref[:, at : at + BLOCK]
        scores = dot(keys, query, NT)
        own_ref[:, at : at + BLOCK] = jnp.where(causal, scores, NEGATIVE)
        window = jnp.where(near, scores * SCALE, NEGATIVE)
        weights = jnp.exp2(window - jnp.max(window, axis=0, keepdims=True))
        near_ref[at : at + BLOCK, :] = dot(weights.T.astype(BF16), values)
        u = dot(qm_ref[h * FEATURES : (h + 1) * FEATURES, :], query, NT)
        phi = two_softmax(u[None])[0]
        phi_ref[at : at + BLOCK, :] = phi
        both = jnp.concatenate(
            [jnp.where(first_half, phi, 0.0), jnp.where(first_half, 0.0, phi)], axis=0
        )
        both_ref[at : at + BLOCK, :] = both.T.astype(BF16)


def local_call(q, k, v, qm, km, routes, documents):
    vmem = pl.BlockSpec(memory_space=pltpu.VMEM)
    return pl.pallas_call(
        local_kernel,
        out_shape=(
            jax.ShapeDtypeStruct((BLOCK, ROWS), F32),
            jax.ShapeDtypeStruct((ROWS, CHUNK), F32),
            jax.ShapeDtypeStruct((ROWS, BLOCK), F32),
            jax.ShapeDtypeStruct((ROWS, CHUNK), BF16),
            jax.ShapeDtypeStruct((ROWS, BLOCK), BF16),
            jax.ShapeDtypeStruct((BLOCK, BLOCK), BF16),
            jax.ShapeDtypeStruct((2 * CHUNKS, BLOCK), F32),
        ),
        in_specs=[pl.BlockSpec(memory_space=pltpu.HBM)] * 7,
        out_specs=(vmem,) * 7,
        scratch_shapes=[
            pltpu.VMEM((BLOCK, ROWS), BF16),
            pltpu.VMEM((HEADS * FEATURES, HEAD_DIM), BF16),
            pltpu.VMEM((HEADS * FEATURES, HEAD_DIM), BF16),
            pltpu.VMEM((64, 64), jnp.int32),
            pltpu.VMEM((1, 64), jnp.int32),
            pltpu.VMEM((BLOCK, HEAD_DIM), BF16),
            pltpu.VMEM((BLOCK, HEAD_DIM), BF16),
            pltpu.SemaphoreType.DMA((7,)),
        ],
        compiler_params=pltpu.CompilerParams(vmem_limit_bytes=16 * 1024 * 1024),
        cost_estimate=pl.CostEstimate(
            flops=400_000_000, bytes_accessed=4_000_000, transcendentals=500_000
        ),
        name="local_block",
    )(*[in_hbm(each) for each in (q, qm, km, routes, documents, k, v)])


def slot_kernel(k0_ref, v0_ref, k1_ref, v1_ref, k2_ref, v2_ref, out_ref):
    y, c = lax.axis_index("y"), lax.axis_index("c")
    planes = ((k0_ref, v0_ref), (k1_ref, v1_ref), (k2_ref, v2_ref))

    def put(d, k, plane):
        for n in range(2):
            out_ref[d, k, n] = planes[plane][n][...]

    for d in range(4):

        @pl.when(d > y)
        def _():
            put(d, 0, 0)
            put(d, 1, 1)

        @pl.when(d < y)
        def _():
            put(d, 0, 1)
            put(d, 1, 2)

        @pl.when((d == y) & (c == 0))
        def _():
            put(d, 0, 0)
            put(d, 1, 1)

        @pl.when((d == y) & (c == 1))
        def _():
            put(d, 0, 2)
            put(d, 1, 1)


def slot_call(*blocks):
    vmem = pl.BlockSpec(memory_space=pltpu.VMEM)
    return pl.pallas_call(
        slot_kernel,
        out_shape=jax.ShapeDtypeStruct((4, 2, 2, BLOCK, HEAD_DIM), BF16),
        in_specs=[vmem] * 6,
        out_specs=vmem,
        compiler_params=pltpu.CompilerParams(vmem_limit_bytes=8 * 1024 * 1024),
        name="fill_slots",
    )(*blocks)


def main_kernel(
    loss_scale,
    q_ref,
    k_ref,
    v_ref,
    a_ref,
    b_ref,
    km_ref,
    own_ref,
    near_ref,
    phi_ref,
    both_ref,
    psi_own_ref,
    dest_ref,
    ok_ref,
    diff_ref,
    buf_ref,
    s_scr,
    p_scr,
    psi_scr,
    key_scr,
    vp_scr,
    wide_scr,
):
    first_key = k_ref[0:1, :]
    all_ones = jnp.ones((BLOCK, BLOCK), BF16)
    ones = jnp.ones((TALL - HEAD_DIM, BLOCK), BF16)
    for i in range(CHUNKS):
        src = a_ref if i < 4 else b_ref
        for k in range(2):
            at = i * CHUNK + k * BLOCK
            one = ok_ref[2 * i + k : 2 * i + k + 1, :]
            other = (1.0 - one).astype(BF16)
            one = one.astype(BF16)
            value = src[i % 4, k, 1] * one
            key_scr[at : at + BLOCK, :] = src[i % 4, k, 0] * one + first_key * other
            vp_scr[:HEAD_DIM, at : at + BLOCK] = value.T
            vp_scr[HEAD_DIM:, at : at + BLOCK] = ones * one
            wide_scr[at : at + BLOCK, :BLOCK] = value
            wide_scr[at : at + BLOCK, BLOCK:] = all_ones * one
    vp_scr[:HEAD_DIM, FAR:] = v_ref[...].T
    vp_scr[HEAD_DIM:, FAR:] = ones
    early = lax.broadcasted_iota(jnp.int32, (BLOCK, CHUNK), 0) < WINDOW
    value_early = jnp.concatenate([v_ref[...], all_ones], axis=1)
    value_early = jnp.where(early, value_early.astype(F32), 0.0).astype(BF16)
    first_half = lax.broadcasted_iota(jnp.int32, (BLOCK, BLOCK), 1) < WINDOW
    dest = dest_ref[...]

    groups = HEADS // 2
    tops, sums = [None] * groups, [None] * groups

    def scores(g):
        query = jnp.concatenate(
            [q_ref[:, (2 * g + k) * BLOCK : (2 * g + k + 1) * BLOCK] for k in range(2)], axis=0
        )
        top = jnp.max(
            own_ref[:, g * CHUNK : (g + 1) * CHUNK].reshape(BLOCK // 8, 8, CHUNK), axis=0
        )
        for i in range(CHUNKS):
            s = dot(key_scr[i * CHUNK : (i + 1) * CHUNK, :], query, NT)
            s_scr[g % 2, i * CHUNK : (i + 1) * CHUNK, :] = s
            top = jnp.maximum(top, jnp.max(s.reshape(CHUNK // 8, 8, CHUNK), axis=0))
            yield
        tops[g] = jnp.max(top, axis=0, keepdims=True) * SCALE

    def features(g):
        for i in range(CHUNKS):
            keys = key_scr[i * CHUNK : (i + 1) * CHUNK, :]
            u = dot(km_ref[g * BLOCK : (g + 1) * BLOCK, :], keys, NT)
            psi = two_softmax(u.reshape(2, FEATURES, CHUNK)).reshape(CHUNK, CHUNK)
            psi_scr[g % 3, :, i * CHUNK : (i + 1) * CHUNK] = psi.astype(BF16)
            yield

    def weights(g):
        for i in range(CHUNKS):
            s = s_scr[g % 2, i * CHUNK : (i + 1) * CHUNK, :]
            w = jnp.exp2(s * SCALE - tops[g])
            p_scr[g % 2, i * CHUNK : (i + 1) * CHUNK, :] = w.astype(BF16)
            yield
        s = own_ref[:, g * CHUNK : (g + 1) * CHUNK]
        p_scr[g % 2, FAR:, :] = jnp.exp2(s * SCALE - tops[g]).astype(BF16)
        yield

    def mixes(g):
        mixed = dot(vp_scr[...], p_scr[g % 2])
        yield
        state = dot(psi_scr[g % 3], wide_scr[...])
        yield
        late = state + dot(psi_own_ref[g * CHUNK : (g + 1) * CHUNK, :], value_early)
        sums[g] = (mixed, state.astype(BF16), late.astype(BF16))
        yield

    def outputs(g):
        mixed, state, late = sums[g]
        heads = [2 * g, 2 * g + 1]
        parts = [slice(0, BLOCK), slice(BLOCK, CHUNK)]
        states = [jnp.concatenate([state[p], late[p]], axis=0) for p in parts]
        far = [dot(both_ref[h * BLOCK : (h + 1) * BLOCK, :], states[k]) for k, h in enumerate(heads)]
        yield
        total = jnp.concatenate(far, axis=0) + near_ref[g * CHUNK : (g + 1) * CHUNK, :]
        share = 1.0 / mixed[HEAD_DIM : HEAD_DIM + 1]
        teacher = mixed[:HEAD_DIM] * share
        teacher = jnp.concatenate([teacher[:, p].T for p in parts], axis=0).astype(BF16)
        yield
        moved = [dot(dest, teacher[p]) for p in parts]
        inverse = 1.0 / total[:, HEAD_DIM:]
        student = total[:, :HEAD_DIM] * inverse
        gap = student - teacher.astype(F32)
        for k in range(2):
            diff_ref[:, heads[k] * BLOCK : (heads[k] + 1) * BLOCK] = gap[parts[k]]
        yield
        grad_out = gap * (inverse * (2.0 * loss_scale))
        grad_both = jnp.concatenate([grad_out, -grad_out * student], axis=1).astype(BF16)
        yield
        dphi = [dot(states[k], grad_both[parts[k]], NT) for k in range(2)]
        yield
        for k in range(2):
            for shard in range(8):
                buf_ref[shard, :, heads[k] * BLOCK : (heads[k] + 1) * BLOCK] = moved[k][
                    shard * 16 : (shard + 1) * 16
                ].astype(BF16)
        yield
        du = []
        for k in range(2):
            phi = phi_ref[heads[k] * BLOCK : (heads[k] + 1) * BLOCK, :]
            terms = phi * jnp.where(first_half, dphi[k][:BLOCK], dphi[k][BLOCK:])
            up, down = phi[:FEATURES], phi[FEATURES:]
            du.append(
                terms[:FEATURES]
                - terms[FEATURES:]
                - up * jnp.sum(terms[:FEATURES], axis=0, keepdims=True)
                + down * jnp.sum(terms[FEATURES:], axis=0, keepdims=True)
            )
        yield
        for k in range(2):
            h = heads[k]
            grad = dot(du[k].astype(BF16), q_ref[:, h * BLOCK : (h + 1) * BLOCK]).astype(BF16)
            for i in range(4):
                at = (HEADS + i) * BLOCK
                buf_ref[h, :, at : at + BLOCK] = grad[i * 16 : (i + 1) * 16]
        yield

    for step in range(groups + 3):
        running = []
        for stage, length, late_by in (
            (scores, 9, 0),
            (features, 8, 0),
            (weights, 9, 1),
            (mixes, 3, 2),
            (outputs, 8, 3),
        ):
            if 0 <= step - late_by < groups:
                running.append((stage(step - late_by), length))
        marks = sorted(
            ((n + 0.5) / length, at) for at, (_, length) in enumerate(running) for n in range(length)
        )
        for _, at in marks:
            next(running[at][0], None)
        for stage, _ in running:
            for _ in stage:
                pass


def main_call(loss_scale, q, k, v, a, b, km, local):
    vmem = pl.BlockSpec(memory_space=pltpu.VMEM)
    return pl.pallas_call(
        functools.partial(main_kernel, loss_scale),
        out_shape=(
            jax.ShapeDtypeStruct((BLOCK, HEADS * HEAD_DIM), F32),
            jax.ShapeDtypeStruct((8, 16, 1536), BF16),
        ),
        in_specs=[vmem] * 13,
        out_specs=(vmem, vmem),
        scratch_shapes=[
            pltpu.VMEM((2, FAR, CHUNK), F32),
            pltpu.VMEM((2, FAR + BLOCK, CHUNK), BF16),
            pltpu.VMEM((3, CHUNK, FAR), BF16),
            pltpu.VMEM((FAR, BLOCK), BF16),
            pltpu.VMEM((TALL, FAR + BLOCK), BF16),
            pltpu.VMEM((FAR, CHUNK), BF16),
        ],
        compiler_params=pltpu.CompilerParams(vmem_limit_bytes=32 * 1024 * 1024),
        cost_estimate=pl.CostEstimate(
            flops=3_000_000_000, bytes_accessed=3_000_000, transcendentals=4_000_000
        ),
        name="transfer",
    )(q, k, v, a, b, km, *local)


def on_device(queries, keys, values, query_map, key_map, documents, assignment):
    c = lax.axis_index("c")
    query_rows = jnp.swapaxes(query_map, 1, 2).reshape(HEADS * FEATURES, HEAD_DIM)
    key_rows = jnp.swapaxes(key_map, 1, 2).reshape(HEADS * FEATURES, HEAD_DIM)
    shift1 = [(i, (i + 1) % 8) for i in range(8)]
    shift2 = [(i, (i + 2) % 8) for i in range(8)]
    plane0 = (keys[0], values[0])
    plane2 = tuple(lax.ppermute(each, "z", shift2) for each in plane0)
    plane1 = tuple(lax.ppermute(each, "z", shift1) for each in plane0)
    local = local_call(
        queries[0], keys[0], values[0], query_rows, key_rows, assignment[0], documents
    )
    plane1, plane2, local = lax.optimization_barrier((plane1, plane2, local))

    slots = slot_call(*plane0, *plane1, *plane2)
    mine = lax.all_to_all(slots, "y", 0, 0, tiled=True)
    other = lax.ppermute(mine, "c", [(0, 1), (1, 0)])
    loss_scale = HEAD_DIM / math.sqrt(4 * 64 * BLOCK)
    difference, outgoing = main_call(
        loss_scale, queries[0], keys[0], values[0], mine, other, key_rows, local
    )
    got = lax.all_to_all(outgoing, ("y", "c"), 0, 0, tiled=True)
    relay = got[:, :, :1024].reshape(8, 8, 2, 1024).transpose(1, 0, 2, 3).reshape(8, 16, 1024)
    part = jnp.sum(got[:, :, 1024:].astype(F32), axis=0).astype(BF16)
    part = jnp.broadcast_to(part[None], (8, 16, 512))
    got = lax.all_to_all(jnp.concatenate([relay, part], axis=2), "z", 0, 0, tiled=True)
    relaid = got[:, :, :1024].reshape(1, BLOCK, 1024)
    part = jnp.sum(got[:, :, 1024:].astype(F32), axis=0).astype(BF16)
    part = part.reshape(16, 4, HEAD_DIM).transpose(1, 0, 2).reshape(FEATURES, HEAD_DIM)
    part = jnp.broadcast_to(part[None], (16, FEATURES, HEAD_DIM))
    got = lax.all_to_all(part, ("x", "y"), 0, 0, tiled=True)
    part = jnp.sum(got.reshape(4, 4, FEATURES, HEAD_DIM).astype(F32), axis=0).astype(BF16)
    far = lax.ppermute(part, "c", [(0, 1), (1, 0)])
    mine_first = lax.broadcasted_iota(jnp.int32, (4, 2, FEATURES, HEAD_DIM), 1) == c
    grad = jnp.where(mine_first, part[:, None], far[:, None]).astype(F32)
    grad = grad.reshape(HEADS, FEATURES, HEAD_DIM)
    return relaid, difference[None], jnp.swapaxes(grad, 1, 2)


def solution(mesh):
    split = Mesh(np.array(mesh.devices).reshape(4, 8, 4, 2), ("x", "z", "y", "c"))
    ctx = ("z", "y", "c")
    return jax.shard_map(
        on_device,
        mesh=split,
        in_specs=(
            P("x", ctx, None),
            P("x", ctx, None),
            P("x", ctx, None),
            P(),
            P(),
            P("x", None),
            P("x", None, None),
        ),
        out_specs=(P("x", ctx, None), P("x", ctx, None), P()),
        check_vma=False,
    )
```

```python
import functools
import math

import jax
import jax.numpy as jnp
import numpy as np
from jax import lax
from jax.experimental import pallas as pl
from jax.experimental.pallas import tpu as pltpu
from jax.sharding import Mesh, PartitionSpec as P

HEAD_DIM = 128
WINDOW = 64
BLOCK = 128
HEADS = 8
FEATURES = 64
ROWS = HEADS * BLOCK
CHUNK = 2 * BLOCK
CHUNKS = 8
FAR = CHUNK * CHUNKS
SCALE = math.log2(math.e) / math.sqrt(HEAD_DIM)
NEGATIVE = -1e30
NT = (((1,), (1,)), ((), ()))
NN = (((1,), (0,)), ((), ()))
TN = (((0,), (0,)), ((), ()))
TALL = HEAD_DIM + 16
F32 = jnp.float32
BF16 = jnp.bfloat16
LOG2E = math.log2(math.e)


def dot(a, b, dims=NN):
    return lax.dot_general(a, b, dims, preferred_element_type=F32)


def two_softmax(u):
    u = u * LOG2E
    top = jnp.max(u, axis=1, keepdims=True)
    low = jnp.min(u, axis=1, keepdims=True)
    up = jnp.exp2(u - top)
    down = jnp.exp2(low - u)
    up = up * (1.0 / jnp.sum(up, axis=1, keepdims=True))
    down = down * (1.0 / jnp.sum(down, axis=1, keepdims=True))
    return jnp.concatenate([up, down], axis=1)


def in_hbm(x):
    return pltpu.with_memory_space_constraint(x, pltpu.HBM)


def iota(shape, axis):
    return lax.broadcasted_iota(jnp.int32, shape, axis)


def place_kernel(
    km_hbm, route_hbm, doc_hbm, k_hbm, psi_ref, dest_ref, ok_ref, km_ref, route_ref, doc_ref, k_ref, sems
):
    pairs = ((route_hbm, route_ref), (doc_hbm, doc_ref), (k_hbm, k_ref), (km_hbm, km_ref))
    copies = [pltpu.make_async_copy(a, b, sems.at[n]) for n, (a, b) in enumerate(pairs)]
    for copy in copies:
        copy.start()
    copies[0].wait()
    copies[1].wait()
    z, y, c = lax.axis_index("z"), lax.axis_index("y"), lax.axis_index("c")
    here = (z * 4 + y) * 2 + c
    place = iota((2 * CHUNKS, 64), 0)
    block = iota((2 * CHUNKS, 64), 1)
    from_y = lax.shift_right_logical(place, 1) & 3
    from_c = jnp.where(place < CHUNKS, c, 1 - c)
    first = jnp.where(from_y < y, 0, jnp.where(from_y > y, 1, 2 * from_c))
    second = jnp.where(from_y > y, 2, 1)
    source = (z - jnp.where((place & 1) == 0, first, second)) * 8 + from_y * 2 + from_c
    documents = doc_ref[...]
    own_document = jnp.sum(jnp.where(iota((1, 64), 1) == here, documents, 0), axis=1, keepdims=True)
    same = (documents == own_document) & (iota((1, 64), 1) < here) & (iota((1, 64), 1) > here - 16)
    found = jnp.where((source == block) & same, 1.0, 0.0)
    ok_ref[...] = jnp.broadcast_to(jnp.max(found, axis=1, keepdims=True), ok_ref.shape)
    shard = route_ref[pl.ds(here, 1), :]
    order = (shard & 7) * 8 + lax.shift_right_logical(shard, 3)
    pieces = (iota((64, 64), 0) == order).astype(BF16)
    rows = (lax.shift_right_logical(iota((BLOCK, 64), 0), 1) == iota((BLOCK, 64), 1)).astype(BF16)
    tokens = (iota((64, BLOCK), 0) == lax.shift_right_logical(iota((64, BLOCK), 1), 1)).astype(BF16)
    placed = dot(dot(rows, pieces).astype(BF16), tokens)
    parity = (iota((BLOCK, BLOCK), 0) & 1) == (iota((BLOCK, BLOCK), 1) & 1)
    dest_ref[...] = jnp.where(parity, placed, 0.0).astype(BF16)
    copies[2].wait()
    copies[3].wait()
    psi = two_softmax(dot(km_ref[...], k_ref[...], NT).reshape(HEADS, FEATURES, BLOCK))
    psi_ref[...] = psi.reshape(ROWS, BLOCK).astype(BF16)


def place_call(k, km, routes, documents):
    vmem = pl.BlockSpec(memory_space=pltpu.VMEM)
    return pl.pallas_call(
        place_kernel,
        out_shape=(
            jax.ShapeDtypeStruct((ROWS, BLOCK), BF16),
            jax.ShapeDtypeStruct((BLOCK, BLOCK), BF16),
            jax.ShapeDtypeStruct((2 * CHUNKS, BLOCK), F32),
        ),
        in_specs=[pl.BlockSpec(memory_space=pltpu.HBM)] * 4,
        out_specs=(vmem,) * 3,
        scratch_shapes=[
            pltpu.VMEM((HEADS * FEATURES, HEAD_DIM), BF16),
            pltpu.VMEM((64, 64), jnp.int32),
            pltpu.VMEM((1, 64), jnp.int32),
            pltpu.VMEM((BLOCK, HEAD_DIM), BF16),
            pltpu.SemaphoreType.DMA((4,)),
        ],
        compiler_params=pltpu.CompilerParams(vmem_limit_bytes=8 * 1024 * 1024),
        cost_estimate=pl.CostEstimate(
            flops=100_000_000, bytes_accessed=1_000_000, transcendentals=200_000
        ),
        name="place",
    )(*[in_hbm(each) for each in (km, routes, documents, k)])


def local_kernel(q_ref, k_ref, v_ref, qm_ref, own_ref, near_ref, phi_ref, both_ref):
    keys = k_ref[...]
    values = jnp.concatenate([v_ref[...], jnp.ones((BLOCK, BLOCK), BF16)], axis=1)
    col = iota((BLOCK, BLOCK), 1)
    row = iota((BLOCK, BLOCK), 0)
    causal = row <= col
    near = causal & ((col < WINDOW) == (row < WINDOW))
    first_half = col < WINDOW
    for h in range(HEADS):
        at = h * BLOCK
        query = q_ref[:, at : at + BLOCK]
        scores = dot(keys, query, NT)
        own_ref[:, at : at + BLOCK] = jnp.where(causal, scores, NEGATIVE)
        window = jnp.where(near, scores * SCALE, NEGATIVE)
        weights = jnp.exp2(window - jnp.max(window, axis=0, keepdims=True))
        near_ref[at : at + BLOCK, :] = dot(weights.T.astype(BF16), values)
        u = dot(qm_ref[h * FEATURES : (h + 1) * FEATURES, :], query, NT)
        phi = two_softmax(u[None])[0]
        phi_ref[at : at + BLOCK, :] = phi
        both = jnp.concatenate(
            [jnp.where(first_half, phi, 0.0), jnp.where(first_half, 0.0, phi)], axis=0
        )
        both_ref[at : at + BLOCK, :] = both.T.astype(BF16)


def local_call(q, k, v, qm):
    vmem = pl.BlockSpec(memory_space=pltpu.VMEM)
    return pl.pallas_call(
        local_kernel,
        out_shape=(
            jax.ShapeDtypeStruct((BLOCK, ROWS), F32),
            jax.ShapeDtypeStruct((ROWS, CHUNK), F32),
            jax.ShapeDtypeStruct((ROWS, BLOCK), F32),
            jax.ShapeDtypeStruct((ROWS, CHUNK), BF16),
        ),
        in_specs=[vmem] * 4,
        out_specs=(vmem,) * 4,
        compiler_params=pltpu.CompilerParams(vmem_limit_bytes=16 * 1024 * 1024),
        cost_estimate=pl.CostEstimate(
            flops=400_000_000, bytes_accessed=4_000_000, transcendentals=500_000
        ),
        name="local_block",
    )(q, k, v, qm)


def slot_kernel(now_ref, back1_ref, back2_ref, out_ref):
    y, c = lax.axis_index("y"), lax.axis_index("c")
    planes = (now_ref, back1_ref, back2_ref)

    def put(d, k, plane):
        out_ref[d, k] = planes[plane][...]

    for d in range(4):

        @pl.when(d > y)
        def _():
            put(d, 0, 0)
            put(d, 1, 1)

        @pl.when(d < y)
        def _():
            put(d, 0, 1)
            put(d, 1, 2)

        @pl.when((d == y) & (c == 0))
        def _():
            put(d, 0, 0)
            put(d, 1, 1)

        @pl.when((d == y) & (c == 1))
        def _():
            put(d, 0, 2)
            put(d, 1, 1)


def slot_call(*blocks):
    vmem = pl.BlockSpec(memory_space=pltpu.VMEM)
    return pl.pallas_call(
        slot_kernel,
        out_shape=jax.ShapeDtypeStruct((4, 2, 2, BLOCK, HEAD_DIM), BF16),
        in_specs=[vmem] * 3,
        out_specs=vmem,
        compiler_params=pltpu.CompilerParams(vmem_limit_bytes=8 * 1024 * 1024),
        name="fill_slots",
    )(*blocks)


def main_kernel(
    loss_scale,
    q_ref,
    k_ref,
    v_ref,
    a_ref,
    b_ref,
    km_ref,
    own_ref,
    near_ref,
    phi_ref,
    both_ref,
    psi_own_ref,
    dest_ref,
    ok_ref,
    diff_ref,
    buf_ref,
    s_scr,
    p_scr,
    psi_scr,
    key_scr,
    vp_scr,
    wide_scr,
):
    first_key = k_ref[0:1, :]
    all_ones = jnp.ones((BLOCK, BLOCK), BF16)
    ones = jnp.ones((TALL - HEAD_DIM, BLOCK), BF16)
    for i in range(CHUNKS):
        src = a_ref if i < 4 else b_ref
        for k in range(2):
            at = i * CHUNK + k * BLOCK
            one = ok_ref[2 * i + k : 2 * i + k + 1, :]
            other = (1.0 - one).astype(BF16)
            one = one.astype(BF16)
            value = src[i % 4, k, 1] * one
            key_scr[at : at + BLOCK, :] = src[i % 4, k, 0] * one + first_key * other
            vp_scr[:HEAD_DIM, at : at + BLOCK] = value.T
            vp_scr[HEAD_DIM:, at : at + BLOCK] = ones * one
            wide_scr[at : at + BLOCK, :BLOCK] = value
            wide_scr[at : at + BLOCK, BLOCK:] = all_ones * one
    vp_scr[:HEAD_DIM, FAR:] = v_ref[...].T
    vp_scr[HEAD_DIM:, FAR:] = ones
    early = lax.broadcasted_iota(jnp.int32, (BLOCK, CHUNK), 0) < WINDOW
    value_early = jnp.concatenate([v_ref[...], all_ones], axis=1)
    value_early = jnp.where(early, value_early.astype(F32), 0.0).astype(BF16)
    first_half = lax.broadcasted_iota(jnp.int32, (BLOCK, BLOCK), 1) < WINDOW
    dest = dest_ref[...]

    groups = HEADS // 2
    tops, sums = [None] * groups, [None] * groups

    def scores(g):
        query = jnp.concatenate(
            [q_ref[:, (2 * g + k) * BLOCK : (2 * g + k + 1) * BLOCK] for k in range(2)], axis=0
        )
        top = jnp.max(
            own_ref[:, g * CHUNK : (g + 1) * CHUNK].reshape(BLOCK // 8, 8, CHUNK), axis=0
        )
        for i in range(CHUNKS):
            s = dot(key_scr[i * CHUNK : (i + 1) * CHUNK, :], query, NT)
            s_scr[g % 2, i * CHUNK : (i + 1) * CHUNK, :] = s
            top = jnp.maximum(top, jnp.max(s.reshape(CHUNK // 8, 8, CHUNK), axis=0))
            yield
        tops[g] = jnp.max(top, axis=0, keepdims=True) * SCALE

    def features(g):
        for i in range(CHUNKS):
            keys = key_scr[i * CHUNK : (i + 1) * CHUNK, :]
            u = dot(km_ref[g * BLOCK : (g + 1) * BLOCK, :], keys, NT)
            psi = two_softmax(u.reshape(2, FEATURES, CHUNK)).reshape(CHUNK, CHUNK)
            psi_scr[g % 3, :, i * CHUNK : (i + 1) * CHUNK] = psi.astype(BF16)
            yield

    def weights(g):
        for i in range(CHUNKS):
            s = s_scr[g % 2, i * CHUNK : (i + 1) * CHUNK, :]
            w = jnp.exp2(s * SCALE - tops[g])
            p_scr[g % 2, i * CHUNK : (i + 1) * CHUNK, :] = w.astype(BF16)
            yield
        s = own_ref[:, g * CHUNK : (g + 1) * CHUNK]
        p_scr[g % 2, FAR:, :] = jnp.exp2(s * SCALE - tops[g]).astype(BF16)
        yield

    def mixes(g):
        mixed = dot(vp_scr[...], p_scr[g % 2])
        yield
        state = dot(psi_scr[g % 3], wide_scr[...])
        yield
        late = state + dot(psi_own_ref[g * CHUNK : (g + 1) * CHUNK, :], value_early)
        sums[g] = (mixed, state.astype(BF16), late.astype(BF16))
        yield

    def outputs(g):
        mixed, state, late = sums[g]
        heads = [2 * g, 2 * g + 1]
        parts = [slice(0, BLOCK), slice(BLOCK, CHUNK)]
        states = [jnp.concatenate([state[p], late[p]], axis=0) for p in parts]
        far = [dot(both_ref[h * BLOCK : (h + 1) * BLOCK, :], states[k]) for k, h in enumerate(heads)]
        yield
        total = jnp.concatenate(far, axis=0) + near_ref[g * CHUNK : (g + 1) * CHUNK, :]
        share = 1.0 / mixed[HEAD_DIM : HEAD_DIM + 1]
        teacher = mixed[:HEAD_DIM] * share
        teacher = jnp.concatenate([teacher[:, p].T for p in parts], axis=0).astype(BF16)
        yield
        moved = [dot(dest, teacher[p]) for p in parts]
        inverse = 1.0 / total[:, HEAD_DIM:]
        student = total[:, :HEAD_DIM] * inverse
        gap = student - teacher.astype(F32)
        for k in range(2):
            diff_ref[:, heads[k] * BLOCK : (heads[k] + 1) * BLOCK] = gap[parts[k]]
        yield
        grad_out = gap * (inverse * (2.0 * loss_scale))
        grad_both = jnp.concatenate([grad_out, -grad_out * student], axis=1).astype(BF16)
        yield
        dphi = [dot(states[k], grad_both[parts[k]], NT) for k in range(2)]
        yield
        for k in range(2):
            for shard in range(8):
                buf_ref[shard, :, heads[k] * BLOCK : (heads[k] + 1) * BLOCK] = moved[k][
                    shard * 16 : (shard + 1) * 16
                ].astype(BF16)
        yield
        du = []
        for k in range(2):
            phi = phi_ref[heads[k] * BLOCK : (heads[k] + 1) * BLOCK, :]
            terms = phi * jnp.where(first_half, dphi[k][:BLOCK], dphi[k][BLOCK:])
            up, down = phi[:FEATURES], phi[FEATURES:]
            du.append(
                terms[:FEATURES]
                - terms[FEATURES:]
                - up * jnp.sum(terms[:FEATURES], axis=0, keepdims=True)
                + down * jnp.sum(terms[FEATURES:], axis=0, keepdims=True)
            )
        yield
        for k in range(2):
            h = heads[k]
            grad = dot(du[k].astype(BF16), q_ref[:, h * BLOCK : (h + 1) * BLOCK]).astype(BF16)
            for i in range(4):
                at = (HEADS + i) * BLOCK
                buf_ref[h, :, at : at + BLOCK] = grad[i * 16 : (i + 1) * 16]
        yield

    for step in range(groups + 3):
        running = []
        for stage, length, late_by in (
            (scores, 9, 0),
            (features, 8, 0),
            (weights, 9, 1),
            (mixes, 3, 2),
            (outputs, 8, 3),
        ):
            if 0 <= step - late_by < groups:
                running.append((stage(step - late_by), length))
        marks = sorted(
            ((n + 0.5) / length, at) for at, (_, length) in enumerate(running) for n in range(length)
        )
        for _, at in marks:
            next(running[at][0], None)
        for stage, _ in running:
            for _ in stage:
                pass


def main_call(loss_scale, q, k, v, a, b, km, local):
    vmem = pl.BlockSpec(memory_space=pltpu.VMEM)
    return pl.pallas_call(
        functools.partial(main_kernel, loss_scale),
        out_shape=(
            jax.ShapeDtypeStruct((BLOCK, HEADS * HEAD_DIM), F32),
            jax.ShapeDtypeStruct((8, 16, 1536), BF16),
        ),
        in_specs=[vmem] * 13,
        out_specs=(vmem, vmem),
        scratch_shapes=[
            pltpu.VMEM((2, FAR, CHUNK), F32),
            pltpu.VMEM((2, FAR + BLOCK, CHUNK), BF16),
            pltpu.VMEM((3, CHUNK, FAR), BF16),
            pltpu.VMEM((FAR, BLOCK), BF16),
            pltpu.VMEM((TALL, FAR + BLOCK), BF16),
            pltpu.VMEM((FAR, CHUNK), BF16),
        ],
        compiler_params=pltpu.CompilerParams(vmem_limit_bytes=32 * 1024 * 1024),
        cost_estimate=pl.CostEstimate(
            flops=3_000_000_000, bytes_accessed=3_000_000, transcendentals=4_000_000
        ),
        name="transfer",
    )(q, k, v, a, b, km, *local)


def on_device(queries, keys, values, query_map, key_map, documents, assignment):
    c = lax.axis_index("c")
    query_rows = jnp.swapaxes(query_map, 1, 2).reshape(HEADS * FEATURES, HEAD_DIM)
    key_rows = jnp.swapaxes(key_map, 1, 2).reshape(HEADS * FEATURES, HEAD_DIM)
    shift1 = [(i, (i + 1) % 8) for i in range(8)]
    shift2 = [(i, (i + 2) % 8) for i in range(8)]
    plane0 = jnp.stack([keys[0], values[0]])
    plane2 = lax.ppermute(plane0, "z", shift2)
    plane1 = lax.ppermute(plane0, "z", shift1)
    placed = place_call(keys[0], key_rows, assignment[0], documents)
    plane1, plane2, placed = lax.optimization_barrier((plane1, plane2, placed))
    slots = slot_call(plane0, plane1, plane2)
    mine = lax.all_to_all(slots, "y", 0, 0, tiled=True)
    other = lax.ppermute(mine, "c", [(0, 1), (1, 0)])
    query, _ = lax.optimization_barrier((queries[0], mine))
    local = local_call(query, keys[0], values[0], query_rows) + tuple(placed)
    loss_scale = HEAD_DIM / math.sqrt(4 * 64 * BLOCK)
    difference, outgoing = main_call(
        loss_scale, query, keys[0], values[0], mine, other, key_rows, local
    )
    got = lax.all_to_all(outgoing, ("y", "c"), 0, 0, tiled=True)
    relay = got[:, :, :1024].reshape(8, 8, 2, 1024).transpose(1, 0, 2, 3).reshape(8, 16, 1024)
    part = jnp.sum(got[:, :, 1024:].astype(F32), axis=0).astype(BF16)
    part = jnp.broadcast_to(part[None], (8, 16, 512))
    got = lax.all_to_all(jnp.concatenate([relay, part], axis=2), "z", 0, 0, tiled=True)
    relay = got
    part = jnp.sum(got[:, :, 1024:].astype(F32), axis=0).astype(BF16)
    part = part.reshape(16, 4, HEAD_DIM).transpose(1, 0, 2).reshape(FEATURES, HEAD_DIM)
    part = jnp.broadcast_to(part[None], (16, FEATURES, HEAD_DIM))
    got = lax.all_to_all(part, ("x", "y"), 0, 0, tiled=True)
    part = jnp.sum(got.reshape(4, 4, FEATURES, HEAD_DIM).astype(F32), axis=0).astype(BF16)
    relay, part = lax.optimization_barrier((relay, part))
    far = lax.ppermute(part, "c", [(0, 1), (1, 0)])
    relaid = relay[:, :, :1024].reshape(1, BLOCK, 1024)
    mine_first = lax.broadcasted_iota(jnp.int32, (4, 2, FEATURES, HEAD_DIM), 1) == c
    grad = jnp.where(mine_first, part[:, None], far[:, None]).astype(F32)
    grad = grad.reshape(HEADS, FEATURES, HEAD_DIM)
    return relaid, difference[None], jnp.swapaxes(grad, 1, 2)


def solution(mesh):
    split = Mesh(np.array(mesh.devices).reshape(4, 8, 4, 2), ("x", "z", "y", "c"))
    ctx = ("z", "y", "c")
    return jax.shard_map(
        on_device,
        mesh=split,
        in_specs=(
            P("x", ctx, None),
            P("x", ctx, None),
            P("x", ctx, None),
            P(),
            P(),
            P("x", None),
            P("x", None, None),
        ),
        out_specs=(P("x", ctx, None), P("x", ctx, None), P()),
        check_vma=False,
    )
```

```python
import functools
import math

import jax
import jax.numpy as jnp
import numpy as np
from jax import lax
from jax.experimental import pallas as pl
from jax.experimental.pallas import tpu as pltpu
from jax.sharding import Mesh, PartitionSpec as P

HEAD_DIM = 128
WINDOW = 64
BLOCK = 128
HEADS = 8
FEATURES = 64
ROWS = HEADS * BLOCK
CHUNK = 2 * BLOCK
CHUNKS = 8
FAR = CHUNK * CHUNKS
SCALE = math.log2(math.e) / math.sqrt(HEAD_DIM)
NEGATIVE = -1e30
NT = (((1,), (1,)), ((), ()))
NN = (((1,), (0,)), ((), ()))
TN = (((0,), (0,)), ((), ()))
TALL = HEAD_DIM + 16
F32 = jnp.float32
BF16 = jnp.bfloat16
LOG2E = math.log2(math.e)


def dot(a, b, dims=NN):
    return lax.dot_general(a, b, dims, preferred_element_type=F32)


def two_softmax(u):
    u = u * LOG2E
    top = jnp.max(u, axis=1, keepdims=True)
    low = jnp.min(u, axis=1, keepdims=True)
    up = jnp.exp2(u - top)
    down = jnp.exp2(low - u)
    up = up * (1.0 / jnp.sum(up, axis=1, keepdims=True))
    down = down * (1.0 / jnp.sum(down, axis=1, keepdims=True))
    return jnp.concatenate([up, down], axis=1)


def in_hbm(x):
    return pltpu.with_memory_space_constraint(x, pltpu.HBM)


def iota(shape, axis):
    return lax.broadcasted_iota(jnp.int32, shape, axis)


def pack_kernel(k_hbm, v_hbm, out_ref, sems):
    copies = [
        pltpu.make_async_copy(k_hbm, out_ref.at[0], sems.at[0]),
        pltpu.make_async_copy(v_hbm, out_ref.at[1], sems.at[1]),
    ]
    for copy in copies:
        copy.start()
    for copy in copies:
        copy.wait()


def pack_call(k, v):
    return pl.pallas_call(
        pack_kernel,
        out_shape=jax.ShapeDtypeStruct((2, BLOCK, HEAD_DIM), BF16),
        in_specs=[pl.BlockSpec(memory_space=pltpu.HBM)] * 2,
        out_specs=pl.BlockSpec(memory_space=pltpu.VMEM),
        scratch_shapes=[pltpu.SemaphoreType.DMA((2,))],
        compiler_params=pltpu.CompilerParams(vmem_limit_bytes=8 * 1024 * 1024),
        name="pack_block",
    )(in_hbm(k), in_hbm(v))


def place_kernel(
    km_hbm, route_hbm, doc_hbm, k_hbm, psi_ref, dest_ref, ok_ref, km_ref, route_ref, doc_ref, k_ref, sems
):
    pairs = ((route_hbm, route_ref), (doc_hbm, doc_ref), (k_hbm, k_ref), (km_hbm, km_ref))
    copies = [pltpu.make_async_copy(a, b, sems.at[n]) for n, (a, b) in enumerate(pairs)]
    for copy in copies:
        copy.start()
    copies[0].wait()
    copies[1].wait()
    z, y, c = lax.axis_index("z"), lax.axis_index("y"), lax.axis_index("c")
    here = (z * 4 + y) * 2 + c
    place = iota((2 * CHUNKS, 64), 0)
    block = iota((2 * CHUNKS, 64), 1)
    from_y = lax.shift_right_logical(place, 1) & 3
    from_c = jnp.where(place < CHUNKS, c, 1 - c)
    first = jnp.where(from_y < y, 0, jnp.where(from_y > y, 1, 2 * from_c))
    second = jnp.where(from_y > y, 2, 1)
    source = (z - jnp.where((place & 1) == 0, first, second)) * 8 + from_y * 2 + from_c
    documents = doc_ref[...]
    own_document = jnp.sum(jnp.where(iota((1, 64), 1) == here, documents, 0), axis=1, keepdims=True)
    same = (documents == own_document) & (iota((1, 64), 1) < here) & (iota((1, 64), 1) > here - 16)
    found = jnp.where((source == block) & same, 1.0, 0.0)
    ok_ref[...] = jnp.broadcast_to(jnp.max(found, axis=1, keepdims=True), ok_ref.shape)
    shard = route_ref[pl.ds(here, 1), :]
    order = (shard & 7) * 8 + lax.shift_right_logical(shard, 3)
    pieces = (iota((64, 64), 0) == order).astype(BF16)
    rows = (lax.shift_right_logical(iota((BLOCK, 64), 0), 1) == iota((BLOCK, 64), 1)).astype(BF16)
    tokens = (iota((64, BLOCK), 0) == lax.shift_right_logical(iota((64, BLOCK), 1), 1)).astype(BF16)
    placed = dot(dot(rows, pieces).astype(BF16), tokens)
    parity = (iota((BLOCK, BLOCK), 0) & 1) == (iota((BLOCK, BLOCK), 1) & 1)
    dest_ref[...] = jnp.where(parity, placed, 0.0).astype(BF16)
    copies[2].wait()
    copies[3].wait()
    psi = two_softmax(dot(km_ref[...], k_ref[...], NT).reshape(HEADS, FEATURES, BLOCK))
    psi_ref[...] = psi.reshape(ROWS, BLOCK).astype(BF16)


def place_call(k, km, routes, documents):
    vmem = pl.BlockSpec(memory_space=pltpu.VMEM)
    return pl.pallas_call(
        place_kernel,
        out_shape=(
            jax.ShapeDtypeStruct((ROWS, BLOCK), BF16),
            jax.ShapeDtypeStruct((BLOCK, BLOCK), BF16),
            jax.ShapeDtypeStruct((2 * CHUNKS, BLOCK), F32),
        ),
        in_specs=[pl.BlockSpec(memory_space=pltpu.HBM)] * 4,
        out_specs=(vmem,) * 3,
        scratch_shapes=[
            pltpu.VMEM((HEADS * FEATURES, HEAD_DIM), BF16),
            pltpu.VMEM((64, 64), jnp.int32),
            pltpu.VMEM((1, 64), jnp.int32),
            pltpu.VMEM((BLOCK, HEAD_DIM), BF16),
            pltpu.SemaphoreType.DMA((4,)),
        ],
        compiler_params=pltpu.CompilerParams(vmem_limit_bytes=8 * 1024 * 1024),
        cost_estimate=pl.CostEstimate(
            flops=100_000_000, bytes_accessed=1_000_000, transcendentals=200_000
        ),
        name="place",
    )(*[in_hbm(each) for each in (km, routes, documents, k)])


def local_kernel(q_ref, k_ref, v_ref, qm_ref, own_ref, near_ref, phi_ref, both_ref):
    keys = k_ref[...]
    values = jnp.concatenate([v_ref[...], jnp.ones((BLOCK, BLOCK), BF16)], axis=1)
    col = iota((BLOCK, BLOCK), 1)
    row = iota((BLOCK, BLOCK), 0)
    causal = row <= col
    near = causal & ((col < WINDOW) == (row < WINDOW))
    first_half = col < WINDOW
    for h in range(HEADS):
        at = h * BLOCK
        query = q_ref[:, at : at + BLOCK]
        scores = dot(keys, query, NT)
        own_ref[:, at : at + BLOCK] = jnp.where(causal, scores, NEGATIVE)
        window = jnp.where(near, scores * SCALE, NEGATIVE)
        weights = jnp.exp2(window - jnp.max(window, axis=0, keepdims=True))
        near_ref[at : at + BLOCK, :] = dot(weights.T.astype(BF16), values)
        u = dot(qm_ref[h * FEATURES : (h + 1) * FEATURES, :], query, NT)
        phi = two_softmax(u[None])[0]
        phi_ref[at : at + BLOCK, :] = phi
        both = jnp.concatenate(
            [jnp.where(first_half, phi, 0.0), jnp.where(first_half, 0.0, phi)], axis=0
        )
        both_ref[at : at + BLOCK, :] = both.T.astype(BF16)


def local_call(q, k, v, qm):
    vmem = pl.BlockSpec(memory_space=pltpu.VMEM)
    return pl.pallas_call(
        local_kernel,
        out_shape=(
            jax.ShapeDtypeStruct((BLOCK, ROWS), F32),
            jax.ShapeDtypeStruct((ROWS, CHUNK), F32),
            jax.ShapeDtypeStruct((ROWS, BLOCK), F32),
            jax.ShapeDtypeStruct((ROWS, CHUNK), BF16),
        ),
        in_specs=[vmem] * 4,
        out_specs=(vmem,) * 4,
        compiler_params=pltpu.CompilerParams(vmem_limit_bytes=16 * 1024 * 1024),
        cost_estimate=pl.CostEstimate(
            flops=400_000_000, bytes_accessed=4_000_000, transcendentals=500_000
        ),
        name="local_block",
    )(q, k, v, qm)


def slot_kernel(now_ref, back1_ref, back2_ref, out_ref):
    y, c = lax.axis_index("y"), lax.axis_index("c")
    planes = (now_ref, back1_ref, back2_ref)

    def put(d, k, plane):
        out_ref[d, k] = planes[plane][...]

    for d in range(4):

        @pl.when(d > y)
        def _():
            put(d, 0, 0)
            put(d, 1, 1)

        @pl.when(d < y)
        def _():
            put(d, 0, 1)
            put(d, 1, 2)

        @pl.when((d == y) & (c == 0))
        def _():
            put(d, 0, 0)
            put(d, 1, 1)

        @pl.when((d == y) & (c == 1))
        def _():
            put(d, 0, 2)
            put(d, 1, 1)


def slot_call(*blocks):
    vmem = pl.BlockSpec(memory_space=pltpu.VMEM)
    return pl.pallas_call(
        slot_kernel,
        out_shape=jax.ShapeDtypeStruct((4, 2, 2, BLOCK, HEAD_DIM), BF16),
        in_specs=[vmem] * 3,
        out_specs=vmem,
        compiler_params=pltpu.CompilerParams(vmem_limit_bytes=8 * 1024 * 1024),
        name="fill_slots",
    )(*blocks)


def main_kernel(
    loss_scale,
    q_ref,
    k_ref,
    v_ref,
    a_ref,
    b_ref,
    km_ref,
    own_ref,
    near_ref,
    phi_ref,
    both_ref,
    psi_own_ref,
    dest_ref,
    ok_ref,
    diff_ref,
    buf_ref,
    s_scr,
    p_scr,
    psi_scr,
    key_scr,
    vp_scr,
    wide_scr,
):
    first_key = k_ref[0:1, :]
    all_ones = jnp.ones((BLOCK, BLOCK), BF16)
    ones = jnp.ones((TALL - HEAD_DIM, BLOCK), BF16)
    for i in range(CHUNKS):
        src = a_ref if i < 4 else b_ref
        for k in range(2):
            at = i * CHUNK + k * BLOCK
            one = ok_ref[2 * i + k : 2 * i + k + 1, :]
            other = (1.0 - one).astype(BF16)
            one = one.astype(BF16)
            value = src[i % 4, k, 1] * one
            key_scr[at : at + BLOCK, :] = src[i % 4, k, 0] * one + first_key * other
            vp_scr[:HEAD_DIM, at : at + BLOCK] = value.T
            vp_scr[HEAD_DIM:, at : at + BLOCK] = ones * one
            wide_scr[at : at + BLOCK, :BLOCK] = value
            wide_scr[at : at + BLOCK, BLOCK:] = all_ones * one
    vp_scr[:HEAD_DIM, FAR:] = v_ref[...].T
    vp_scr[HEAD_DIM:, FAR:] = ones
    early = lax.broadcasted_iota(jnp.int32, (BLOCK, CHUNK), 0) < WINDOW
    value_early = jnp.concatenate([v_ref[...], all_ones], axis=1)
    value_early = jnp.where(early, value_early.astype(F32), 0.0).astype(BF16)
    first_half = lax.broadcasted_iota(jnp.int32, (BLOCK, BLOCK), 1) < WINDOW
    dest = dest_ref[...]

    groups = HEADS // 2
    tops, sums = [None] * groups, [None] * groups

    def scores(g):
        query = jnp.concatenate(
            [q_ref[:, (2 * g + k) * BLOCK : (2 * g + k + 1) * BLOCK] for k in range(2)], axis=0
        )
        top = jnp.max(
            own_ref[:, g * CHUNK : (g + 1) * CHUNK].reshape(BLOCK // 8, 8, CHUNK), axis=0
        )
        for i in range(CHUNKS):
            s = dot(key_scr[i * CHUNK : (i + 1) * CHUNK, :], query, NT)
            s_scr[g % 2, i * CHUNK : (i + 1) * CHUNK, :] = s
            top = jnp.maximum(top, jnp.max(s.reshape(CHUNK // 8, 8, CHUNK), axis=0))
            yield
        tops[g] = jnp.max(top, axis=0, keepdims=True) * SCALE

    def features(g):
        for i in range(CHUNKS):
            keys = key_scr[i * CHUNK : (i + 1) * CHUNK, :]
            u = dot(km_ref[g * BLOCK : (g + 1) * BLOCK, :], keys, NT)
            psi = two_softmax(u.reshape(2, FEATURES, CHUNK)).reshape(CHUNK, CHUNK)
            psi_scr[g % 3, :, i * CHUNK : (i + 1) * CHUNK] = psi.astype(BF16)
            yield

    def weights(g):
        for i in range(CHUNKS):
            s = s_scr[g % 2, i * CHUNK : (i + 1) * CHUNK, :]
            w = jnp.exp2(s * SCALE - tops[g])
            p_scr[g % 2, i * CHUNK : (i + 1) * CHUNK, :] = w.astype(BF16)
            yield
        s = own_ref[:, g * CHUNK : (g + 1) * CHUNK]
        p_scr[g % 2, FAR:, :] = jnp.exp2(s * SCALE - tops[g]).astype(BF16)
        yield

    def mixes(g):
        mixed = dot(vp_scr[...], p_scr[g % 2])
        yield
        state = dot(psi_scr[g % 3], wide_scr[...])
        yield
        late = state + dot(psi_own_ref[g * CHUNK : (g + 1) * CHUNK, :], value_early)
        sums[g] = (mixed, state.astype(BF16), late.astype(BF16))
        yield

    def outputs(g):
        mixed, state, late = sums[g]
        heads = [2 * g, 2 * g + 1]
        parts = [slice(0, BLOCK), slice(BLOCK, CHUNK)]
        states = [jnp.concatenate([state[p], late[p]], axis=0) for p in parts]
        far = [dot(both_ref[h * BLOCK : (h + 1) * BLOCK, :], states[k]) for k, h in enumerate(heads)]
        yield
        total = jnp.concatenate(far, axis=0) + near_ref[g * CHUNK : (g + 1) * CHUNK, :]
        share = 1.0 / mixed[HEAD_DIM : HEAD_DIM + 1]
        teacher = mixed[:HEAD_DIM] * share
        teacher = jnp.concatenate([teacher[:, p].T for p in parts], axis=0).astype(BF16)
        yield
        moved = [dot(dest, teacher[p]) for p in parts]
        inverse = 1.0 / total[:, HEAD_DIM:]
        student = total[:, :HEAD_DIM] * inverse
        gap = student - teacher.astype(F32)
        for k in range(2):
            diff_ref[:, heads[k] * BLOCK : (heads[k] + 1) * BLOCK] = gap[parts[k]]
        yield
        grad_out = gap * (inverse * (2.0 * loss_scale))
        grad_both = jnp.concatenate([grad_out, -grad_out * student], axis=1).astype(BF16)
        yield
        dphi = [dot(states[k], grad_both[parts[k]], NT) for k in range(2)]
        yield
        for k in range(2):
            for shard in range(8):
                buf_ref[shard, :, heads[k] * BLOCK : (heads[k] + 1) * BLOCK] = moved[k][
                    shard * 16 : (shard + 1) * 16
                ].astype(BF16)
        yield
        du = []
        for k in range(2):
            phi = phi_ref[heads[k] * BLOCK : (heads[k] + 1) * BLOCK, :]
            terms = phi * jnp.where(first_half, dphi[k][:BLOCK], dphi[k][BLOCK:])
            up, down = phi[:FEATURES], phi[FEATURES:]
            du.append(
                terms[:FEATURES]
                - terms[FEATURES:]
                - up * jnp.sum(terms[:FEATURES], axis=0, keepdims=True)
                + down * jnp.sum(terms[FEATURES:], axis=0, keepdims=True)
            )
        yield
        for k in range(2):
            h = heads[k]
            grad = dot(du[k].astype(BF16), q_ref[:, h * BLOCK : (h + 1) * BLOCK]).astype(BF16)
            for i in range(4):
                at = (HEADS + i) * BLOCK
                buf_ref[h, :, at : at + BLOCK] = grad[i * 16 : (i + 1) * 16]
        yield

    for step in range(groups + 3):
        running = []
        for stage, length, late_by in (
            (scores, 9, 0),
            (features, 8, 1),
            (weights, 9, 1),
            (mixes, 3, 2),
            (outputs, 8, 3),
        ):
            if 0 <= step - late_by < groups:
                running.append((stage(step - late_by), length))
        marks = sorted(
            ((n + 0.5) / length, at) for at, (_, length) in enumerate(running) for n in range(length)
        )
        for _, at in marks:
            next(running[at][0], None)
        for stage, _ in running:
            for _ in stage:
                pass


def main_call(loss_scale, q, k, v, a, b, km, local):
    vmem = pl.BlockSpec(memory_space=pltpu.VMEM)
    return pl.pallas_call(
        functools.partial(main_kernel, loss_scale),
        out_shape=(
            jax.ShapeDtypeStruct((BLOCK, HEADS * HEAD_DIM), F32),
            jax.ShapeDtypeStruct((8, 16, 1536), BF16),
        ),
        in_specs=[vmem] * 13,
        out_specs=(vmem, vmem),
        scratch_shapes=[
            pltpu.VMEM((2, FAR, CHUNK), F32),
            pltpu.VMEM((2, FAR + BLOCK, CHUNK), BF16),
            pltpu.VMEM((3, CHUNK, FAR), BF16),
            pltpu.VMEM((FAR, BLOCK), BF16),
            pltpu.VMEM((TALL, FAR + BLOCK), BF16),
            pltpu.VMEM((FAR, CHUNK), BF16),
        ],
        compiler_params=pltpu.CompilerParams(vmem_limit_bytes=32 * 1024 * 1024),
        cost_estimate=pl.CostEstimate(
            flops=3_000_000_000, bytes_accessed=3_000_000, transcendentals=4_000_000
        ),
        name="transfer",
    )(q, k, v, a, b, km, *local)


def finish_kernel(part_ref, far_ref, out_ref):
    c = lax.axis_index("c")

    def put(first_ref, second_ref):
        for y in range(4):
            out_ref[2 * y] = first_ref[y].astype(F32)
            out_ref[2 * y + 1] = second_ref[y].astype(F32)

    @pl.when(c == 0)
    def _():
        put(part_ref, far_ref)

    @pl.when(c == 1)
    def _():
        put(far_ref, part_ref)


def finish_call(part, far):
    vmem = pl.BlockSpec(memory_space=pltpu.VMEM)
    return pl.pallas_call(
        finish_kernel,
        out_shape=jax.ShapeDtypeStruct((HEADS, FEATURES, HEAD_DIM), F32),
        in_specs=[vmem] * 2,
        out_specs=vmem,
        compiler_params=pltpu.CompilerParams(vmem_limit_bytes=8 * 1024 * 1024),
        name="finish",
    )(part, far)


def on_device(queries, keys, values, query_map, key_map, documents, assignment):
    query_rows = jnp.swapaxes(query_map, 1, 2).reshape(HEADS * FEATURES, HEAD_DIM)
    key_rows = jnp.swapaxes(key_map, 1, 2).reshape(HEADS * FEATURES, HEAD_DIM)
    shift1 = [(i, (i + 1) % 8) for i in range(8)]
    shift2 = [(i, (i + 2) % 8) for i in range(8)]
    plane0 = pack_call(keys[0], values[0])
    plane2 = lax.ppermute(plane0, "z", shift2)
    plane1 = lax.ppermute(plane0, "z", shift1)
    placed = place_call(keys[0], key_rows, assignment[0], documents)
    plane1, plane2, placed = lax.optimization_barrier((plane1, plane2, placed))
    slots = slot_call(plane0, plane1, plane2)
    mine = lax.all_to_all(slots, "y", 0, 0, tiled=True)
    other = lax.ppermute(mine, "c", [(0, 1), (1, 0)])
    query, _ = lax.optimization_barrier((queries[0], mine))
    local = local_call(query, keys[0], values[0], query_rows) + tuple(placed)
    loss_scale = HEAD_DIM / math.sqrt(4 * 64 * BLOCK)
    difference, outgoing = main_call(
        loss_scale, query, keys[0], values[0], mine, other, key_rows, local
    )
    got = lax.all_to_all(outgoing, ("y", "c"), 0, 0, tiled=True)
    relay = got[:, :, :1024].reshape(8, 8, 2, 1024).transpose(1, 0, 2, 3).reshape(8, 16, 1024)
    part = jnp.sum(got[:, :, 1024:].astype(F32), axis=0).astype(BF16)
    part = jnp.broadcast_to(part[None], (8, 16, 512))
    got = lax.all_to_all(jnp.concatenate([relay, part], axis=2), "z", 0, 0, tiled=True)
    relay = got
    part = jnp.sum(got[:, :, 1024:].astype(F32), axis=0).astype(BF16)
    part = part.reshape(16, 4, HEAD_DIM).transpose(1, 0, 2).reshape(FEATURES, HEAD_DIM)
    part = jnp.broadcast_to(part[None], (16, FEATURES, HEAD_DIM))
    got = lax.all_to_all(part, ("x", "y"), 0, 0, tiled=True)
    part = jnp.sum(got.reshape(4, 4, FEATURES, HEAD_DIM).astype(F32), axis=0).astype(BF16)
    relay, part = lax.optimization_barrier((relay, part))
    far = lax.ppermute(part, "c", [(0, 1), (1, 0)])
    relaid = relay[:, :, :1024].reshape(1, BLOCK, 1024)
    grad = finish_call(part, far)
    return relaid, difference[None], jnp.swapaxes(grad, 1, 2)


def solution(mesh):
    split = Mesh(np.array(mesh.devices).reshape(4, 8, 4, 2), ("x", "z", "y", "c"))
    ctx = ("z", "y", "c")
    return jax.shard_map(
        on_device,
        mesh=split,
        in_specs=(
            P("x", ctx, None),
            P("x", ctx, None),
            P("x", ctx, None),
            P(),
            P(),
            P("x", None),
            P("x", None, None),
        ),
        out_specs=(P("x", ctx, None), P("x", ctx, None), P()),
        check_vma=False,
    )
```

```python
import functools
import math

import jax
import jax.numpy as jnp
import numpy as np
from jax import lax
from jax.experimental import pallas as pl
from jax.experimental.pallas import tpu as pltpu
from jax.sharding import Mesh, PartitionSpec as P

HEAD_DIM = 128
WINDOW = 64
BLOCK = 128
HEADS = 8
FEATURES = 64
ROWS = HEADS * BLOCK
CHUNK = 2 * BLOCK
CHUNKS = 8
FAR = CHUNK * CHUNKS
SCALE = math.log2(math.e) / math.sqrt(HEAD_DIM)
NEGATIVE = -1e30
NT = (((1,), (1,)), ((), ()))
NN = (((1,), (0,)), ((), ()))
TN = (((0,), (0,)), ((), ()))
TALL = HEAD_DIM + 16
F32 = jnp.float32
BF16 = jnp.bfloat16
LOG2E = math.log2(math.e)


def dot(a, b, dims=NN):
    return lax.dot_general(a, b, dims, preferred_element_type=F32)


def two_softmax(u):
    u = u * LOG2E
    top = jnp.max(u, axis=1, keepdims=True)
    low = jnp.min(u, axis=1, keepdims=True)
    up = jnp.exp2(u - top)
    down = jnp.exp2(low - u)
    up = up * (1.0 / jnp.sum(up, axis=1, keepdims=True))
    down = down * (1.0 / jnp.sum(down, axis=1, keepdims=True))
    return jnp.concatenate([up, down], axis=1)


def in_hbm(x):
    return pltpu.with_memory_space_constraint(x, pltpu.HBM)


def iota(shape, axis):
    return lax.broadcasted_iota(jnp.int32, shape, axis)


def pack_kernel(k_hbm, v_hbm, out_ref, sems):
    copies = [
        pltpu.make_async_copy(k_hbm, out_ref.at[0], sems.at[0]),
        pltpu.make_async_copy(v_hbm, out_ref.at[1], sems.at[1]),
    ]
    for copy in copies:
        copy.start()
    for copy in copies:
        copy.wait()


def pack_call(k, v):
    return pl.pallas_call(
        pack_kernel,
        out_shape=jax.ShapeDtypeStruct((2, BLOCK, HEAD_DIM), BF16),
        in_specs=[pl.BlockSpec(memory_space=pltpu.HBM)] * 2,
        out_specs=pl.BlockSpec(memory_space=pltpu.VMEM),
        scratch_shapes=[pltpu.SemaphoreType.DMA((2,))],
        compiler_params=pltpu.CompilerParams(vmem_limit_bytes=8 * 1024 * 1024),
        name="pack_block",
    )(in_hbm(k), in_hbm(v))


def local_kernel(
    q_hbm,
    qm_hbm,
    km_hbm,
    route_hbm,
    doc_hbm,
    k_hbm,
    v_hbm,
    own_ref,
    near_ref,
    phi_ref,
    both_ref,
    psi_ref,
    dest_ref,
    ok_ref,
    q_ref,
    k_ref,
    v_ref,
    km_ref,
    qm_ref,
    route_ref,
    doc_ref,
    sems,
):
    pairs = (
        (route_hbm, route_ref),
        (doc_hbm, doc_ref),
        (k_hbm, k_ref),
        (v_hbm, v_ref),
        (km_hbm, km_ref),
        (qm_hbm, qm_ref),
        (q_hbm, q_ref),
    )
    copies = [pltpu.make_async_copy(a, b, sems.at[n]) for n, (a, b) in enumerate(pairs)]
    for copy in copies:
        copy.start()
    copies[0].wait()
    copies[1].wait()
    col = lax.broadcasted_iota(jnp.int32, (BLOCK, BLOCK), 1)
    row = lax.broadcasted_iota(jnp.int32, (BLOCK, BLOCK), 0)
    causal = row <= col
    near = causal & ((col < WINDOW) == (row < WINDOW))
    first_half = col < WINDOW
    z, y, c = lax.axis_index("z"), lax.axis_index("y"), lax.axis_index("c")
    here = (z * 4 + y) * 2 + c
    place = iota((2 * CHUNKS, 64), 0)
    block = iota((2 * CHUNKS, 64), 1)
    from_y = lax.shift_right_logical(place, 1) & 3
    from_c = jnp.where(place < CHUNKS, c, 1 - c)
    first = jnp.where(from_y < y, 0, jnp.where(from_y > y, 1, 2 * from_c))
    second = jnp.where(from_y > y, 2, 1)
    source = (z - jnp.where((place & 1) == 0, first, second)) * 8 + from_y * 2 + from_c
    documents = doc_ref[...]
    own_document = jnp.sum(jnp.where(iota((1, 64), 1) == here, documents, 0), axis=1, keepdims=True)
    same = (documents == own_document) & (iota((1, 64), 1) < here) & (iota((1, 64), 1) > here - 16)
    found = jnp.where((source == block) & same, 1.0, 0.0)
    ok_ref[...] = jnp.broadcast_to(jnp.max(found, axis=1, keepdims=True), ok_ref.shape)
    shard = route_ref[pl.ds(here, 1), :]
    order = (shard & 7) * 8 + lax.shift_right_logical(shard, 3)
    pieces = (iota((64, 64), 0) == order).astype(BF16)
    rows = (lax.shift_right_logical(iota((BLOCK, 64), 0), 1) == iota((BLOCK, 64), 1)).astype(BF16)
    tokens = (iota((64, BLOCK), 0) == lax.shift_right_logical(iota((64, BLOCK), 1), 1)).astype(BF16)
    placed = dot(dot(rows, pieces).astype(BF16), tokens)
    dest_ref[...] = jnp.where((row & 1) == (col & 1), placed, 0.0).astype(BF16)
    for copy in copies[2:5]:
        copy.wait()
    keys = k_ref[...]
    values = jnp.concatenate([v_ref[...], jnp.ones((BLOCK, BLOCK), BF16)], axis=1)
    psi = two_softmax(dot(km_ref[...], keys, NT).reshape(HEADS, FEATURES, BLOCK))
    psi_ref[...] = psi.reshape(ROWS, BLOCK).astype(BF16)
    copies[5].wait()
    copies[6].wait()
    for h in range(HEADS):
        at = h * BLOCK
        query = q_ref[:, at : at + BLOCK]
        scores = dot(keys, query, NT)
        own_ref[:, at : at + BLOCK] = jnp.where(causal, scores, NEGATIVE)
        window = jnp.where(near, scores * SCALE, NEGATIVE)
        weights = jnp.exp2(window - jnp.max(window, axis=0, keepdims=True))
        near_ref[at : at + BLOCK, :] = dot(weights.T.astype(BF16), values)
        u = dot(qm_ref[h * FEATURES : (h + 1) * FEATURES, :], query, NT)
        phi = two_softmax(u[None])[0]
        phi_ref[at : at + BLOCK, :] = phi
        both = jnp.concatenate(
            [jnp.where(first_half, phi, 0.0), jnp.where(first_half, 0.0, phi)], axis=0
        )
        both_ref[at : at + BLOCK, :] = both.T.astype(BF16)


def local_call(q, k, v, qm, km, routes, documents):
    vmem = pl.BlockSpec(memory_space=pltpu.VMEM)
    return pl.pallas_call(
        local_kernel,
        out_shape=(
            jax.ShapeDtypeStruct((BLOCK, ROWS), F32),
            jax.ShapeDtypeStruct((ROWS, CHUNK), F32),
            jax.ShapeDtypeStruct((ROWS, BLOCK), F32),
            jax.ShapeDtypeStruct((ROWS, CHUNK), BF16),
            jax.ShapeDtypeStruct((ROWS, BLOCK), BF16),
            jax.ShapeDtypeStruct((BLOCK, BLOCK), BF16),
            jax.ShapeDtypeStruct((2 * CHUNKS, BLOCK), F32),
            jax.ShapeDtypeStruct((BLOCK, ROWS), BF16),
            jax.ShapeDtypeStruct((BLOCK, HEAD_DIM), BF16),
            jax.ShapeDtypeStruct((BLOCK, HEAD_DIM), BF16),
            jax.ShapeDtypeStruct((HEADS * FEATURES, HEAD_DIM), BF16),
        ),
        in_specs=[pl.BlockSpec(memory_space=pltpu.HBM)] * 7,
        out_specs=(vmem,) * 11,
        scratch_shapes=[
            pltpu.VMEM((HEADS * FEATURES, HEAD_DIM), BF16),
            pltpu.VMEM((64, 64), jnp.int32),
            pltpu.VMEM((1, 64), jnp.int32),
            pltpu.SemaphoreType.DMA((7,)),
        ],
        compiler_params=pltpu.CompilerParams(vmem_limit_bytes=16 * 1024 * 1024),
        cost_estimate=pl.CostEstimate(
            flops=400_000_000, bytes_accessed=4_000_000, transcendentals=500_000
        ),
        name="local_block",
    )(*[in_hbm(each) for each in (q, qm, km, routes, documents, k, v)])


def half_kernel(q_ref, k_ref, a_ref, km_ref, ok_ref, s_ref, psi_ref, top_ref, key_scr):
    fill_keys(key_scr, a_ref, k_ref, ok_ref, 0)
    for g in range(HEADS // 2):
        query = two_heads(q_ref, g)
        top = None
        for i in range(CHUNKS // 2):
            keys = key_scr[i * CHUNK : (i + 1) * CHUNK, :]
            s = dot(keys, query, NT)
            s_ref[i * CHUNK : (i + 1) * CHUNK, g * CHUNK : (g + 1) * CHUNK] = s
            now = jnp.max(s.reshape(CHUNK // 8, 8, CHUNK), axis=0)
            top = now if top is None else jnp.maximum(top, now)
            u = dot(km_ref[g * BLOCK : (g + 1) * BLOCK, :], keys, NT)
            psi = two_softmax(u.reshape(2, FEATURES, CHUNK)).reshape(CHUNK, CHUNK)
            psi_ref[g * CHUNK : (g + 1) * CHUNK, i * CHUNK : (i + 1) * CHUNK] = psi.astype(BF16)
        top_ref[:, g * CHUNK : (g + 1) * CHUNK] = top


def two_heads(q_ref, g):
    return jnp.concatenate(
        [q_ref[:, (2 * g + k) * BLOCK : (2 * g + k + 1) * BLOCK] for k in range(2)], axis=0
    )


def fill_keys(key_scr, src, k_ref, ok_ref, first):
    first_key = k_ref[0:1, :]
    for i in range(CHUNKS // 2):
        for k in range(2):
            at = i * CHUNK + k * BLOCK
            one = ok_ref[2 * (first + i) + k : 2 * (first + i) + k + 1, :]
            other = (1.0 - one).astype(BF16)
            key_scr[at : at + BLOCK, :] = src[i, k, 0] * one.astype(BF16) + first_key * other


def half_call(q, k, a, km, ok):
    vmem = pl.BlockSpec(memory_space=pltpu.VMEM)
    return pl.pallas_call(
        half_kernel,
        out_shape=(
            jax.ShapeDtypeStruct((FAR // 2, ROWS), F32),
            jax.ShapeDtypeStruct((ROWS, FAR // 2), BF16),
            jax.ShapeDtypeStruct((8, ROWS), F32),
        ),
        in_specs=[vmem] * 5,
        out_specs=(vmem,) * 3,
        scratch_shapes=[pltpu.VMEM((FAR // 2, BLOCK), BF16)],
        compiler_params=pltpu.CompilerParams(vmem_limit_bytes=16 * 1024 * 1024),
        cost_estimate=pl.CostEstimate(
            flops=400_000_000, bytes_accessed=4_000_000, transcendentals=1_000_000
        ),
        name="first_half",
    )(q, k, a, km, ok)


def slot_kernel(now_ref, back1_ref, back2_ref, out_ref):
    y, c = lax.axis_index("y"), lax.axis_index("c")
    planes = (now_ref, back1_ref, back2_ref)

    def put(d, k, plane):
        out_ref[d, k] = planes[plane][...]

    for d in range(4):

        @pl.when(d > y)
        def _():
            put(d, 0, 0)
            put(d, 1, 1)

        @pl.when(d < y)
        def _():
            put(d, 0, 1)
            put(d, 1, 2)

        @pl.when((d == y) & (c == 0))
        def _():
            put(d, 0, 0)
            put(d, 1, 1)

        @pl.when((d == y) & (c == 1))
        def _():
            put(d, 0, 2)
            put(d, 1, 1)


def slot_call(*blocks):
    vmem = pl.BlockSpec(memory_space=pltpu.VMEM)
    return pl.pallas_call(
        slot_kernel,
        out_shape=jax.ShapeDtypeStruct((4, 2, 2, BLOCK, HEAD_DIM), BF16),
        in_specs=[vmem] * 3,
        out_specs=vmem,
        compiler_params=pltpu.CompilerParams(vmem_limit_bytes=8 * 1024 * 1024),
        name="fill_slots",
    )(*blocks)


def main_kernel(
    loss_scale,
    q_ref,
    k_ref,
    v_ref,
    a_ref,
    b_ref,
    km_ref,
    s_half,
    psi_half,
    top_half,
    own_ref,
    near_ref,
    phi_ref,
    both_ref,
    psi_own_ref,
    dest_ref,
    ok_ref,
    diff_ref,
    buf_ref,
    s_scr,
    p_scr,
    psi_scr,
    key_scr,
    vp_scr,
    wide_scr,
):
    all_ones = jnp.ones((BLOCK, BLOCK), BF16)
    ones = jnp.ones((TALL - HEAD_DIM, BLOCK), BF16)
    fill_keys(key_scr, b_ref, k_ref, ok_ref, CHUNKS // 2)
    for i in range(CHUNKS):
        src = a_ref if i < 4 else b_ref
        for k in range(2):
            at = i * CHUNK + k * BLOCK
            one = ok_ref[2 * i + k : 2 * i + k + 1, :].astype(BF16)
            value = src[i % 4, k, 1] * one
            vp_scr[:HEAD_DIM, at : at + BLOCK] = value.T
            vp_scr[HEAD_DIM:, at : at + BLOCK] = ones * one
            wide_scr[at : at + BLOCK, :BLOCK] = value
            wide_scr[at : at + BLOCK, BLOCK:] = all_ones * one
    vp_scr[:HEAD_DIM, FAR:] = v_ref[...].T
    vp_scr[HEAD_DIM:, FAR:] = ones
    early = lax.broadcasted_iota(jnp.int32, (BLOCK, CHUNK), 0) < WINDOW
    value_early = jnp.concatenate([v_ref[...], all_ones], axis=1)
    value_early = jnp.where(early, value_early.astype(F32), 0.0).astype(BF16)
    first_half = lax.broadcasted_iota(jnp.int32, (BLOCK, BLOCK), 1) < WINDOW
    dest = dest_ref[...]

    groups = HEADS // 2
    half = CHUNKS // 2
    tops, sums = [None] * groups, [None] * groups

    def scores(g):
        query = two_heads(q_ref, g)
        top = jnp.max(
            own_ref[:, g * CHUNK : (g + 1) * CHUNK].reshape(BLOCK // 8, 8, CHUNK), axis=0
        )
        top = jnp.maximum(top, top_half[:, g * CHUNK : (g + 1) * CHUNK])
        for i in range(half):
            s = dot(key_scr[i * CHUNK : (i + 1) * CHUNK, :], query, NT)
            s_scr[g % 2, i * CHUNK : (i + 1) * CHUNK, :] = s
            top = jnp.maximum(top, jnp.max(s.reshape(CHUNK // 8, 8, CHUNK), axis=0))
            yield
        tops[g] = jnp.max(top, axis=0, keepdims=True) * SCALE

    def features(g):
        for i in range(half):
            keys = key_scr[i * CHUNK : (i + 1) * CHUNK, :]
            u = dot(km_ref[g * BLOCK : (g + 1) * BLOCK, :], keys, NT)
            psi = two_softmax(u.reshape(2, FEATURES, CHUNK)).reshape(CHUNK, CHUNK)
            psi_scr[g % 3, :, i * CHUNK : (i + 1) * CHUNK] = psi.astype(BF16)
            yield

    def weights(g):
        for i in range(CHUNKS):
            if i < half:
                s = s_half[i * CHUNK : (i + 1) * CHUNK, g * CHUNK : (g + 1) * CHUNK]
            else:
                s = s_scr[g % 2, (i - half) * CHUNK : (i - half + 1) * CHUNK, :]
            w = jnp.exp2(s * SCALE - tops[g])
            p_scr[g % 2, i * CHUNK : (i + 1) * CHUNK, :] = w.astype(BF16)
            yield
        s = own_ref[:, g * CHUNK : (g + 1) * CHUNK]
        p_scr[g % 2, FAR:, :] = jnp.exp2(s * SCALE - tops[g]).astype(BF16)
        yield

    def mixes(g):
        mixed = dot(vp_scr[...], p_scr[g % 2])
        yield
        state = dot(psi_half[g * CHUNK : (g + 1) * CHUNK, :], wide_scr[: FAR // 2, :])
        state = state + dot(psi_scr[g % 3], wide_scr[FAR // 2 :, :])
        yield
        late = state + dot(psi_own_ref[g * CHUNK : (g + 1) * CHUNK, :], value_early)
        sums[g] = (mixed, state.astype(BF16), late.astype(BF16))
        yield

    def outputs(g):
        mixed, state, late = sums[g]
        heads = [2 * g, 2 * g + 1]
        parts = [slice(0, BLOCK), slice(BLOCK, CHUNK)]
        states = [jnp.concatenate([state[p], late[p]], axis=0) for p in parts]
        far = [dot(both_ref[h * BLOCK : (h + 1) * BLOCK, :], states[k]) for k, h in enumerate(heads)]
        yield
        total = jnp.concatenate(far, axis=0) + near_ref[g * CHUNK : (g + 1) * CHUNK, :]
        share = 1.0 / mixed[HEAD_DIM : HEAD_DIM + 1]
        teacher = mixed[:HEAD_DIM] * share
        teacher = jnp.concatenate([teacher[:, p].T for p in parts], axis=0).astype(BF16)
        yield
        moved = [dot(dest, teacher[p]) for p in parts]
        inverse = 1.0 / total[:, HEAD_DIM:]
        student = total[:, :HEAD_DIM] * inverse
        gap = student - teacher.astype(F32)
        for k in range(2):
            diff_ref[:, heads[k] * BLOCK : (heads[k] + 1) * BLOCK] = gap[parts[k]]
        yield
        grad_out = gap * (inverse * (2.0 * loss_scale))
        grad_both = jnp.concatenate([grad_out, -grad_out * student], axis=1).astype(BF16)
        yield
        dphi = [dot(states[k], grad_both[parts[k]], NT) for k in range(2)]
        yield
        for k in range(2):
            for shard in range(8):
                buf_ref[shard, :, heads[k] * BLOCK : (heads[k] + 1) * BLOCK] = moved[k][
                    shard * 16 : (shard + 1) * 16
                ].astype(BF16)
        yield
        du = []
        for k in range(2):
            phi = phi_ref[heads[k] * BLOCK : (heads[k] + 1) * BLOCK, :]
            terms = phi * jnp.where(first_half, dphi[k][:BLOCK], dphi[k][BLOCK:])
            up, down = phi[:FEATURES], phi[FEATURES:]
            du.append(
                terms[:FEATURES]
                - terms[FEATURES:]
                - up * jnp.sum(terms[:FEATURES], axis=0, keepdims=True)
                + down * jnp.sum(terms[FEATURES:], axis=0, keepdims=True)
            )
        yield
        for k in range(2):
            h = heads[k]
            grad = dot(du[k].astype(BF16), q_ref[:, h * BLOCK : (h + 1) * BLOCK]).astype(BF16)
            for i in range(4):
                at = (HEADS + i) * BLOCK
                buf_ref[h, :, at : at + BLOCK] = grad[i * 16 : (i + 1) * 16]
        yield

    for step in range(groups + 3):
        running = []
        for stage, length, late_by in (
            (scores, 5, 0),
            (features, 4, 1),
            (weights, 9, 1),
            (mixes, 3, 2),
            (outputs, 8, 3),
        ):
            if 0 <= step - late_by < groups:
                running.append((stage(step - late_by), length))
        marks = sorted(
            ((n + 0.5) / length, at) for at, (_, length) in enumerate(running) for n in range(length)
        )
        for _, at in marks:
            next(running[at][0], None)
        for stage, _ in running:
            for _ in stage:
                pass


def main_call(loss_scale, q, k, v, a, b, km, half, local):
    vmem = pl.BlockSpec(memory_space=pltpu.VMEM)
    return pl.pallas_call(
        functools.partial(main_kernel, loss_scale),
        out_shape=(
            jax.ShapeDtypeStruct((BLOCK, HEADS * HEAD_DIM), F32),
            jax.ShapeDtypeStruct((8, 16, 1536), BF16),
        ),
        in_specs=[vmem] * 16,
        out_specs=(vmem, vmem),
        scratch_shapes=[
            pltpu.VMEM((2, FAR // 2, CHUNK), F32),
            pltpu.VMEM((2, FAR + BLOCK, CHUNK), BF16),
            pltpu.VMEM((3, CHUNK, FAR // 2), BF16),
            pltpu.VMEM((FAR // 2, BLOCK), BF16),
            pltpu.VMEM((TALL, FAR + BLOCK), BF16),
            pltpu.VMEM((FAR, CHUNK), BF16),
        ],
        compiler_params=pltpu.CompilerParams(vmem_limit_bytes=24 * 1024 * 1024),
        cost_estimate=pl.CostEstimate(
            flops=3_000_000_000, bytes_accessed=3_000_000, transcendentals=4_000_000
        ),
        name="transfer",
    )(q, k, v, a, b, km, *half, *local)


def finish_kernel(part_ref, far_ref, out_ref):
    c = lax.axis_index("c")

    def put(first_ref, second_ref):
        for y in range(4):
            out_ref[2 * y] = first_ref[y].astype(F32)
            out_ref[2 * y + 1] = second_ref[y].astype(F32)

    @pl.when(c == 0)
    def _():
        put(part_ref, far_ref)

    @pl.when(c == 1)
    def _():
        put(far_ref, part_ref)


def finish_call(part, far):
    vmem = pl.BlockSpec(memory_space=pltpu.VMEM)
    return pl.pallas_call(
        finish_kernel,
        out_shape=jax.ShapeDtypeStruct((HEADS, FEATURES, HEAD_DIM), F32),
        in_specs=[vmem] * 2,
        out_specs=vmem,
        compiler_params=pltpu.CompilerParams(vmem_limit_bytes=8 * 1024 * 1024),
        name="finish",
    )(part, far)


def on_device(queries, keys, values, query_map, key_map, documents, assignment):
    query_rows = jnp.swapaxes(query_map, 1, 2).reshape(HEADS * FEATURES, HEAD_DIM)
    key_rows = jnp.swapaxes(key_map, 1, 2).reshape(HEADS * FEATURES, HEAD_DIM)
    shift1 = [(i, (i + 1) % 8) for i in range(8)]
    shift2 = [(i, (i + 2) % 8) for i in range(8)]
    plane0 = pack_call(keys[0], values[0])
    plane2 = lax.ppermute(plane0, "z", shift2)
    plane1 = lax.ppermute(plane0, "z", shift1)
    local = local_call(
        queries[0], keys[0], values[0], query_rows, key_rows, assignment[0], documents
    )
    plane1, plane2, local = lax.optimization_barrier((plane1, plane2, local))
    slots = slot_call(plane0, plane1, plane2)
    mine = lax.all_to_all(slots, "y", 0, 0, tiled=True)
    other = lax.ppermute(mine, "c", [(0, 1), (1, 0)])
    local, (q, k, v, km) = local[:7], local[7:]
    half = half_call(q, k, mine, km, local[-1])
    loss_scale = HEAD_DIM / math.sqrt(4 * 64 * BLOCK)
    difference, outgoing = main_call(
        loss_scale, q, k, v, mine, other, km, half, local
    )
    got = lax.all_to_all(outgoing, ("y", "c"), 0, 0, tiled=True)
    relay = got[:, :, :1024].reshape(8, 8, 2, 1024).transpose(1, 0, 2, 3).reshape(8, 16, 1024)
    part = jnp.sum(got[:, :, 1024:].astype(F32), axis=0).astype(BF16)
    part = jnp.broadcast_to(part[None], (8, 16, 512))
    got = lax.all_to_all(jnp.concatenate([relay, part], axis=2), "z", 0, 0, tiled=True)
    relay = got
    part = jnp.sum(got[:, :, 1024:].astype(F32), axis=0).astype(BF16)
    part = part.reshape(16, 4, HEAD_DIM).transpose(1, 0, 2).reshape(FEATURES, HEAD_DIM)
    part = jnp.broadcast_to(part[None], (16, FEATURES, HEAD_DIM))
    got = lax.all_to_all(part, ("x", "y"), 0, 0, tiled=True)
    part = jnp.sum(got.reshape(4, 4, FEATURES, HEAD_DIM).astype(F32), axis=0).astype(BF16)
    relay, part = lax.optimization_barrier((relay, part))
    far = lax.ppermute(part, "c", [(0, 1), (1, 0)])
    relaid = relay[:, :, :1024].reshape(1, BLOCK, 1024)
    grad = finish_call(part, far)
    return relaid, difference[None], jnp.swapaxes(grad, 1, 2)


def solution(mesh):
    split = Mesh(np.array(mesh.devices).reshape(4, 8, 4, 2), ("x", "z", "y", "c"))
    ctx = ("z", "y", "c")
    return jax.shard_map(
        on_device,
        mesh=split,
        in_specs=(
            P("x", ctx, None),
            P("x", ctx, None),
            P("x", ctx, None),
            P(),
            P(),
            P("x", None),
            P("x", None, None),
        ),
        out_specs=(P("x", ctx, None), P("x", ctx, None), P()),
        check_vma=False,
    )
```

```python
import functools
import math

import jax
import jax.numpy as jnp
import numpy as np
from jax import lax
from jax.experimental import pallas as pl
from jax.experimental.pallas import tpu as pltpu
from jax.sharding import Mesh, PartitionSpec as P

HEAD_DIM = 128
WINDOW = 64
BLOCK = 128
HEADS = 8
FEATURES = 64
ROWS = HEADS * BLOCK
CHUNK = 2 * BLOCK
CHUNKS = 8
FAR = CHUNK * CHUNKS
SCALE = math.log2(math.e) / math.sqrt(HEAD_DIM)
NEGATIVE = -1e30
NT = (((1,), (1,)), ((), ()))
NN = (((1,), (0,)), ((), ()))
TN = (((0,), (0,)), ((), ()))
TALL = HEAD_DIM + 16
F32 = jnp.float32
BF16 = jnp.bfloat16
LOG2E = math.log2(math.e)


def dot(a, b, dims=NN):
    return lax.dot_general(a, b, dims, preferred_element_type=F32)


def two_softmax(u):
    u = u * LOG2E
    top = jnp.max(u, axis=1, keepdims=True)
    low = jnp.min(u, axis=1, keepdims=True)
    up = jnp.exp2(u - top)
    down = jnp.exp2(low - u)
    up = up * (1.0 / jnp.sum(up, axis=1, keepdims=True))
    down = down * (1.0 / jnp.sum(down, axis=1, keepdims=True))
    return jnp.concatenate([up, down], axis=1)


def in_hbm(x):
    return pltpu.with_memory_space_constraint(x, pltpu.HBM)


def iota(shape, axis):
    return lax.broadcasted_iota(jnp.int32, shape, axis)


def pack_kernel(k_hbm, v_hbm, out_ref, sems):
    copies = [
        pltpu.make_async_copy(k_hbm, out_ref.at[0], sems.at[0]),
        pltpu.make_async_copy(v_hbm, out_ref.at[1], sems.at[1]),
    ]
    for copy in copies:
        copy.start()
    for copy in copies:
        copy.wait()


def pack_call(k, v):
    return pl.pallas_call(
        pack_kernel,
        out_shape=jax.ShapeDtypeStruct((2, BLOCK, HEAD_DIM), BF16),
        in_specs=[pl.BlockSpec(memory_space=pltpu.HBM)] * 2,
        out_specs=pl.BlockSpec(memory_space=pltpu.VMEM),
        scratch_shapes=[pltpu.SemaphoreType.DMA((2,))],
        compiler_params=pltpu.CompilerParams(vmem_limit_bytes=8 * 1024 * 1024),
        name="pack_block",
    )(in_hbm(k), in_hbm(v))


def local_kernel(
    q_hbm,
    qm_hbm,
    km_hbm,
    route_hbm,
    doc_hbm,
    k_hbm,
    v_hbm,
    own_ref,
    near_ref,
    phi_ref,
    both_ref,
    early_ref,
    dest_ref,
    ok_ref,
    q_ref,
    k_ref,
    v_ref,
    km_ref,
    qm_ref,
    route_ref,
    doc_ref,
    sems,
):
    pairs = (
        (route_hbm, route_ref),
        (doc_hbm, doc_ref),
        (k_hbm, k_ref),
        (v_hbm, v_ref),
        (km_hbm, km_ref),
        (qm_hbm, qm_ref),
        (q_hbm, q_ref),
    )
    copies = [pltpu.make_async_copy(a, b, sems.at[n]) for n, (a, b) in enumerate(pairs)]
    for copy in copies:
        copy.start()
    copies[0].wait()
    copies[1].wait()
    col = lax.broadcasted_iota(jnp.int32, (BLOCK, BLOCK), 1)
    row = lax.broadcasted_iota(jnp.int32, (BLOCK, BLOCK), 0)
    causal = row <= col
    near = causal & ((col < WINDOW) == (row < WINDOW))
    first_half = col < WINDOW
    z, y, c = lax.axis_index("z"), lax.axis_index("y"), lax.axis_index("c")
    here = (z * 4 + y) * 2 + c
    place = iota((2 * CHUNKS, 64), 0)
    block = iota((2 * CHUNKS, 64), 1)
    from_y = lax.shift_right_logical(place, 1) & 3
    from_c = jnp.where(place < CHUNKS, c, 1 - c)
    first = jnp.where(from_y < y, 0, jnp.where(from_y > y, 1, 2 * from_c))
    second = jnp.where(from_y > y, 2, 1)
    source = (z - jnp.where((place & 1) == 0, first, second)) * 8 + from_y * 2 + from_c
    documents = doc_ref[...]
    own_document = jnp.sum(jnp.where(iota((1, 64), 1) == here, documents, 0), axis=1, keepdims=True)
    same = (documents == own_document) & (iota((1, 64), 1) < here) & (iota((1, 64), 1) > here - 16)
    found = jnp.where((source == block) & same, 1.0, 0.0)
    ok_ref[...] = jnp.broadcast_to(jnp.max(found, axis=1, keepdims=True), ok_ref.shape)
    shard = route_ref[pl.ds(here, 1), :]
    order = (shard & 7) * 8 + lax.shift_right_logical(shard, 3)
    pieces = (iota((64, 64), 0) == order).astype(BF16)
    rows = (lax.shift_right_logical(iota((BLOCK, 64), 0), 1) == iota((BLOCK, 64), 1)).astype(BF16)
    tokens = (iota((64, BLOCK), 0) == lax.shift_right_logical(iota((64, BLOCK), 1), 1)).astype(BF16)
    placed = dot(dot(rows, pieces).astype(BF16), tokens)
    dest_ref[...] = jnp.where((row & 1) == (col & 1), placed, 0.0).astype(BF16)
    for copy in copies[2:5]:
        copy.wait()
    keys = k_ref[...]
    values = jnp.concatenate([v_ref[...], jnp.ones((BLOCK, BLOCK), BF16)], axis=1)
    psi = two_softmax(dot(km_ref[...], keys, NT).reshape(HEADS, FEATURES, BLOCK))
    early = jnp.where(iota((BLOCK, CHUNK), 0) < WINDOW, values.astype(F32), 0.0).astype(BF16)
    early_ref[...] = dot(psi.reshape(ROWS, BLOCK).astype(BF16), early)
    copies[5].wait()
    copies[6].wait()
    for h in range(HEADS):
        at = h * BLOCK
        query = q_ref[:, at : at + BLOCK]
        scores = dot(keys, query, NT)
        own_ref[:, at : at + BLOCK] = jnp.where(causal, scores, NEGATIVE)
        window = jnp.where(near, scores * SCALE, NEGATIVE)
        weights = jnp.exp2(window - jnp.max(window, axis=0, keepdims=True))
        near_ref[at : at + BLOCK, :] = dot(weights.T.astype(BF16), values)
        u = dot(qm_ref[h * FEATURES : (h + 1) * FEATURES, :], query, NT)
        phi = two_softmax(u[None])[0]
        phi_ref[at : at + BLOCK, :] = phi
        both = jnp.concatenate(
            [jnp.where(first_half, phi, 0.0), jnp.where(first_half, 0.0, phi)], axis=0
        )
        both_ref[at : at + BLOCK, :] = both.T.astype(BF16)


def local_call(q, k, v, qm, km, routes, documents):
    vmem = pl.BlockSpec(memory_space=pltpu.VMEM)
    return pl.pallas_call(
        local_kernel,
        out_shape=(
            jax.ShapeDtypeStruct((BLOCK, ROWS), F32),
            jax.ShapeDtypeStruct((ROWS, CHUNK), F32),
            jax.ShapeDtypeStruct((ROWS, BLOCK), F32),
            jax.ShapeDtypeStruct((ROWS, CHUNK), BF16),
            jax.ShapeDtypeStruct((ROWS, CHUNK), F32),
            jax.ShapeDtypeStruct((BLOCK, BLOCK), BF16),
            jax.ShapeDtypeStruct((2 * CHUNKS, BLOCK), F32),
            jax.ShapeDtypeStruct((BLOCK, ROWS), BF16),
            jax.ShapeDtypeStruct((BLOCK, HEAD_DIM), BF16),
            jax.ShapeDtypeStruct((BLOCK, HEAD_DIM), BF16),
            jax.ShapeDtypeStruct((HEADS * FEATURES, HEAD_DIM), BF16),
        ),
        in_specs=[pl.BlockSpec(memory_space=pltpu.HBM)] * 7,
        out_specs=(vmem,) * 11,
        scratch_shapes=[
            pltpu.VMEM((HEADS * FEATURES, HEAD_DIM), BF16),
            pltpu.VMEM((64, 64), jnp.int32),
            pltpu.VMEM((1, 64), jnp.int32),
            pltpu.SemaphoreType.DMA((7,)),
        ],
        compiler_params=pltpu.CompilerParams(vmem_limit_bytes=16 * 1024 * 1024),
        cost_estimate=pl.CostEstimate(
            flops=400_000_000, bytes_accessed=4_000_000, transcendentals=500_000
        ),
        name="local_block",
    )(*[in_hbm(each) for each in (q, qm, km, routes, documents, k, v)])


def half_kernel(
    q_ref, k_ref, a_ref, km_ref, ok_ref, s_ref, state_ref, top_ref, key_scr, psi_scr, wide_scr
):
    fill_keys(key_scr, a_ref, k_ref, ok_ref, 0)
    for i in range(CHUNKS // 2):
        for k in range(2):
            at = i * CHUNK + k * BLOCK
            one = ok_ref[2 * i + k : 2 * i + k + 1, :].astype(BF16)
            wide_scr[at : at + BLOCK, :BLOCK] = a_ref[i, k, 1] * one
            wide_scr[at : at + BLOCK, BLOCK:] = jnp.ones((BLOCK, BLOCK), BF16) * one
    for g in range(HEADS // 2):
        query = two_heads(q_ref, g)
        top = None
        for i in range(CHUNKS // 2):
            keys = key_scr[i * CHUNK : (i + 1) * CHUNK, :]
            s = dot(keys, query, NT)
            s_ref[i * CHUNK : (i + 1) * CHUNK, g * CHUNK : (g + 1) * CHUNK] = s
            now = jnp.max(s.reshape(CHUNK // 8, 8, CHUNK), axis=0)
            top = now if top is None else jnp.maximum(top, now)
            u = dot(km_ref[g * BLOCK : (g + 1) * BLOCK, :], keys, NT)
            psi = two_softmax(u.reshape(2, FEATURES, CHUNK)).reshape(CHUNK, CHUNK)
            psi_scr[g * CHUNK : (g + 1) * CHUNK, i * CHUNK : (i + 1) * CHUNK] = psi.astype(BF16)
        state_ref[g * CHUNK : (g + 1) * CHUNK, :] = dot(
            psi_scr[g * CHUNK : (g + 1) * CHUNK, :], wide_scr[...]
        )
        top_ref[:, g * CHUNK : (g + 1) * CHUNK] = top


def two_heads(q_ref, g):
    return jnp.concatenate(
        [q_ref[:, (2 * g + k) * BLOCK : (2 * g + k + 1) * BLOCK] for k in range(2)], axis=0
    )


def fill_keys(key_scr, src, k_ref, ok_ref, first):
    first_key = k_ref[0:1, :]
    for i in range(CHUNKS // 2):
        for k in range(2):
            at = i * CHUNK + k * BLOCK
            one = ok_ref[2 * (first + i) + k : 2 * (first + i) + k + 1, :]
            other = (1.0 - one).astype(BF16)
            key_scr[at : at + BLOCK, :] = src[i, k, 0] * one.astype(BF16) + first_key * other


def half_call(q, k, a, km, ok):
    vmem = pl.BlockSpec(memory_space=pltpu.VMEM)
    return pl.pallas_call(
        half_kernel,
        out_shape=(
            jax.ShapeDtypeStruct((FAR // 2, ROWS), F32),
            jax.ShapeDtypeStruct((ROWS, CHUNK), F32),
            jax.ShapeDtypeStruct((8, ROWS), F32),
        ),
        in_specs=[vmem] * 5,
        out_specs=(vmem,) * 3,
        scratch_shapes=[
            pltpu.VMEM((FAR // 2, BLOCK), BF16),
            pltpu.VMEM((ROWS, FAR // 2), BF16),
            pltpu.VMEM((FAR // 2, CHUNK), BF16),
        ],
        compiler_params=pltpu.CompilerParams(vmem_limit_bytes=16 * 1024 * 1024),
        cost_estimate=pl.CostEstimate(
            flops=400_000_000, bytes_accessed=4_000_000, transcendentals=1_000_000
        ),
        name="first_half",
    )(q, k, a, km, ok)


def slot_kernel(now_ref, back1_ref, back2_ref, out_ref):
    y, c = lax.axis_index("y"), lax.axis_index("c")
    planes = (now_ref, back1_ref, back2_ref)

    def put(d, k, plane):
        out_ref[d, k] = planes[plane][...]

    for d in range(4):

        @pl.when(d > y)
        def _():
            put(d, 0, 0)
            put(d, 1, 1)

        @pl.when(d < y)
        def _():
            put(d, 0, 1)
            put(d, 1, 2)

        @pl.when((d == y) & (c == 0))
        def _():
            put(d, 0, 0)
            put(d, 1, 1)

        @pl.when((d == y) & (c == 1))
        def _():
            put(d, 0, 2)
            put(d, 1, 1)


def slot_call(*blocks):
    vmem = pl.BlockSpec(memory_space=pltpu.VMEM)
    return pl.pallas_call(
        slot_kernel,
        out_shape=jax.ShapeDtypeStruct((4, 2, 2, BLOCK, HEAD_DIM), BF16),
        in_specs=[vmem] * 3,
        out_specs=vmem,
        compiler_params=pltpu.CompilerParams(vmem_limit_bytes=8 * 1024 * 1024),
        name="fill_slots",
    )(*blocks)


def main_kernel(
    loss_scale,
    q_ref,
    k_ref,
    v_ref,
    a_ref,
    b_ref,
    km_ref,
    s_half,
    state_half,
    top_half,
    own_ref,
    near_ref,
    phi_ref,
    both_ref,
    early_ref,
    dest_ref,
    ok_ref,
    diff_ref,
    buf_ref,
    s_scr,
    p_scr,
    psi_scr,
    key_scr,
    vp_scr,
    wide_scr,
):
    all_ones = jnp.ones((BLOCK, BLOCK), BF16)
    ones = jnp.ones((TALL - HEAD_DIM, BLOCK), BF16)
    fill_keys(key_scr, b_ref, k_ref, ok_ref, CHUNKS // 2)
    for i in range(CHUNKS):
        src = a_ref if i < 4 else b_ref
        for k in range(2):
            at = i * CHUNK + k * BLOCK
            one = ok_ref[2 * i + k : 2 * i + k + 1, :].astype(BF16)
            value = src[i % 4, k, 1] * one
            vp_scr[:HEAD_DIM, at : at + BLOCK] = value.T
            vp_scr[HEAD_DIM:, at : at + BLOCK] = ones * one
            if i >= 4:
                wide_scr[at - FAR // 2 : at - FAR // 2 + BLOCK, :BLOCK] = value
                wide_scr[at - FAR // 2 : at - FAR // 2 + BLOCK, BLOCK:] = all_ones * one
    vp_scr[:HEAD_DIM, FAR:] = v_ref[...].T
    vp_scr[HEAD_DIM:, FAR:] = ones
    first_half = lax.broadcasted_iota(jnp.int32, (BLOCK, BLOCK), 1) < WINDOW
    dest = dest_ref[...]

    groups = HEADS // 2
    half = CHUNKS // 2
    tops, sums = [None] * groups, [None] * groups

    def scores(g):
        query = two_heads(q_ref, g)
        top = jnp.max(
            own_ref[:, g * CHUNK : (g + 1) * CHUNK].reshape(BLOCK // 8, 8, CHUNK), axis=0
        )
        top = jnp.maximum(top, top_half[:, g * CHUNK : (g + 1) * CHUNK])
        for i in range(half):
            s = dot(key_scr[i * CHUNK : (i + 1) * CHUNK, :], query, NT)
            s_scr[g % 2, i * CHUNK : (i + 1) * CHUNK, :] = s
            top = jnp.maximum(top, jnp.max(s.reshape(CHUNK // 8, 8, CHUNK), axis=0))
            yield
        tops[g] = jnp.max(top, axis=0, keepdims=True) * SCALE

    def features(g):
        for i in range(half):
            keys = key_scr[i * CHUNK : (i + 1) * CHUNK, :]
            u = dot(km_ref[g * BLOCK : (g + 1) * BLOCK, :], keys, NT)
            psi = two_softmax(u.reshape(2, FEATURES, CHUNK)).reshape(CHUNK, CHUNK)
            psi_scr[g % 3, :, i * CHUNK : (i + 1) * CHUNK] = psi.astype(BF16)
            yield

    def weights(g):
        for i in range(CHUNKS):
            if i < half:
                s = s_half[i * CHUNK : (i + 1) * CHUNK, g * CHUNK : (g + 1) * CHUNK]
            else:
                s = s_scr[g % 2, (i - half) * CHUNK : (i - half + 1) * CHUNK, :]
            w = jnp.exp2(s * SCALE - tops[g])
            p_scr[g % 2, i * CHUNK : (i + 1) * CHUNK, :] = w.astype(BF16)
            yield
        s = own_ref[:, g * CHUNK : (g + 1) * CHUNK]
        p_scr[g % 2, FAR:, :] = jnp.exp2(s * SCALE - tops[g]).astype(BF16)
        yield

    def mixes(g):
        mixed = dot(vp_scr[...], p_scr[g % 2])
        yield
        state = state_half[g * CHUNK : (g + 1) * CHUNK, :] + dot(psi_scr[g % 3], wide_scr[...])
        yield
        late = state + early_ref[g * CHUNK : (g + 1) * CHUNK, :]
        sums[g] = (mixed, state.astype(BF16), late.astype(BF16))
        yield

    def outputs(g):
        mixed, state, late = sums[g]
        heads = [2 * g, 2 * g + 1]
        parts = [slice(0, BLOCK), slice(BLOCK, CHUNK)]
        states = [jnp.concatenate([state[p], late[p]], axis=0) for p in parts]
        far = [dot(both_ref[h * BLOCK : (h + 1) * BLOCK, :], states[k]) for k, h in enumerate(heads)]
        yield
        total = jnp.concatenate(far, axis=0) + near_ref[g * CHUNK : (g + 1) * CHUNK, :]
        share = 1.0 / mixed[HEAD_DIM : HEAD_DIM + 1]
        teacher = mixed[:HEAD_DIM] * share
        teacher = jnp.concatenate([teacher[:, p].T for p in parts], axis=0).astype(BF16)
        yield
        moved = [dot(dest, teacher[p]) for p in parts]
        inverse = 1.0 / total[:, HEAD_DIM:]
        student = total[:, :HEAD_DIM] * inverse
        gap = student - teacher.astype(F32)
        for k in range(2):
            diff_ref[:, heads[k] * BLOCK : (heads[k] + 1) * BLOCK] = gap[parts[k]]
        yield
        grad_out = gap * (inverse * (2.0 * loss_scale))
        grad_both = jnp.concatenate([grad_out, -grad_out * student], axis=1).astype(BF16)
        yield
        dphi = [dot(states[k], grad_both[parts[k]], NT) for k in range(2)]
        yield
        for k in range(2):
            for shard in range(8):
                buf_ref[shard, :, heads[k] * BLOCK : (heads[k] + 1) * BLOCK] = moved[k][
                    shard * 16 : (shard + 1) * 16
                ].astype(BF16)
        yield
        du = []
        for k in range(2):
            phi = phi_ref[heads[k] * BLOCK : (heads[k] + 1) * BLOCK, :]
            terms = phi * jnp.where(first_half, dphi[k][:BLOCK], dphi[k][BLOCK:])
            up, down = phi[:FEATURES], phi[FEATURES:]
            du.append(
                terms[:FEATURES]
                - terms[FEATURES:]
                - up * jnp.sum(terms[:FEATURES], axis=0, keepdims=True)
                + down * jnp.sum(terms[FEATURES:], axis=0, keepdims=True)
            )
        yield
        for k in range(2):
            h = heads[k]
            grad = dot(du[k].astype(BF16), q_ref[:, h * BLOCK : (h + 1) * BLOCK]).astype(BF16)
            for i in range(4):
                at = (HEADS + i) * BLOCK
                buf_ref[h, :, at : at + BLOCK] = grad[i * 16 : (i + 1) * 16]
        yield

    for step in range(groups + 3):
        running = []
        for stage, length, late_by in (
            (outputs, 8, 3),
            (mixes, 3, 2),
            (weights, 9, 1),
            (features, 4, 1),
            (scores, 5, 0),
        ):
            if 0 <= step - late_by < groups:
                running.append((stage(step - late_by), length))
        marks = sorted(
            ((n + 0.5) / length, at) for at, (_, length) in enumerate(running) for n in range(length)
        )
        for _, at in marks:
            next(running[at][0], None)
        for stage, _ in running:
            for _ in stage:
                pass


def main_call(loss_scale, q, k, v, a, b, km, half, local):
    vmem = pl.BlockSpec(memory_space=pltpu.VMEM)
    return pl.pallas_call(
        functools.partial(main_kernel, loss_scale),
        out_shape=(
            jax.ShapeDtypeStruct((BLOCK, HEADS * HEAD_DIM), F32),
            jax.ShapeDtypeStruct((8, 16, 1536), BF16),
        ),
        in_specs=[vmem] * 16,
        out_specs=(vmem, vmem),
        scratch_shapes=[
            pltpu.VMEM((2, FAR // 2, CHUNK), F32),
            pltpu.VMEM((2, FAR + BLOCK, CHUNK), BF16),
            pltpu.VMEM((3, CHUNK, FAR // 2), BF16),
            pltpu.VMEM((FAR // 2, BLOCK), BF16),
            pltpu.VMEM((TALL, FAR + BLOCK), BF16),
            pltpu.VMEM((FAR // 2, CHUNK), BF16),
        ],
        compiler_params=pltpu.CompilerParams(vmem_limit_bytes=24 * 1024 * 1024),
        cost_estimate=pl.CostEstimate(
            flops=3_000_000_000, bytes_accessed=3_000_000, transcendentals=4_000_000
        ),
        name="transfer",
    )(q, k, v, a, b, km, *half, *local)


def finish_kernel(part_ref, far_ref, out_ref):
    c = lax.axis_index("c")

    def put(first_ref, second_ref):
        for y in range(4):
            out_ref[2 * y] = first_ref[y].astype(F32)
            out_ref[2 * y + 1] = second_ref[y].astype(F32)

    @pl.when(c == 0)
    def _():
        put(part_ref, far_ref)

    @pl.when(c == 1)
    def _():
        put(far_ref, part_ref)


def finish_call(part, far):
    vmem = pl.BlockSpec(memory_space=pltpu.VMEM)
    return pl.pallas_call(
        finish_kernel,
        out_shape=jax.ShapeDtypeStruct((HEADS, FEATURES, HEAD_DIM), F32),
        in_specs=[vmem] * 2,
        out_specs=vmem,
        compiler_params=pltpu.CompilerParams(vmem_limit_bytes=8 * 1024 * 1024),
        name="finish",
    )(part, far)


def on_device(queries, keys, values, query_map, key_map, documents, assignment):
    query_rows = jnp.swapaxes(query_map, 1, 2).reshape(HEADS * FEATURES, HEAD_DIM)
    key_rows = jnp.swapaxes(key_map, 1, 2).reshape(HEADS * FEATURES, HEAD_DIM)
    shift1 = [(i, (i + 1) % 8) for i in range(8)]
    shift2 = [(i, (i + 2) % 8) for i in range(8)]
    plane0 = pack_call(keys[0], values[0])
    plane2 = lax.ppermute(plane0, "z", shift2)
    plane1 = lax.ppermute(plane0, "z", shift1)
    local = local_call(
        queries[0], keys[0], values[0], query_rows, key_rows, assignment[0], documents
    )
    plane1, plane2, local = lax.optimization_barrier((plane1, plane2, local))
    slots = slot_call(plane0, plane1, plane2)
    mine = lax.all_to_all(slots, "y", 0, 0, tiled=True)
    other = lax.ppermute(mine, "c", [(0, 1), (1, 0)])
    local, (q, k, v, km) = local[:7], local[7:]
    half = half_call(q, k, mine, km, local[-1])
    loss_scale = HEAD_DIM / math.sqrt(4 * 64 * BLOCK)
    difference, outgoing = main_call(
        loss_scale, q, k, v, mine, other, km, half, local
    )
    got = lax.all_to_all(outgoing, ("y", "c"), 0, 0, tiled=True)
    relay = got[:, :, :1024].reshape(8, 8, 2, 1024).transpose(1, 0, 2, 3).reshape(8, 16, 1024)
    part = jnp.sum(got[:, :, 1024:].astype(F32), axis=0).astype(BF16)
    part = jnp.broadcast_to(part[None], (8, 16, 512))
    got = lax.all_to_all(jnp.concatenate([relay, part], axis=2), "z", 0, 0, tiled=True)
    relay = got
    part = jnp.sum(got[:, :, 1024:].astype(F32), axis=0).astype(BF16)
    part = part.reshape(16, 4, HEAD_DIM).transpose(1, 0, 2).reshape(FEATURES, HEAD_DIM)
    part = jnp.broadcast_to(part[None], (16, FEATURES, HEAD_DIM))
    got = lax.all_to_all(part, ("x", "y"), 0, 0, tiled=True)
    part = jnp.sum(got.reshape(4, 4, FEATURES, HEAD_DIM).astype(F32), axis=0).astype(BF16)
    relay, part = lax.optimization_barrier((relay, part))
    far = lax.ppermute(part, "c", [(0, 1), (1, 0)])
    relaid = relay[:, :, :1024].reshape(1, BLOCK, 1024)
    grad = finish_call(part, far)
    return relaid, difference[None], jnp.swapaxes(grad, 1, 2)


def solution(mesh):
    split = Mesh(np.array(mesh.devices).reshape(4, 8, 4, 2), ("x", "z", "y", "c"))
    ctx = ("z", "y", "c")
    return jax.shard_map(
        on_device,
        mesh=split,
        in_specs=(
            P("x", ctx, None),
            P("x", ctx, None),
            P("x", ctx, None),
            P(),
            P(),
            P("x", None),
            P("x", None, None),
        ),
        out_specs=(P("x", ctx, None), P("x", ctx, None), P()),
        check_vma=False,
    )
```

```python
import functools
import math

import jax
import jax.numpy as jnp
import numpy as np
from jax import lax
from jax.experimental import pallas as pl
from jax.experimental.pallas import tpu as pltpu
from jax.sharding import Mesh, PartitionSpec as P

HEAD_DIM = 128
WINDOW = 64
BLOCK = 128
HEADS = 8
FEATURES = 64
ROWS = HEADS * BLOCK
CHUNK = 2 * BLOCK
CHUNKS = 8
FAR = CHUNK * CHUNKS
SCALE = math.log2(math.e) / math.sqrt(HEAD_DIM)
NEGATIVE = -1e30
NT = (((1,), (1,)), ((), ()))
NN = (((1,), (0,)), ((), ()))
TN = (((0,), (0,)), ((), ()))
TALL = HEAD_DIM + 16
F32 = jnp.float32
BF16 = jnp.bfloat16
LOG2E = math.log2(math.e)


def dot(a, b, dims=NN):
    return lax.dot_general(a, b, dims, preferred_element_type=F32)


def two_softmax(u):
    u = u * LOG2E
    top = jnp.max(u, axis=1, keepdims=True)
    low = jnp.min(u, axis=1, keepdims=True)
    up = jnp.exp2(u - top)
    down = jnp.exp2(low - u)
    up = up * (1.0 / jnp.sum(up, axis=1, keepdims=True))
    down = down * (1.0 / jnp.sum(down, axis=1, keepdims=True))
    return jnp.concatenate([up, down], axis=1)


def in_hbm(x):
    return pltpu.with_memory_space_constraint(x, pltpu.HBM)


def iota(shape, axis):
    return lax.broadcasted_iota(jnp.int32, shape, axis)


def pack_kernel(k_hbm, v_hbm, out_ref, sems):
    copies = [
        pltpu.make_async_copy(k_hbm, out_ref.at[0], sems.at[0]),
        pltpu.make_async_copy(v_hbm, out_ref.at[1], sems.at[1]),
    ]
    for copy in copies:
        copy.start()
    for copy in copies:
        copy.wait()


def pack_call(k, v):
    return pl.pallas_call(
        pack_kernel,
        out_shape=jax.ShapeDtypeStruct((2, BLOCK, HEAD_DIM), BF16),
        in_specs=[pl.BlockSpec(memory_space=pltpu.HBM)] * 2,
        out_specs=pl.BlockSpec(memory_space=pltpu.VMEM),
        scratch_shapes=[pltpu.SemaphoreType.DMA((2,))],
        compiler_params=pltpu.CompilerParams(vmem_limit_bytes=8 * 1024 * 1024),
        name="pack_block",
    )(in_hbm(k), in_hbm(v))


def local_kernel(
    q_hbm,
    qm_hbm,
    km_hbm,
    route_hbm,
    doc_hbm,
    k_hbm,
    v_hbm,
    own_ref,
    near_ref,
    phi_ref,
    both_ref,
    early_ref,
    dest_ref,
    ok_ref,
    q_ref,
    k_ref,
    v_ref,
    km_ref,
    qm_ref,
    route_ref,
    doc_ref,
    sems,
):
    pairs = (
        (route_hbm, route_ref),
        (doc_hbm, doc_ref),
        (k_hbm, k_ref),
        (v_hbm, v_ref),
        (km_hbm, km_ref),
        (qm_hbm, qm_ref),
        (q_hbm, q_ref),
    )
    copies = [pltpu.make_async_copy(a, b, sems.at[n]) for n, (a, b) in enumerate(pairs)]
    for copy in copies:
        copy.start()
    copies[0].wait()
    copies[1].wait()
    col = lax.broadcasted_iota(jnp.int32, (BLOCK, BLOCK), 1)
    row = lax.broadcasted_iota(jnp.int32, (BLOCK, BLOCK), 0)
    causal = row <= col
    near = causal & ((col < WINDOW) == (row < WINDOW))
    first_half = col < WINDOW
    z, y, c = lax.axis_index("z"), lax.axis_index("y"), lax.axis_index("c")
    here = (z * 4 + y) * 2 + c
    place = iota((2 * CHUNKS, 64), 0)
    block = iota((2 * CHUNKS, 64), 1)
    from_y = lax.shift_right_logical(place, 1) & 3
    from_c = jnp.where(place < CHUNKS, c, 1 - c)
    first = jnp.where(from_y < y, 0, jnp.where(from_y > y, 1, 2 * from_c))
    second = jnp.where(from_y > y, 2, 1)
    source = (z - jnp.where((place & 1) == 0, first, second)) * 8 + from_y * 2 + from_c
    documents = doc_ref[...]
    own_document = jnp.sum(jnp.where(iota((1, 64), 1) == here, documents, 0), axis=1, keepdims=True)
    same = (documents == own_document) & (iota((1, 64), 1) < here) & (iota((1, 64), 1) > here - 16)
    found = jnp.where((source == block) & same, 1.0, 0.0)
    ok_ref[...] = jnp.broadcast_to(jnp.max(found, axis=1, keepdims=True), ok_ref.shape)
    shard = route_ref[pl.ds(here, 1), :]
    order = (shard & 7) * 8 + lax.shift_right_logical(shard, 3)
    pieces = (iota((64, 64), 0) == order).astype(BF16)
    rows = (lax.shift_right_logical(iota((BLOCK, 64), 0), 1) == iota((BLOCK, 64), 1)).astype(BF16)
    tokens = (iota((64, BLOCK), 0) == lax.shift_right_logical(iota((64, BLOCK), 1), 1)).astype(BF16)
    placed = dot(dot(rows, pieces).astype(BF16), tokens)
    dest_ref[...] = jnp.where((row & 1) == (col & 1), placed, 0.0).astype(BF16)
    for copy in copies[2:5]:
        copy.wait()
    keys = k_ref[...]
    values = jnp.concatenate([v_ref[...], jnp.ones((BLOCK, BLOCK), BF16)], axis=1)
    psi = two_softmax(dot(km_ref[...], keys, NT).reshape(HEADS, FEATURES, BLOCK))
    early = jnp.where(iota((BLOCK, CHUNK), 0) < WINDOW, values.astype(F32), 0.0).astype(BF16)
    early_ref[...] = dot(psi.reshape(ROWS, BLOCK).astype(BF16), early)
    copies[5].wait()
    copies[6].wait()
    for h in range(HEADS):
        at = h * BLOCK
        query = q_ref[:, at : at + BLOCK]
        scores = dot(keys, query, NT)
        own_ref[:, at : at + BLOCK] = jnp.where(causal, scores, NEGATIVE)
        window = jnp.where(near, scores * SCALE, NEGATIVE)
        weights = jnp.exp2(window - jnp.max(window, axis=0, keepdims=True))
        near_ref[at : at + BLOCK, :] = dot(weights.T.astype(BF16), values)
        u = dot(qm_ref[h * FEATURES : (h + 1) * FEATURES, :], query, NT)
        phi = two_softmax(u[None])[0]
        phi_ref[at : at + BLOCK, :] = phi
        both = jnp.concatenate(
            [jnp.where(first_half, phi, 0.0), jnp.where(first_half, 0.0, phi)], axis=0
        )
        both_ref[at : at + BLOCK, :] = both.T.astype(BF16)


def local_call(q, k, v, qm, km, routes, documents):
    vmem = pl.BlockSpec(memory_space=pltpu.VMEM)
    return pl.pallas_call(
        local_kernel,
        out_shape=(
            jax.ShapeDtypeStruct((BLOCK, ROWS), F32),
            jax.ShapeDtypeStruct((ROWS, CHUNK), F32),
            jax.ShapeDtypeStruct((ROWS, BLOCK), F32),
            jax.ShapeDtypeStruct((ROWS, CHUNK), BF16),
            jax.ShapeDtypeStruct((ROWS, CHUNK), F32),
            jax.ShapeDtypeStruct((BLOCK, BLOCK), BF16),
            jax.ShapeDtypeStruct((2 * CHUNKS, BLOCK), F32),
            jax.ShapeDtypeStruct((BLOCK, ROWS), BF16),
            jax.ShapeDtypeStruct((BLOCK, HEAD_DIM), BF16),
            jax.ShapeDtypeStruct((BLOCK, HEAD_DIM), BF16),
            jax.ShapeDtypeStruct((HEADS * FEATURES, HEAD_DIM), BF16),
        ),
        in_specs=[pl.BlockSpec(memory_space=pltpu.HBM)] * 7,
        out_specs=(vmem,) * 11,
        scratch_shapes=[
            pltpu.VMEM((HEADS * FEATURES, HEAD_DIM), BF16),
            pltpu.VMEM((64, 64), jnp.int32),
            pltpu.VMEM((1, 64), jnp.int32),
            pltpu.SemaphoreType.DMA((7,)),
        ],
        compiler_params=pltpu.CompilerParams(vmem_limit_bytes=16 * 1024 * 1024),
        cost_estimate=pl.CostEstimate(
            flops=400_000_000, bytes_accessed=4_000_000, transcendentals=500_000
        ),
        name="local_block",
    )(*[in_hbm(each) for each in (q, qm, km, routes, documents, k, v)])


def half_kernel(
    q_ref, k_ref, a_ref, km_ref, ok_ref, s_ref, state_ref, top_ref, key_scr, psi_scr, wide_scr
):
    fill_keys(key_scr, a_ref, k_ref, ok_ref, 0)
    for i in range(CHUNKS // 2):
        for k in range(2):
            at = i * CHUNK + k * BLOCK
            one = ok_ref[2 * i + k : 2 * i + k + 1, :].astype(BF16)
            wide_scr[at : at + BLOCK, :BLOCK] = a_ref[i, k, 1] * one
            wide_scr[at : at + BLOCK, BLOCK:] = jnp.ones((BLOCK, BLOCK), BF16) * one
    for g in range(HEADS // 2):
        query = two_heads(q_ref, g)
        top = None
        for i in range(CHUNKS // 2):
            keys = key_scr[i * CHUNK : (i + 1) * CHUNK, :]
            s = dot(keys, query, NT)
            s_ref[i * CHUNK : (i + 1) * CHUNK, g * CHUNK : (g + 1) * CHUNK] = s
            now = jnp.max(s.reshape(CHUNK // 8, 8, CHUNK), axis=0)
            top = now if top is None else jnp.maximum(top, now)
            u = dot(km_ref[g * BLOCK : (g + 1) * BLOCK, :], keys, NT)
            psi = two_softmax(u.reshape(2, FEATURES, CHUNK)).reshape(CHUNK, CHUNK)
            psi_scr[g * CHUNK : (g + 1) * CHUNK, i * CHUNK : (i + 1) * CHUNK] = psi.astype(BF16)
        state_ref[g * CHUNK : (g + 1) * CHUNK, :] = dot(
            psi_scr[g * CHUNK : (g + 1) * CHUNK, :], wide_scr[...]
        )
        top_ref[:, g * CHUNK : (g + 1) * CHUNK] = top


def two_heads(q_ref, g):
    return jnp.concatenate(
        [q_ref[:, (2 * g + k) * BLOCK : (2 * g + k + 1) * BLOCK] for k in range(2)], axis=0
    )


def fill_keys(key_scr, src, k_ref, ok_ref, first):
    first_key = k_ref[0:16, :].astype(F32)[0:1, :]
    for i in range(CHUNKS // 2):
        for k in range(2):
            at = i * CHUNK + k * BLOCK
            one = ok_ref[2 * (first + i) + k : 2 * (first + i) + k + 1, :]
            other = (first_key * (1.0 - one)).astype(BF16)
            key_scr[at : at + BLOCK, :] = src[i, k, 0] * one.astype(BF16) + other


def half_call(q, k, a, km, ok):
    vmem = pl.BlockSpec(memory_space=pltpu.VMEM)
    return pl.pallas_call(
        half_kernel,
        out_shape=(
            jax.ShapeDtypeStruct((FAR // 2, ROWS), F32),
            jax.ShapeDtypeStruct((ROWS, CHUNK), F32),
            jax.ShapeDtypeStruct((8, ROWS), F32),
        ),
        in_specs=[vmem] * 5,
        out_specs=(vmem,) * 3,
        scratch_shapes=[
            pltpu.VMEM((FAR // 2, BLOCK), BF16),
            pltpu.VMEM((ROWS, FAR // 2), BF16),
            pltpu.VMEM((FAR // 2, CHUNK), BF16),
        ],
        compiler_params=pltpu.CompilerParams(vmem_limit_bytes=16 * 1024 * 1024),
        cost_estimate=pl.CostEstimate(
            flops=400_000_000, bytes_accessed=4_000_000, transcendentals=1_000_000
        ),
        name="first_half",
    )(q, k, a, km, ok)


def slot_kernel(now_ref, back1_ref, back2_ref, out_ref):
    y, c = lax.axis_index("y"), lax.axis_index("c")
    planes = (now_ref, back1_ref, back2_ref)

    def put(d, k, plane):
        out_ref[d, k] = planes[plane][...]

    for d in range(4):

        @pl.when(d > y)
        def _():
            put(d, 0, 0)
            put(d, 1, 1)

        @pl.when(d < y)
        def _():
            put(d, 0, 1)
            put(d, 1, 2)

        @pl.when((d == y) & (c == 0))
        def _():
            put(d, 0, 0)
            put(d, 1, 1)

        @pl.when((d == y) & (c == 1))
        def _():
            put(d, 0, 2)
            put(d, 1, 1)


def slot_call(*blocks):
    vmem = pl.BlockSpec(memory_space=pltpu.VMEM)
    return pl.pallas_call(
        slot_kernel,
        out_shape=jax.ShapeDtypeStruct((4, 2, 2, BLOCK, HEAD_DIM), BF16),
        in_specs=[vmem] * 3,
        out_specs=vmem,
        compiler_params=pltpu.CompilerParams(vmem_limit_bytes=8 * 1024 * 1024),
        name="fill_slots",
    )(*blocks)


def main_kernel(
    loss_scale,
    q_ref,
    k_ref,
    v_ref,
    a_ref,
    b_ref,
    km_ref,
    s_half,
    state_half,
    top_half,
    own_ref,
    near_ref,
    phi_ref,
    both_ref,
    early_ref,
    dest_ref,
    ok_ref,
    diff_ref,
    buf_ref,
    s_scr,
    p_scr,
    psi_scr,
    key_scr,
    vp_scr,
    wide_scr,
):
    all_ones = jnp.ones((BLOCK, BLOCK), BF16)
    ones = jnp.ones((TALL - HEAD_DIM, BLOCK), BF16)
    fill_keys(key_scr, b_ref, k_ref, ok_ref, CHUNKS // 2)
    for i in range(CHUNKS):
        src = a_ref if i < 4 else b_ref
        for k in range(2):
            at = i * CHUNK + k * BLOCK
            one = ok_ref[2 * i + k : 2 * i + k + 1, :].astype(BF16)
            value = src[i % 4, k, 1] * one
            vp_scr[:HEAD_DIM, at : at + BLOCK] = value.T
            vp_scr[HEAD_DIM:, at : at + BLOCK] = ones * one
            if i >= 4:
                wide_scr[at - FAR // 2 : at - FAR // 2 + BLOCK, :BLOCK] = value
                wide_scr[at - FAR // 2 : at - FAR // 2 + BLOCK, BLOCK:] = all_ones * one
    vp_scr[:HEAD_DIM, FAR:] = v_ref[...].T
    vp_scr[HEAD_DIM:, FAR:] = ones
    first_half = lax.broadcasted_iota(jnp.int32, (BLOCK, BLOCK), 1) < WINDOW
    dest = dest_ref[...]

    groups = HEADS // 2
    half = CHUNKS // 2
    tops, sums = [None] * groups, [None] * groups

    def scores(g):
        query = two_heads(q_ref, g)
        top = jnp.max(
            own_ref[:, g * CHUNK : (g + 1) * CHUNK].reshape(BLOCK // 8, 8, CHUNK), axis=0
        )
        top = jnp.maximum(top, top_half[:, g * CHUNK : (g + 1) * CHUNK])
        for i in range(half):
            s = dot(key_scr[i * CHUNK : (i + 1) * CHUNK, :], query, NT)
            s_scr[g % 2, i * CHUNK : (i + 1) * CHUNK, :] = s
            top = jnp.maximum(top, jnp.max(s.reshape(CHUNK // 8, 8, CHUNK), axis=0))
            yield
        tops[g] = jnp.max(top, axis=0, keepdims=True) * SCALE

    def features(g):
        for i in range(half):
            keys = key_scr[i * CHUNK : (i + 1) * CHUNK, :]
            u = dot(km_ref[g * BLOCK : (g + 1) * BLOCK, :], keys, NT)
            psi = two_softmax(u.reshape(2, FEATURES, CHUNK)).reshape(CHUNK, CHUNK)
            psi_scr[g % 3, :, i * CHUNK : (i + 1) * CHUNK] = psi.astype(BF16)
            yield

    def weights(g):
        for i in range(CHUNKS):
            if i < half:
                s = s_half[i * CHUNK : (i + 1) * CHUNK, g * CHUNK : (g + 1) * CHUNK]
            else:
                s = s_scr[g % 2, (i - half) * CHUNK : (i - half + 1) * CHUNK, :]
            w = jnp.exp2(s * SCALE - tops[g])
            p_scr[g % 2, i * CHUNK : (i + 1) * CHUNK, :] = w.astype(BF16)
            yield
        s = own_ref[:, g * CHUNK : (g + 1) * CHUNK]
        p_scr[g % 2, FAR:, :] = jnp.exp2(s * SCALE - tops[g]).astype(BF16)
        yield

    def mixes(g):
        mixed = dot(vp_scr[...], p_scr[g % 2])
        yield
        state = state_half[g * CHUNK : (g + 1) * CHUNK, :] + dot(psi_scr[g % 3], wide_scr[...])
        yield
        late = state + early_ref[g * CHUNK : (g + 1) * CHUNK, :]
        sums[g] = (mixed, state.astype(BF16), late.astype(BF16))
        yield

    def outputs(g):
        mixed, state, late = sums[g]
        heads = [2 * g, 2 * g + 1]
        parts = [slice(0, BLOCK), slice(BLOCK, CHUNK)]
        states = [jnp.concatenate([state[p], late[p]], axis=0) for p in parts]
        far = [dot(both_ref[h * BLOCK : (h + 1) * BLOCK, :], states[k]) for k, h in enumerate(heads)]
        yield
        total = jnp.concatenate(far, axis=0) + near_ref[g * CHUNK : (g + 1) * CHUNK, :]
        share = 1.0 / mixed[HEAD_DIM : HEAD_DIM + 1]
        teacher = mixed[:HEAD_DIM] * share
        teacher = jnp.concatenate([teacher[:, p].T for p in parts], axis=0).astype(BF16)
        yield
        moved = [dot(dest, teacher[p]) for p in parts]
        inverse = 1.0 / total[:, HEAD_DIM:]
        student = total[:, :HEAD_DIM] * inverse
        gap = student - teacher.astype(F32)
        for k in range(2):
            diff_ref[:, heads[k] * BLOCK : (heads[k] + 1) * BLOCK] = gap[parts[k]]
        yield
        grad_out = gap * (inverse * (2.0 * loss_scale))
        grad_both = jnp.concatenate([grad_out, -grad_out * student], axis=1).astype(BF16)
        yield
        dphi = [dot(states[k], grad_both[parts[k]], NT) for k in range(2)]
        yield
        for k in range(2):
            for shard in range(8):
                buf_ref[shard, :, heads[k] * BLOCK : (heads[k] + 1) * BLOCK] = moved[k][
                    shard * 16 : (shard + 1) * 16
                ].astype(BF16)
        yield
        du = []
        for k in range(2):
            phi = phi_ref[heads[k] * BLOCK : (heads[k] + 1) * BLOCK, :]
            terms = phi * jnp.where(first_half, dphi[k][:BLOCK], dphi[k][BLOCK:])
            up, down = phi[:FEATURES], phi[FEATURES:]
            du.append(
                terms[:FEATURES]
                - terms[FEATURES:]
                - up * jnp.sum(terms[:FEATURES], axis=0, keepdims=True)
                + down * jnp.sum(terms[FEATURES:], axis=0, keepdims=True)
            )
        yield
        for k in range(2):
            h = heads[k]
            grad = dot(du[k].astype(BF16), q_ref[:, h * BLOCK : (h + 1) * BLOCK]).astype(BF16)
            for i in range(4):
                at = (HEADS + i) * BLOCK
                buf_ref[h, :, at : at + BLOCK] = grad[i * 16 : (i + 1) * 16]
        yield

    for step in range(groups + 3):
        running = []
        for stage, length, late_by in (
            (outputs, 8, 3),
            (mixes, 3, 2),
            (weights, 9, 1),
            (features, 4, 1),
            (scores, 5, 0),
        ):
            if 0 <= step - late_by < groups:
                running.append((stage(step - late_by), length))
        marks = sorted(
            ((n + 0.5) / length, at) for at, (_, length) in enumerate(running) for n in range(length)
        )
        for _, at in marks:
            next(running[at][0], None)
        for stage, _ in running:
            for _ in stage:
                pass


def main_call(loss_scale, q, k, v, a, b, km, half, local):
    vmem = pl.BlockSpec(memory_space=pltpu.VMEM)
    return pl.pallas_call(
        functools.partial(main_kernel, loss_scale),
        out_shape=(
            jax.ShapeDtypeStruct((BLOCK, HEADS * HEAD_DIM), F32),
            jax.ShapeDtypeStruct((8, 16, 1536), BF16),
        ),
        in_specs=[vmem] * 16,
        out_specs=(vmem, vmem),
        scratch_shapes=[
            pltpu.VMEM((2, FAR // 2, CHUNK), F32),
            pltpu.VMEM((2, FAR + BLOCK, CHUNK), BF16),
            pltpu.VMEM((3, CHUNK, FAR // 2), BF16),
            pltpu.VMEM((FAR // 2, BLOCK), BF16),
            pltpu.VMEM((TALL, FAR + BLOCK), BF16),
            pltpu.VMEM((FAR // 2, CHUNK), BF16),
        ],
        compiler_params=pltpu.CompilerParams(vmem_limit_bytes=24 * 1024 * 1024),
        cost_estimate=pl.CostEstimate(
            flops=3_000_000_000, bytes_accessed=3_000_000, transcendentals=4_000_000
        ),
        name="transfer",
    )(q, k, v, a, b, km, *half, *local)


def finish_kernel(part_ref, far_ref, out_ref):
    c = lax.axis_index("c")

    def put(first_ref, second_ref):
        for y in range(4):
            out_ref[2 * y] = first_ref[y].astype(F32)
            out_ref[2 * y + 1] = second_ref[y].astype(F32)

    @pl.when(c == 0)
    def _():
        put(part_ref, far_ref)

    @pl.when(c == 1)
    def _():
        put(far_ref, part_ref)


def finish_call(part, far):
    vmem = pl.BlockSpec(memory_space=pltpu.VMEM)
    return pl.pallas_call(
        finish_kernel,
        out_shape=jax.ShapeDtypeStruct((HEADS, FEATURES, HEAD_DIM), F32),
        in_specs=[vmem] * 2,
        out_specs=vmem,
        compiler_params=pltpu.CompilerParams(vmem_limit_bytes=8 * 1024 * 1024),
        name="finish",
    )(part, far)


def on_device(queries, keys, values, query_map, key_map, documents, assignment):
    query_rows = jnp.swapaxes(query_map, 1, 2).reshape(HEADS * FEATURES, HEAD_DIM)
    key_rows = jnp.swapaxes(key_map, 1, 2).reshape(HEADS * FEATURES, HEAD_DIM)
    shift1 = [(i, (i + 1) % 8) for i in range(8)]
    shift2 = [(i, (i + 2) % 8) for i in range(8)]
    plane0 = pack_call(keys[0], values[0])
    plane2 = lax.ppermute(plane0, "z", shift2)
    plane1 = lax.ppermute(plane0, "z", shift1)
    local = local_call(
        queries[0], keys[0], values[0], query_rows, key_rows, assignment[0], documents
    )
    plane1, plane2, local = lax.optimization_barrier((plane1, plane2, local))
    slots = slot_call(plane0, plane1, plane2)
    mine = lax.all_to_all(slots, "y", 0, 0, tiled=True)
    other = lax.ppermute(mine, "c", [(0, 1), (1, 0)])
    local, (q, k, v, km) = local[:7], local[7:]
    half = half_call(q, k, mine, km, local[-1])
    loss_scale = HEAD_DIM / math.sqrt(4 * 64 * BLOCK)
    difference, outgoing = main_call(
        loss_scale, q, k, v, mine, other, km, half, local
    )
    got = lax.all_to_all(outgoing, ("y", "c"), 0, 0, tiled=True)
    relay = got[:, :, :1024].reshape(8, 8, 2, 1024).transpose(1, 0, 2, 3).reshape(8, 16, 1024)
    part = jnp.sum(got[:, :, 1024:].astype(F32), axis=0).astype(BF16)
    part = jnp.broadcast_to(part[None], (8, 16, 512))
    got = lax.all_to_all(jnp.concatenate([relay, part], axis=2), "z", 0, 0, tiled=True)
    relay = got
    part = jnp.sum(got[:, :, 1024:].astype(F32), axis=0).astype(BF16)
    part = part.reshape(16, 4, HEAD_DIM).transpose(1, 0, 2).reshape(FEATURES, HEAD_DIM)
    part = jnp.broadcast_to(part[None], (16, FEATURES, HEAD_DIM))
    got = lax.all_to_all(part, ("x", "y"), 0, 0, tiled=True)
    part = jnp.sum(got.reshape(4, 4, FEATURES, HEAD_DIM).astype(F32), axis=0).astype(BF16)
    relay, part = lax.optimization_barrier((relay, part))
    far = lax.ppermute(part, "c", [(0, 1), (1, 0)])
    relaid = relay[:, :, :1024].reshape(1, BLOCK, 1024)
    grad = finish_call(part, far)
    return relaid, difference[None], jnp.swapaxes(grad, 1, 2)


def solution(mesh):
    split = Mesh(np.array(mesh.devices).reshape(4, 8, 4, 2), ("x", "z", "y", "c"))
    ctx = ("z", "y", "c")
    return jax.shard_map(
        on_device,
        mesh=split,
        in_specs=(
            P("x", ctx, None),
            P("x", ctx, None),
            P("x", ctx, None),
            P(),
            P(),
            P("x", None),
            P("x", None, None),
        ),
        out_specs=(P("x", ctx, None), P("x", ctx, None), P()),
        check_vma=False,
    )
```
